32 devices in a mesh: img: 8 (over z, core), mp: 4 (over y, x).
Axes of the slice: x: 2, y: 2, z: 4, core: 2. Of those that a mesh axis runs over, the one named last changes fastest.
Arguments:
- tokens: bfloat16 [6144, 2048], P('img'), may hold values from -6 to 6
- caption: bfloat16 [3072, 4096], P('img'), may hold values from -6 to 6
- masked: int32 [24, 256], P('img'), may hold values from 0 to 1, as said below
- out_grad: bfloat16 [6144, 2048], P('img'), may hold values from -6 to 6
- mask_embed: bfloat16 [2048], replicated, may hold values from -6 to 6
- norm_gains: float32 [3, 2048], replicated, may hold values from 0.25 to 1.75
- attention_in: bfloat16 [2048, 3, 2048], P(None, None, 'mp'), may hold values from -0.125 to 0.125
- attention_out: bfloat16 [2048, 2048], P('mp'), may hold values from -0.5 to 0.5
- cross_query: bfloat16 [2048, 2048], P(None, 'mp'), may hold values from -0.125 to 0.125
- cross_text: bfloat16 [4096, 2, 2048], P(None, None, 'mp'), may hold values from -0.09375 to 0.09375
- cross_out: bfloat16 [2048, 2048], P('mp'), may hold values from -0.375 to 0.375
- feed_expand: bfloat16 [2048, 8192], P(None, 'mp'), may hold values from -0.125 to 0.125
- feed_shrink: bfloat16 [8192, 2048], P('mp'), may hold values from -0.0625 to 0.0625
Outputs:
- mixed_out: bfloat16 [6144, 2048], P(('img', 'mp'))
- tokens_grad: float32 [6144, 2048], P(('img', 'mp'))
- caption_grad: float32 [3072, 4096], P('img', 'mp')
- embed_grad: float32 [2048], P(('img', 'mp'))
- gains_grad: float32 [3, 2048], P(None, ('img', 'mp'))
- grad_attention_in: float32 [2048, 3, 2048], P('img', None, 'mp')
- grad_attention_out: float32 [2048, 2048], P('mp', 'img')
- grad_cross_query: float32 [2048, 2048], P('img', 'mp')
- grad_cross_text: float32 [4096, 2, 2048], P('img', None, 'mp')
- grad_cross_out: float32 [2048, 2048], P('mp', 'img')
- grad_feed_expand: float32 [2048, 8192], P('img', 'mp')
- grad_feed_shrink: float32 [8192, 2048], P('mp', 'img')
The draws below stay inside these ranges and needn't reach their ends.
Inputs may be any that keep to these rules, and one draw needn't show every extreme that they name: 1 marks a masked token. Each image masks 256 // k of its tokens for a whole k of 1 to 8, at positions drawn afresh; in every draw one image masks all 256 and one masks 256 // 8.
All inputs are finite; a program needn't handle non-finite values.
Results may differ from the reference program's by a relative error of at most 0.02.
Values may be sent and summed in bfloat16 or wider, within the bound.
A program may use at most 384 MiB of HBM per device.

```python
import math
import jax
import jax.numpy as jnp
from jax import lax

D = 2048
HEADS = 16
HDIM = 128
FF = 8192
DT = 4096
TXT = 128
L = 256
IMG_DEV = 3
HD = 2048
IMAGES = 24


def draw_masked(key, part):
    key = jax.random.fold_in(key, 11)
    keys_all = jax.random.split(key, 3)
    divisor = jax.random.randint(keys_all[0], (IMAGES,), 1, 9)
    chosen = jax.random.permutation(keys_all[1], IMAGES)
    divisor = divisor.at[chosen[0]].set(1).at[chosen[1]].set(8)
    counts_img = L // divisor
    order_keys = jax.random.split(keys_all[2], IMAGES)

    def one_order(key_one):
        return jax.random.permutation(key_one, L)
    rank_rows = jax.vmap(one_order)(order_keys)
    return (rank_rows < counts_img[:, None]).astype(jnp.int32)


def level_of(rng, extent, pieces, smallest, largest):
    level = 1.0
    for position, shards_of in pieces:
        draws = jax.random.uniform(jax.random.fold_in(jax.random.fold_in(rng, 6), position), (shards_of,), jnp.float32, smallest / len(pieces), largest / len(pieces))
        level = level * jnp.repeat(jnp.exp(draws), extent[position] // shards_of).reshape((-1,) + (1,) * (len(extent) - 1 - position))
    return level


def gaussian(stream_key, dims, scale, limit, pieces=(), kind=jnp.bfloat16):
    level = level_of(stream_key, dims, pieces, -0.22, 0.18) if pieces else 1.0
    drawn = jax.random.normal(stream_key, dims, jnp.float32) * scale * level
    return jnp.minimum(jnp.maximum(drawn, -limit), limit).astype(kind)


def setup_inputs(seed: int = 0) -> dict:
    key_list = jax.random.split(jax.random.key(seed), 14)
    tokens = gaussian(key_list[0], (IMAGES * L, D), 1.0, 6.0, ((0, 8),))
    caption = gaussian(key_list[1], (IMAGES * TXT, DT), 1.0, 6.0, ((0, 8),))
    masked = draw_masked(jax.random.fold_in(key_list[13], 71), 0)
    out_grad = gaussian(key_list[3], (IMAGES * L, D), 1.0, 6.0, ((0, 8),))
    mask_embed = gaussian(key_list[4], (D,), 1.0, 6.0)
    norm_gains = jnp.clip(1.0 + 0.15 * jax.random.normal(key_list[5], (3, D), jnp.float32), 0.25, 1.75)
    attention_in = gaussian(key_list[6], (D, 3, HD), D ** -0.5, 0.125, ((2, 4),))
    attention_out = gaussian(key_list[7], (HD, D), (HD // 16) ** -0.5, 0.5, ((0, 4),))
    cross_query = gaussian(key_list[8], (D, HD), D ** -0.5, 0.125, ((1, 4),))
    cross_text = gaussian(key_list[9], (DT, 2, HD), DT ** -0.5, 0.09375, ((2, 4),))
    cross_out = gaussian(key_list[10], (HD, D), (HD // 8) ** -0.5, 0.375, ((0, 4),))
    feed_expand = gaussian(key_list[11], (D, FF), D ** -0.5, 0.125, ((1, 4),))
    feed_shrink = gaussian(key_list[12], (FF, D), FF ** -0.5, 0.0625, ((0, 4),))
    return dict(tokens=tokens, caption=caption, masked=masked, out_grad=out_grad, mask_embed=mask_embed, norm_gains=norm_gains, attention_in=attention_in, attention_out=attention_out, cross_query=cross_query, cross_text=cross_text, cross_out=cross_out, feed_expand=feed_expand, feed_shrink=feed_shrink)


EPSILON = 1e-05

@jax.custom_vjp
def low(v):
    return lax.optimization_barrier(v.astype(jnp.bfloat16)).astype(jnp.float32)

@jax.custom_vjp
def low_back(v):
    return v

def low_keep(v):
    return (low(v), None)

def low_pass(kept, grad):
    return (grad,)

def back_keep(v):
    return (v, None)

def back_low(kept, grad):
    return (low(grad),)
low.defvjp(low_keep, low_pass)
low_back.defvjp(back_keep, back_low)

def matmul(left, right):
    return jnp.dot(left, right, precision=lax.Precision.HIGHEST)

def layer_norm(rows_in, gain_row):
    centre = rows_in - lax.optimization_barrier(jnp.mean(rows_in, axis=-1, keepdims=True))
    spread = lax.optimization_barrier(jnp.mean(centre * centre, axis=-1, keepdims=True))
    return centre * lax.rsqrt(spread + EPSILON) * gain_row

def attention(queries, keys_in, values_in):
    raw_scores = low_back(jnp.einsum('bqhe,bkhe->bhqk', queries, keys_in, precision=lax.Precision.HIGHEST))
    probs_low = low(jax.nn.softmax(raw_scores * (1.0 / math.sqrt(HDIM)), axis=-1))
    return jnp.einsum('bhqk,bkhe->bqhe', probs_low, values_in, precision=lax.Precision.HIGHEST)

def block(tokens_in, caption_in, mask_rows, mask_embed, norm_gains, attention_in, attention_out, cross_query, cross_text, cross_out, feed_expand, feed_shrink):
    images = mask_rows.shape[0] // L
    entry_rows = jnp.where(mask_rows[:, None] > 0, mask_embed[None, :], tokens_in)
    first_normed = low(layer_norm(entry_rows, norm_gains[0]))
    projected = low(low_back(matmul(first_normed, attention_in.reshape(D, 3 * HD)))).reshape(images, L, 3, HEADS, HDIM)
    self_mixed = attention(projected[:, :, 0], projected[:, :, 1], projected[:, :, 2])
    self_mixed = low(low_back(self_mixed.reshape(images * L, HD)))
    after_self = entry_rows + low_back(matmul(self_mixed, attention_out))
    second_normed = low(layer_norm(after_self, norm_gains[1]))
    queries = low(low_back(matmul(second_normed, cross_query))).reshape(images, L, HEADS, HDIM)
    text_pairs = low(low_back(matmul(caption_in, cross_text.reshape(DT, 2 * HD)))).reshape(images, TXT, 2, HEADS, HDIM)
    cross_mixed = attention(queries, text_pairs[:, :, 0], text_pairs[:, :, 1])
    cross_mixed = low(low_back(cross_mixed.reshape(images * L, HD)))
    after_cross = after_self + low_back(matmul(cross_mixed, cross_out))
    third_normed = low(layer_norm(after_cross, norm_gains[2]))
    hidden = low_back(matmul(third_normed, feed_expand))
    active = low(jax.nn.gelu(hidden, approximate=False))
    return after_cross + low_back(matmul(active, feed_shrink))

def reference(tokens, caption, masked, out_grad, mask_embed, norm_gains, attention_in, attention_out, cross_query, cross_text, cross_out, feed_expand, feed_shrink):
    weight_set = tuple((w.astype(jnp.float32) for w in (mask_embed, norm_gains, attention_in, attention_out, cross_query, cross_text, cross_out, feed_expand, feed_shrink)))
    groups = IMAGES // IMG_DEV
    token_groups = tokens.astype(jnp.float32).reshape(groups, IMG_DEV * L, D)
    caption_groups = caption.astype(jnp.float32).reshape(groups, IMG_DEV * TXT, DT)
    mask_groups = masked.reshape(groups, IMG_DEV * L)
    cot_groups = out_grad.astype(jnp.float32).reshape(groups, IMG_DEV * L, D)

    def one_group(totals, group_item):
        tokens_in, caption_in, mask_rows, cot_rows = group_item

        def forward(rows_in, text_in, *weights):
            return block(rows_in, text_in, mask_rows, *weights)
        result, pullback = jax.vjp(forward, tokens_in, caption_in, *weight_set)
        gradients = pullback(cot_rows * (mask_rows[:, None] > 0).astype(jnp.float32))
        totals = tuple((running + fresh for running, fresh in zip(totals, gradients[2:])))
        return (totals, (result.astype(jnp.bfloat16), gradients[0], gradients[1]))
    zero_totals = tuple((jnp.zeros(w.shape, jnp.float32) for w in weight_set))
    totals, outputs = lax.scan(one_group, zero_totals, (token_groups, caption_groups, mask_groups, cot_groups))
    mixed_out = outputs[0].reshape(IMAGES * L, D)
    tokens_grad = outputs[1].reshape(IMAGES * L, D)
    caption_grad = outputs[2].reshape(IMAGES * TXT, DT)
    return (mixed_out, tokens_grad, caption_grad, totals[0], totals[1], totals[2], totals[3], totals[4], totals[5], totals[6], totals[7], totals[8])
```

```python
import functools
import math

import jax
import jax.numpy as jnp
from jax import lax
from jax.experimental import pallas as pl
from jax.experimental.pallas import tpu as pltpu
from jax.sharding import PartitionSpec as P

HDIM = 128
EPSILON = 1e-05
SCALE = 1.0 / math.sqrt(HDIM)
VMEM_BYTES = 52 * 1024 * 1024
MESH = pl.DeviceIdType.MESH
BF16 = jnp.bfloat16
F32 = jnp.float32

NN = (((1,), (0,)), ((), ()))
NT = (((1,), (1,)), ((), ()))
TN = (((0,), (0,)), ((), ()))


def product(left, right, dims=NN):
    return lax.dot_general(left, right, dims, preferred_element_type=F32)


def norm_parts(rows_in):
    centre = rows_in - jnp.mean(rows_in, axis=-1, keepdims=True)
    root_inverse = lax.rsqrt(jnp.mean(centre * centre, axis=-1, keepdims=True) + EPSILON)
    return (centre * root_inverse, root_inverse)


def norm_back(grad_rows, unit_rows, root_inverse, gain_row):
    weighted = grad_rows * gain_row
    middle = jnp.mean(weighted, axis=-1, keepdims=True)
    along = jnp.mean(weighted * unit_rows, axis=-1, keepdims=True)
    return root_inverse * (weighted - middle - unit_rows * along)


def post_forward(total, rows_in, gain):
    fresh = rows_in[0] + total
    unit, _ = norm_parts(fresh)
    return fresh, (unit * gain).astype(BF16), ()


def post_backward(total, rows_in, gain):
    before, source = rows_in
    unit, root = norm_parts(source)
    grad = before + norm_back(total, unit, root, gain)
    return grad, grad.astype(BF16), (jnp.sum(total * unit, axis=0, keepdims=True),)


def post_entry(total, rows_in, gain):
    before, source, mask = rows_in
    unit, root = norm_parts(source)
    grad = before + norm_back(total, unit, root, gain)
    sums = (
        jnp.sum(total * unit, axis=0, keepdims=True),
        jnp.sum(grad * mask, axis=0, keepdims=True),
    )
    return grad * (1.0 - mask), None, sums


def post_plain(total, rows_in, gain):
    return (rows_in[0] + total).astype(BF16), None, ()


def square_kernel(
    post, dims, row_count, sum_count, gather, tile, *refs
):
    lhs_ref, weight_ref, gain_ref = refs[:3]
    refs = refs[3:]
    row_refs, refs = refs[:row_count], refs[row_count:]
    wide_ref, refs = refs[0], refs[1:]
    if gather:
        full_ref, refs = refs[0], refs[1:]
    sum_refs, refs = refs[:sum_count], refs[sum_count:]
    first_out, first_in, second_out, second_in, mine, send_sem, recv_sem = refs
    place = lax.axis_index("mp")
    up, across = lax.div(place, 2), lax.rem(place, 2)
    beside = up * 2 + (1 - across)
    above = (1 - up) * 2 + across
    corner = (1 - up) * 2 + (1 - across)
    share = mine.shape[0]
    half = mine.shape[1] // 2
    columns = 256
    peers = (beside, above)

    barrier = pltpu.get_barrier_semaphore()
    for peer in peers:
        pl.semaphore_signal(barrier, inc=1, device_id={"mp": peer}, device_id_type=MESH)
    pl.semaphore_wait(barrier, 2)

    def rows_of(owner):
        return pl.ds(pl.multiple_of(owner * share, 16), share)

    def remote(source, target, slot, peer):
        return pltpu.make_async_remote_copy(
            src_ref=source,
            dst_ref=target,
            send_sem=send_sem.at[slot],
            recv_sem=recv_sem.at[slot],
            device_id={"mp": peer},
            device_id_type=MESH,
        )

    def partial_into(owner, side, put):
        block = rows_of(owner)

        def step(j, carry):
            at = pl.multiple_of(j * columns, columns)
            there = pl.ds(pl.multiple_of(side * half + j * columns, columns), columns)
            if dims == NT:
                part = product(lhs_ref[block, :], weight_ref[there, :], NT)
            else:
                part = product(lhs_ref[block, :], weight_ref[:, there])
            put(pl.ds(at, columns), there, part)
            return carry

        lax.fori_loop(0, half // columns, step, 0)

    copies = []
    for order, targets in ((0, (corner, corner)), (1, (beside, above))):
        for side in range(2):

            def put(at, there, part, side=side, order=order):
                first_out[side, order, :, at] = part.astype(BF16)

            partial_into(targets[side], side, put)
            copy = remote(
                first_out.at[side, order], first_in.at[side, order], side * 2 + order, peers[side]
            )
            copy.start()
            copies.append(copy)

    def put_mine(at, there, part):
        mine[:, there] = part

    for side, owner in ((0, above), (1, beside)):

        def put_on(at, there, part, side=side):
            second_out[side, :, at] = part.astype(BF16)

        partial_into(owner, side, put_on)
    for side in range(2):
        partial_into(place, side, put_mine)

    onward = []
    for side in range(2):
        copies[side].wait_recv()
        second_out[side] = (
            second_out[side].astype(F32) + first_in[side, 0].astype(F32)
        ).astype(BF16)
        copy = remote(second_out.at[side], second_in.at[side], 4 + side, peers[1 - side])
        copy.start()
        onward.append(copy)
    for side in range(2):
        copies[2 + side].wait_recv()
    for side in range(2):
        onward[side].wait_recv()

    for sum_ref in sum_refs:
        sum_ref[...] = jnp.zeros_like(sum_ref)

    def finish(t, carry):
        at = pl.ds(pl.multiple_of(t * tile, 16), tile)
        total = jnp.concatenate(
            [
                mine[at, side * half : (side + 1) * half]
                + first_in[side, 1, at, :].astype(F32)
                + second_in[side, at, :].astype(F32)
                for side in range(2)
            ],
            axis=1,
        )
        wide, narrow, sums = post(total, tuple(r[at, :] for r in row_refs), gain_ref[...])
        wide_ref[at, :] = wide
        if gather:
            full_ref[pl.ds(pl.multiple_of(place * share + t * tile, 16), tile), :] = narrow
        for sum_ref, term in zip(sum_refs, sums):
            sum_ref[...] += term
        return carry

    lax.fori_loop(0, share // tile, finish, 0)

    if gather:

        def spread(owner, side, slot, peer):
            where = full_ref.at[rows_of(owner), pl.ds(side * half, half)]
            copy = remote(where, where, slot, peer)
            copy.start()
            return copy

        first = [spread(place, 0, 6, above), spread(place, 1, 7, beside)]
        rest = [spread(place, 0, 8, beside), spread(place, 1, 9, above)]
        first[0].wait_recv()
        rest.append(spread(above, 0, 10, beside))
        first[1].wait_recv()
        rest.append(spread(beside, 1, 11, above))
        for copy in rest:
            copy.wait_recv()
        for copy in first + rest:
            copy.wait_send()
    for copy in copies + onward:
        copy.wait_send()


def square_step(lhs, weight, dims, post, gain, rows_in, wide_type, sum_count, gather, ident):
    rows = lhs.shape[0]
    width = gain.shape[1]
    share = rows // 4
    outs = [jax.ShapeDtypeStruct((share, width), wide_type)]
    if gather:
        outs.append(jax.ShapeDtypeStruct((rows, width), BF16))
    outs += [jax.ShapeDtypeStruct((1, width), F32)] * sum_count
    half = width // 2
    vmem = pl.BlockSpec(memory_space=pltpu.VMEM)
    slots = 12 if gather else 6
    return pl.pallas_call(
        functools.partial(
            square_kernel, post, dims, len(rows_in), sum_count, gather, 32
        ),
        out_shape=outs,
        in_specs=[vmem] * (3 + len(rows_in)),
        out_specs=[vmem] * len(outs),
        scratch_shapes=[
            pltpu.VMEM((2, 2, share, half), BF16),
            pltpu.VMEM((2, 2, share, half), BF16),
            pltpu.VMEM((2, share, half), BF16),
            pltpu.VMEM((2, share, half), BF16),
            pltpu.VMEM((share, width), F32),
            pltpu.SemaphoreType.DMA((slots,)),
            pltpu.SemaphoreType.DMA((slots,)),
        ],
        compiler_params=pltpu.CompilerParams(
            collective_id=ident, has_side_effects=True, vmem_limit_bytes=VMEM_BYTES
        ),
        cost_estimate=pl.CostEstimate(
            flops=2 * rows * width * lhs.shape[1],
            bytes_accessed=2 * (lhs.size + weight.size + 6 * share * width),
            transcendentals=0,
        ),
    )(lhs, weight, gain, *rows_in)


def plain_step(lhs, weight, dims, post, gain, rows_in, wide_type, sum_count, gather, ident):
    part = product(lhs, weight, dims).astype(BF16)
    total = lax.psum_scatter(part, "mp", scatter_dimension=0, tiled=True).astype(F32)
    wide, narrow, sums = post(total, rows_in, gain)
    outs = [wide.astype(wide_type)]
    if gather:
        outs.append(lax.all_gather(narrow, "mp", axis=0, tiled=True))
    return outs + list(sums)


def softmax_rows(queries, keys_in):
    scores = product(queries, keys_in, NT) * SCALE
    powers = jnp.exp(scores - jnp.max(scores, axis=-1, keepdims=True))
    return powers * (1.0 / jnp.sum(powers, axis=-1, keepdims=True))


def attend_forward_kernel(heads, separate, query_ref, pair_ref, out_ref):
    key_at = 0 if separate else heads
    for h in range(heads):
        queries = query_ref[:, h * HDIM : (h + 1) * HDIM]
        keys_in = pair_ref[:, (key_at + h) * HDIM : (key_at + h + 1) * HDIM]
        values_in = pair_ref[:, (key_at + heads + h) * HDIM : (key_at + heads + h + 1) * HDIM]
        probs = softmax_rows(queries, keys_in).astype(BF16)
        out_ref[:, h * HDIM : (h + 1) * HDIM] = product(probs, values_in).astype(BF16)


def attend_backward_kernel(heads, separate, query_ref, pair_ref, grad_ref, *outs):
    key_at = 0 if separate else heads
    query_out, pair_out = outs if separate else (outs[0], outs[0])
    for h in range(heads):
        own = slice(h * HDIM, (h + 1) * HDIM)
        key_slice = slice((key_at + h) * HDIM, (key_at + h + 1) * HDIM)
        value_slice = slice((key_at + heads + h) * HDIM, (key_at + heads + h + 1) * HDIM)
        queries, keys_in, values_in = query_ref[:, own], pair_ref[:, key_slice], pair_ref[:, value_slice]
        grad = grad_ref[:, own]
        probs = softmax_rows(queries, keys_in)
        pair_out[:, value_slice] = product(probs.astype(BF16), grad, TN).astype(BF16)
        grad_probs = product(grad, values_in, NT)
        centred = grad_probs - jnp.sum(probs * grad_probs, axis=-1, keepdims=True)
        grad_scores = (probs * centred * SCALE).astype(BF16)
        query_out[:, own] = product(grad_scores, keys_in).astype(BF16)
        pair_out[:, key_slice] = product(grad_scores, queries, TN).astype(BF16)


def image_blocks(images, *arrays):
    return [pl.BlockSpec((a.shape[0] // images, a.shape[1]), lambda i: (i, 0)) for a in arrays]


def attend_forward(images, heads, queries, pairs):
    separate = queries is not pairs
    out = jax.ShapeDtypeStruct((queries.shape[0], heads * HDIM), BF16)
    return pl.pallas_call(
        functools.partial(attend_forward_kernel, heads, separate),
        grid=(images,),
        out_shape=out,
        in_specs=image_blocks(images, queries, pairs),
        out_specs=image_blocks(images, out)[0],
        compiler_params=pltpu.CompilerParams(vmem_limit_bytes=VMEM_BYTES),
    )(queries, pairs)


def attend_backward(images, heads, queries, pairs, grad):
    separate = queries is not pairs
    outs = [jax.ShapeDtypeStruct(queries.shape, BF16)]
    if separate:
        outs.append(jax.ShapeDtypeStruct(pairs.shape, BF16))
    result = pl.pallas_call(
        functools.partial(attend_backward_kernel, heads, separate),
        grid=(images,),
        out_shape=outs,
        in_specs=image_blocks(images, queries, pairs, grad),
        out_specs=image_blocks(images, *outs),
        compiler_params=pltpu.CompilerParams(vmem_limit_bytes=VMEM_BYTES),
    )(queries, pairs, grad)
    return result if separate else result[0]


def gelu_exact(values_in):
    return jax.nn.gelu(values_in, approximate=False)


def body(
    step,
    tokens,
    caption,
    masked,
    out_grad,
    mask_embed,
    norm_gains,
    attention_in,
    attention_out,
    cross_query,
    cross_text,
    cross_out,
    feed_expand,
    feed_shrink,
):
    axis_count = lax.axis_size("mp")
    axis_place = lax.axis_index("mp")
    images, length = masked.shape
    rows_all = images * length
    share_rows = rows_all // axis_count
    model_width = tokens.shape[1]
    text_width = caption.shape[1]
    heads_here = attention_in.shape[2] // HDIM

    def own_rows(rows_in):
        return lax.dynamic_slice_in_dim(rows_in, axis_place * share_rows, share_rows, 0)

    def image_sum(part, dimension):
        return lax.psum_scatter(
            part.astype(BF16), "img", scatter_dimension=dimension, tiled=True
        ).astype(F32)

    gains = [norm_gains[k : k + 1] for k in range(3)]
    mask_column = (masked.reshape(rows_all, 1) > 0)

    def enter(rows_in, mask):
        return jnp.where(mask, mask_embed.astype(F32)[None, :], rows_in.astype(F32))

    own_mask = own_rows(mask_column)
    own_float = own_mask.astype(F32)
    own_entry = enter(own_rows(tokens), own_mask)
    first_unit, _ = norm_parts(enter(tokens, mask_column))
    first_normed = (first_unit * gains[0]).astype(BF16)
    weight_in = attention_in.reshape(model_width, -1)
    projected = product(first_normed, weight_in).astype(BF16)
    self_mixed = attend_forward(images, heads_here, projected, projected)
    own_self, second_normed = step(
        self_mixed, attention_out, NN, post_forward, gains[1], (own_entry,), F32, 0, True, 1
    )
    cross_queries = product(second_normed, cross_query).astype(BF16)
    weight_text = cross_text.reshape(text_width, -1)
    text_pairs = product(caption, weight_text).astype(BF16)
    cross_mixed = attend_forward(images, heads_here, cross_queries, text_pairs)
    own_cross, third_normed = step(
        cross_mixed, cross_out, NN, post_forward, gains[2], (own_self,), F32, 0, True, 2
    )

    feed_grad = jnp.where(mask_column, out_grad, jnp.zeros_like(out_grad))
    own_feed_grad = own_rows(feed_grad).astype(F32)
    hidden = product(third_normed, feed_expand)
    active = gelu_exact(hidden).astype(BF16)
    shrink_sum = image_sum(product(active, feed_grad, TN), 1)
    grad_active = product(feed_grad, feed_shrink, NT)
    _, gelu_pull = jax.vjp(gelu_exact, hidden)
    grad_hidden = gelu_pull(grad_active)[0].astype(BF16)
    expand_sum = image_sum(product(third_normed, grad_hidden, TN), 0)
    own_before_feed, cross_grad, third_gain = step(
        grad_hidden, feed_expand, NT, post_backward, gains[2], (own_feed_grad, own_cross), F32, 1, True, 3
    )

    cross_out_sum = image_sum(product(cross_mixed, cross_grad, TN), 1)
    grad_cross_mixed = product(cross_grad, cross_out, NT).astype(BF16)
    grad_cross_queries, grad_text_pairs = attend_backward(
        images, heads_here, cross_queries, text_pairs, grad_cross_mixed
    )
    cross_query_sum = image_sum(product(second_normed, grad_cross_queries, TN), 0)
    cross_text_sum = image_sum(product(caption, grad_text_pairs, TN), 0)
    caption_grad = lax.psum_scatter(
        product(grad_text_pairs, weight_text, NT).astype(BF16), "mp", scatter_dimension=1, tiled=True
    ).astype(F32)
    own_before_cross, self_grad, second_gain = step(
        grad_cross_queries, cross_query, NT, post_backward, gains[1], (own_before_feed, own_self), F32, 1, True, 4
    )

    self_out_sum = image_sum(product(self_mixed, self_grad, TN), 1)
    grad_self_mixed = product(self_grad, attention_out, NT).astype(BF16)
    grad_projected = attend_backward(images, heads_here, projected, projected, grad_self_mixed)
    self_in_sum = image_sum(product(first_normed, grad_projected, TN), 0)
    tokens_grad, first_gain, embed_term = step(
        grad_projected, weight_in, NT, post_entry, gains[0],
        (own_before_cross, own_entry, own_float), F32, 2, False, 5,
    )
    (mixed_out,) = step(
        active, feed_shrink, NN, post_plain, gains[0], (own_cross,), BF16, 0, False, 6
    )

    small_terms = jnp.concatenate([first_gain, second_gain, third_gain, embed_term], axis=0)
    small_sums = lax.psum_scatter(small_terms, ("img", "mp"), scatter_dimension=1, tiled=True)
    return (
        mixed_out,
        tokens_grad,
        caption_grad,
        small_sums[3],
        small_sums[0:3],
        self_in_sum.reshape(-1, 3, attention_in.shape[2]),
        self_out_sum,
        cross_query_sum,
        cross_text_sum.reshape(-1, 2, cross_text.shape[2]),
        cross_out_sum,
        expand_sum,
        shrink_sum,
    )


def solution(mesh):
    step = square_step if mesh.shape["mp"] == 4 else plain_step
    return jax.shard_map(
        functools.partial(body, step),
        mesh=mesh,
        in_specs=(
            P("img", None),
            P("img", None),
            P("img", None),
            P("img", None),
            P(),
            P(),
            P(None, None, "mp"),
            P("mp", None),
            P(None, "mp"),
            P(None, None, "mp"),
            P("mp", None),
            P(None, "mp"),
            P("mp", None),
        ),
        out_specs=(
            P(("img", "mp"), None),
            P(("img", "mp"), None),
            P("img", "mp"),
            P(("img", "mp")),
            P(None, ("img", "mp")),
            P("img", None, "mp"),
            P("mp", "img"),
            P("img", "mp"),
            P("img", None, "mp"),
            P("mp", "img"),
            P("img", "mp"),
            P("mp", "img"),
        ),
        check_vma=False,
    )
```

```python
import functools
import math

import jax
import jax.numpy as jnp
from jax import lax
from jax.experimental import pallas as pl
from jax.experimental.pallas import tpu as pltpu
from jax.sharding import PartitionSpec as P

HDIM = 128
EPSILON = 1e-05
SCALE = 1.0 / math.sqrt(HDIM)
VMEM_BYTES = 58 * 1024 * 1024
MESH = pl.DeviceIdType.MESH
BF16 = jnp.bfloat16
F32 = jnp.float32

NN = (((1,), (0,)), ((), ()))
NT = (((1,), (1,)), ((), ()))
TN = (((0,), (0,)), ((), ()))


def product(left, right, dims=NN):
    return lax.dot_general(left, right, dims, preferred_element_type=F32)


def image_sum(part, dimension=0):
    return lax.psum_scatter(part, "img", scatter_dimension=dimension, tiled=True).astype(F32)


def rows_product(left, right):
    return product(left, right, TN).astype(BF16)


def norm_parts(rows_in):
    centre = rows_in - jnp.mean(rows_in, axis=-1, keepdims=True)
    root_inverse = lax.rsqrt(jnp.mean(centre * centre, axis=-1, keepdims=True) + EPSILON)
    return (centre * root_inverse, root_inverse)


def norm_back(grad_rows, unit_rows, root_inverse, gain_row):
    weighted = grad_rows * gain_row
    middle = jnp.mean(weighted, axis=-1, keepdims=True)
    along = jnp.mean(weighted * unit_rows, axis=-1, keepdims=True)
    return root_inverse * (weighted - middle - unit_rows * along)


def post_forward(total, rows_in, gain):
    fresh = rows_in[0] + total
    unit, _ = norm_parts(fresh)
    return fresh, (unit * gain).astype(BF16), ()


def post_backward(total, rows_in, gain):
    before, source = rows_in
    unit, root = norm_parts(source)
    grad = before + norm_back(total, unit, root, gain)
    return grad, grad.astype(BF16), (jnp.sum(total * unit, axis=0, keepdims=True),)


def post_entry(total, rows_in, gain):
    before, source, mask = rows_in
    unit, root = norm_parts(source)
    grad = before + norm_back(total, unit, root, gain)
    sums = (
        jnp.sum(total * unit, axis=0, keepdims=True),
        jnp.sum(grad * mask, axis=0, keepdims=True),
    )
    return grad * (1.0 - mask), None, sums


def post_plain(total, rows_in, gain):
    return (rows_in[0] + total).astype(BF16), None, ()


def remote(source, target, send, recv, device):
    return pltpu.make_async_remote_copy(
        src_ref=source,
        dst_ref=target,
        send_sem=send,
        recv_sem=recv,
        device_id=device,
        device_id_type=MESH,
    )


def greet(targets):
    barrier = pltpu.get_barrier_semaphore()
    for target in targets:
        pl.semaphore_signal(barrier, inc=1, device_id=target, device_id_type=MESH)
    pl.semaphore_wait(barrier, len(targets))


class Loader:
    def __init__(self, sources, targets, sem):
        self.targets = targets
        self.copies = [
            pltpu.make_async_copy(source, target, sem.at[i])
            for i, (source, target) in enumerate(zip(sources, targets))
        ]
        self.waiting = set()

    def start(self, i):
        self.copies[i].start()
        self.waiting.add(i)

    def got(self, i):
        if i in self.waiting:
            self.waiting.remove(i)
            self.copies[i].wait()
        return self.targets[i]


class Square:
    def __init__(self):
        self.spot = lax.axis_index("mp")
        up, across = lax.div(self.spot, 2), lax.rem(self.spot, 2)
        self.beside = up * 2 + (1 - across)
        self.above = (1 - up) * 2 + across
        self.corner = (1 - up) * 2 + (1 - across)
        self.peers = (self.beside, self.above)
        self.targets = [{"mp": self.beside}, {"mp": self.above}]


class LineSum:
    width = 512

    def __init__(self, lhs_refs, rhs_refs, pieces, refs, loads=None):
        self.loads = loads
        self.lhs_refs, self.rhs_refs, self.pieces = lhs_refs, rhs_refs, pieces
        self.core_out, self.core_in, self.own, self.line_in = refs[:4]
        self.core_send, self.core_recv, self.line_send, self.line_recv = refs[4:]
        self.count = len(pieces)
        self.share = self.own.shape[2]
        self.place = lax.axis_index("img")
        self.line, self.core = lax.div(self.place, 2), lax.rem(self.place, 2)
        self.twin = self.line * 2 + (1 - self.core)
        self.others = [lax.rem(self.line + j, 4) * 2 + self.core for j in (1, 2, 3)]
        self.targets = [{"img": self.twin}] + [{"img": o} for o in self.others]

    @staticmethod
    def scratch(count, share):
        dma = pltpu.SemaphoreType.DMA
        width = LineSum.width
        return [
            pltpu.VMEM((count, 2, share, width), BF16),
            pltpu.VMEM((count, 2, share, width), BF16),
            pltpu.VMEM((count, 4, share, width), BF16),
            pltpu.VMEM((count, 2, 3, share, width), BF16),
            dma((count, 2)),
            dma((count, 2)),
            dma((count, 2, 3)),
            dma((count, 2, 3)),
        ]

    def core_copy(self, g, k):
        slot = lax.rem(k, 2)
        return remote(
            self.core_out.at[g, slot],
            self.core_in.at[g, slot],
            self.core_send.at[g, slot],
            self.core_recv.at[g, slot],
            {"img": self.twin},
        )

    def line_copy(self, g, way, s, chunk):
        return remote(
            self.own.at[g, chunk],
            self.line_in.at[g, way, s],
            self.line_send.at[g, way, s],
            self.line_recv.at[g, way, s],
            {"img": self.place + (2 if way == 0 else -2)},
        )

    def chunk_at(self, k):
        low = (3 - k) - lax.div(self.line + k, 3)
        high = k + lax.div(k, jnp.maximum(self.line, 1))
        chosen = jnp.where(self.line < 2, low, high)
        return jnp.where(k == 3, self.line, chosen)

    def distance(self, way):
        return self.line if way == 0 else 3 - self.line

    def multiply(self, g, k):
        lhs_at, rhs_at, column = self.pieces[g]
        chunk = self.chunk_at(k)
        if self.loads:
            self.loads.got(lhs_at)
            self.loads.got(len(self.lhs_refs) + rhs_at)

        @pl.when(k >= 2)
        def _():
            self.core_copy(g, k).wait_send()

        for mine in (False, True):
            part = self.core if mine else 1 - self.core
            at = pl.ds(pl.multiple_of((chunk * 2 + part) * self.share, 128), self.share)
            done = product(
                self.lhs_refs[lhs_at][:, at],
                self.rhs_refs[rhs_at][:, column : column + self.width],
                TN,
            ).astype(BF16)
            if mine:
                self.own[g, chunk] = done
            else:
                self.core_out[g, lax.rem(k, 2)] = done
                self.core_copy(g, k).start()

    def add(self, g, chunk, arrived):
        self.own[g, chunk] = (self.own[g, chunk].astype(F32) + arrived.astype(F32)).astype(BF16)

    def send_on(self, g, k):
        self.core_copy(g, k).wait_recv()
        self.add(g, self.chunk_at(k), self.core_in[g, lax.rem(k, 2)])
        for way in range(2):
            gone = self.distance(way)
            to = 3 - k + self.line if way == 0 else k - 3 + self.line

            @pl.when((gone <= k) & (k < 3))
            def _():
                @pl.when(gone >= 1)
                def _():
                    self.line_copy(g, way, k - 1, to).wait_recv()
                    self.add(g, to, self.line_in[g, way, k - 1])

                self.line_copy(g, way, k, to).start()

    def step(self, k):
        for g in range(self.count + 1):
            if g < self.count:
                self.multiply(g, k)
            if g > 0:
                self.send_on(g - 1, k)

    def steps(self, first, last):
        def one(k, carry):
            self.step(k)
            return carry

        lax.fori_loop(first, last, one, 0)

    def collect(self, g):
        for way in range(2):

            @pl.when(self.distance(way) >= 1)
            def _():
                self.line_copy(g, way, 2, self.line).wait_recv()
                self.add(g, self.line, self.line_in[g, way, 2])

        return self.own[g, self.line].astype(F32)

    def settle(self):
        for g in range(self.count):
            for k in (2, 3):
                self.core_copy(g, k).wait_send()

        def one(k, carry):
            for g in range(self.count):
                for way in range(2):

                    @pl.when(self.distance(way) <= k)
                    def _():
                        self.line_copy(g, way, k, self.line).wait_send()

            return carry

        lax.fori_loop(0, 3, one, 0)


def square_kernel(post, dims, row_count, sum_count, gather, tile, pieces, flip, *refs):
    big = 4 if pieces else 2
    gain_ref, sources, refs = refs[0], refs[1 : 1 + big + row_count], refs[1 + big + row_count :]
    wide_ref, refs = refs[0], refs[1:]
    if gather:
        full_ref, refs = refs[0], refs[1:]
    sum_refs, refs = refs[:sum_count], refs[sum_count:]
    if pieces:
        weight_out, refs = refs[0], refs[1:]
    first_out, first_in, second_out, second_in, mine, send_sem, recv_sem = refs[:7]
    loads = Loader(sources, refs[7 : 7 + len(sources)], refs[7 + len(sources)])
    refs = refs[8 + len(sources) :]
    for i in (2, 3, 0, 1)[4 - big :] if pieces else (0, 1):
        loads.start(i)
    for i in range(big, big + row_count):
        loads.start(i)
    lhs_ref, weight_ref = loads.targets[:2]
    row_refs = loads.targets[big:]
    square = Square()
    spot, beside, above, corner, peers = (
        square.spot, square.beside, square.above, square.corner, square.peers
    )
    targets = square.targets
    if pieces:
        sums = LineSum((loads.targets[2],), (loads.targets[3],), pieces, refs)
        targets = targets + sums.targets
    share = mine.shape[0]
    half = mine.shape[1] // 2
    columns = 256
    greet(targets)

    def rows_of(owner):
        return pl.ds(pl.multiple_of(owner * share, 16), share)

    def copy_to(source, target, slot, peer):
        copy = remote(source, target, send_sem.at[slot], recv_sem.at[slot], {"mp": peer})
        copy.start()
        return copy

    def partial_into(owner, side, put):
        block = rows_of(owner)

        def step(j, carry):
            at = pl.multiple_of(j * columns, columns)
            there = pl.ds(pl.multiple_of(side * half + j * columns, columns), columns)
            if dims == NT:
                part = product(lhs_ref[block, :], weight_ref[there, :], NT)
            else:
                part = product(lhs_ref[block, :], weight_ref[:, there])
            put(pl.ds(at, columns), there, part)
            return carry

        lax.fori_loop(0, half // columns, step, 0)

    if pieces:
        loads.got(2)
        loads.got(3)
        sums.step(0)
    loads.got(0)
    loads.got(1)
    copies = []
    for order, owners in ((0, (corner, corner)), (1, (beside, above))):
        for side in range(2):

            def put(at, there, part, side=side, order=order):
                first_out[side, order, :, at] = part.astype(BF16)

            partial_into(owners[side], side, put)
            copies.append(
                copy_to(
                    first_out.at[side, order], first_in.at[side, order], side * 2 + order, peers[side]
                )
            )

    def put_mine(at, there, part):
        mine[:, there] = part

    for side, owner in ((0, above), (1, beside)):

        def put_on(at, there, part, side=side):
            second_out[side, :, at] = part.astype(BF16)

        partial_into(owner, side, put_on)
    onward = []
    for side in range(2):
        copies[side].wait_recv()
        second_out[side] = (
            second_out[side].astype(F32) + first_in[side, 0].astype(F32)
        ).astype(BF16)
        onward.append(copy_to(second_out.at[side], second_in.at[side], 4 + side, peers[1 - side]))
    for side in range(2):
        partial_into(spot, side, put_mine)
    if pieces:
        sums.steps(1, 2)
    for side in range(2):
        copies[2 + side].wait_recv()
    for side in range(2):
        onward[side].wait_recv()
    for i in range(big, big + row_count):
        loads.got(i)

    for sum_ref in sum_refs:
        sum_ref[...] = jnp.zeros_like(sum_ref)

    def finish(t, carry):
        at = pl.ds(pl.multiple_of(t * tile, 16), tile)
        total = jnp.concatenate(
            [
                mine[at, side * half : (side + 1) * half]
                + first_in[side, 1, at, :].astype(F32)
                + second_in[side, at, :].astype(F32)
                for side in range(2)
            ],
            axis=1,
        )
        wide, narrow, terms = post(total, tuple(r[at, :] for r in row_refs), gain_ref[...])
        wide_ref[at, :] = wide
        if gather:
            full_ref[pl.ds(pl.multiple_of(spot * share + t * tile, 16), tile), :] = narrow
        for sum_ref, term in zip(sum_refs, terms):
            sum_ref[...] += term
        return carry

    lax.fori_loop(0, share // tile, finish, 0)

    if gather:

        def spread(owner, side, slot, peer):
            where = full_ref.at[rows_of(owner), pl.ds(side * half, half)]
            return copy_to(where, where, slot, peer)

        first = [spread(spot, 0, 6, above), spread(spot, 1, 7, beside)]
        rest = [spread(spot, 0, 8, beside), spread(spot, 1, 9, above)]
        first[0].wait_recv()
        rest.append(spread(above, 0, 10, beside))
        first[1].wait_recv()
        rest.append(spread(beside, 1, 11, above))
        if pieces:
            sums.steps(2, 4)
        for copy in rest:
            copy.wait_recv()
        for copy in first + rest:
            copy.wait_send()
    for copy in copies + onward:
        copy.wait_send()
    if pieces:
        for g in range(len(pieces)):
            at = slice(g * sums.width, (g + 1) * sums.width)
            if flip:
                weight_out[at, :] = sums.collect(g).T
            else:
                weight_out[:, at] = sums.collect(g)
        sums.settle()


def square_step(
    lhs, weight, dims, post, gain, rows_in, wide_type, sum_count, gather, ident, grads=(), flip=False
):
    rows = lhs.shape[0]
    width = gain.shape[1]
    share = rows // 4
    outs = [jax.ShapeDtypeStruct((share, width), wide_type)]
    if gather:
        outs.append(jax.ShapeDtypeStruct((rows, width), BF16))
    outs += [jax.ShapeDtypeStruct((1, width), F32)] * sum_count
    pieces, extra = (), []
    if grads:
        pieces = tuple((0, 0, c) for c in range(0, grads[1].shape[1], LineSum.width))
        kept = grads[0].shape[1] // 8
        shape = (kept, grads[1].shape[1])
        outs.append(jax.ShapeDtypeStruct(shape[::-1] if flip else shape, F32))
        extra = LineSum.scratch(len(pieces), kept)
    half = width // 2
    sources = (lhs, weight, *grads, *rows_in)
    vmem = pl.BlockSpec(memory_space=pltpu.VMEM)
    slots = 12 if gather else 6
    return pl.pallas_call(
        functools.partial(
            square_kernel, post, dims, len(rows_in), sum_count, gather, 32, pieces, flip
        ),
        out_shape=outs,
        in_specs=[vmem] + [pl.BlockSpec(memory_space=pl.ANY)] * len(sources),
        out_specs=[vmem] * len(outs),
        scratch_shapes=[
            pltpu.VMEM((2, 2, share, half), BF16),
            pltpu.VMEM((2, 2, share, half), BF16),
            pltpu.VMEM((2, share, half), BF16),
            pltpu.VMEM((2, share, half), BF16),
            pltpu.VMEM((share, width), F32),
            pltpu.SemaphoreType.DMA((slots,)),
            pltpu.SemaphoreType.DMA((slots,)),
        ]
        + [pltpu.VMEM(a.shape, a.dtype) for a in sources]
        + [pltpu.SemaphoreType.DMA((len(sources),))]
        + extra,
        compiler_params=pltpu.CompilerParams(
            collective_id=ident, has_side_effects=True, vmem_limit_bytes=VMEM_BYTES
        ),
        cost_estimate=pl.CostEstimate(
            flops=60_000_000_000,
            bytes_accessed=2 * (lhs.size + weight.size + 6 * share * width),
            transcendentals=0,
        ),
    )(gain, *sources)


def plain_step(lhs, weight, dims, post, gain, rows_in, wide_type, sum_count, gather, ident, grads=(), flip=False):
    part = product(lhs, weight, dims).astype(BF16)
    total = lax.psum_scatter(part, "mp", scatter_dimension=0, tiled=True).astype(F32)
    wide, narrow, sums = post(total, rows_in, gain)
    outs = [wide.astype(wide_type)]
    if gather:
        outs.append(lax.all_gather(narrow, "mp", axis=0, tiled=True))
    outs += list(sums)
    if grads:
        outs.append(image_sum(rows_product(grads[0], grads[1])))
        if flip:
            outs[-1] = outs[-1].T
    return outs


def line_kernel(pieces, lhs_count, rhs_count, *refs):
    sources, refs = refs[: lhs_count + rhs_count], refs[lhs_count + rhs_count :]
    loads = Loader(sources, refs[-len(sources) - 1 : -1], refs[-1])
    refs = refs[: -len(sources) - 1]
    lhs_refs, rhs_refs = loads.targets[:lhs_count], loads.targets[lhs_count:]
    for i in range(lhs_count):
        loads.start(i)
        loads.start(lhs_count + i)
    small_ref, mixed_ref, caption_ref, base_ref = refs[:4]
    in_out, self_out, query_out, cross_out, total_ref, mixed_out, caption_out = refs[4:11]
    line_refs, refs = refs[11:19], refs[19:]
    small_in, held, first_in, second_out, second_in = refs[:5]
    small_send, small_recv, load_sem, flat_send, flat_recv = refs[5:]
    square = Square()
    spot, beside, above, corner, peers = (
        square.spot, square.beside, square.above, square.corner, square.peers
    )
    sums = LineSum(lhs_refs, rhs_refs, pieces, line_refs, loads)
    targets = [sums.targets[0]] + square.targets + sums.targets[1:]
    width = sums.width
    rows, columns = held.shape[2], held.shape[3]
    greet(targets)

    def block(job, owner, side):
        if job == 0:
            at = pl.ds(pl.multiple_of(owner * rows, 16), rows)
            return mixed_ref.at[at, pl.ds(side * columns, columns)]
        at = pl.ds(pl.multiple_of(owner * columns, 128), columns)
        return caption_ref.at[pl.ds(side * rows, rows), at]

    def load(job, slot, owner, side):
        return pltpu.make_async_copy(
            block(job, owner, side), held.at[job, slot], load_sem.at[job, slot]
        )

    def first_copy(job, side, order):
        owner = corner if order == 0 else peers[side]
        slot = side * 2 + order
        return remote(
            block(job, owner, side),
            first_in.at[job, slot],
            flat_send.at[job, slot],
            flat_recv.at[job, slot],
            {"mp": peers[side]},
        )

    def second_copy(job, side):
        return remote(
            second_out.at[job, side],
            second_in.at[job, side],
            flat_send.at[job, 4 + side],
            flat_recv.at[job, 4 + side],
            {"mp": peers[1 - side]},
        )

    def flat_start(job):
        for order in range(2):
            for side in range(2):
                first_copy(job, side, order).start()
        for side in range(2):
            load(job, side, peers[1 - side], side).start()
            load(job, 2 + side, spot, side).start()

    def flat_forward(job):
        for side in range(2):
            load(job, side, peers[1 - side], side).wait()
            first_copy(job, side, 0).wait_recv()
            second_out[job, side] = (
                held[job, side].astype(F32) + first_in[job, side * 2].astype(F32)
            ).astype(BF16)
            second_copy(job, side).start()

    def flat_finish(job):
        for side in range(2):
            load(job, 2 + side, spot, side).wait()
            first_copy(job, side, 1).wait_recv()
            second_copy(job, side).wait_recv()
            total = (
                held[job, 2 + side].astype(F32)
                + first_in[job, side * 2 + 1].astype(F32)
                + second_in[job, side].astype(F32)
            )
            if job == 0:
                at = slice(side * columns, (side + 1) * columns)
                mixed_out[:, at] = (base_ref[:, at] + total).astype(BF16)
            else:
                caption_out[side * rows : (side + 1) * rows, :] = total
        for side in range(2):
            for order in range(2):
                first_copy(job, side, order).wait_send()
            second_copy(job, side).wait_send()

    def small_step(slot, device):
        copy = remote(
            total_ref, small_in.at[slot], small_send.at[slot], small_recv.at[slot], device
        )
        copy.start()
        return copy

    total_ref[...] = small_ref[...]
    flat_start(0)
    flat_start(1)
    sums.step(0)
    flat_forward(0)
    sums.steps(1, 3)
    flat_forward(1)
    for slot, device in enumerate(targets[:3]):
        copy = small_step(slot, device)
        copy.wait()
        total_ref[...] += small_in[slot]
    wide = [small_step(3 + j, device) for j, device in enumerate(targets[3:])]
    sums.steps(3, 4)
    flat_finish(0)
    flat_finish(1)
    for copy in wide:
        copy.wait()
    total_ref[...] += small_in[3] + small_in[4] + small_in[5]

    places = ((in_out, 0), (in_out, 1), (in_out, 2), (self_out, None), (query_out, 0), (cross_out, None))
    for g, (target, column) in enumerate(places):
        done = sums.collect(g)
        if column is None:
            target[...] = done.T
        else:
            target[:, column * width : (column + 1) * width] = done
    sums.settle()


def line_sums(lhs_list, rhs_list, pieces, small, mixed_part, caption_part, base, ident):
    width = 512
    share = lhs_list[0].shape[1] // 8
    count = len(pieces)
    sources = (*lhs_list, *rhs_list)
    rows, columns = base.shape[0], base.shape[1] // 2
    outs = [
        jax.ShapeDtypeStruct((share, 3 * width), F32),
        jax.ShapeDtypeStruct((width, share), F32),
        jax.ShapeDtypeStruct((share, width), F32),
        jax.ShapeDtypeStruct((width, share), F32),
        jax.ShapeDtypeStruct(small.shape, F32),
        jax.ShapeDtypeStruct(base.shape, BF16),
        jax.ShapeDtypeStruct((caption_part.shape[0], columns), F32),
    ]
    vmem = pl.BlockSpec(memory_space=pltpu.VMEM)
    hbm = pl.BlockSpec(memory_space=pl.ANY)
    dma = pltpu.SemaphoreType.DMA
    return pl.pallas_call(
        functools.partial(line_kernel, pieces, len(lhs_list), len(rhs_list)),
        out_shape=outs,
        in_specs=[hbm] * len(sources) + [vmem, hbm, hbm, vmem],
        out_specs=[vmem] * len(outs),
        scratch_shapes=LineSum.scratch(count, share)
        + [
            pltpu.VMEM((6,) + small.shape, F32),
            pltpu.VMEM((2, 4, rows, columns), BF16),
            pltpu.VMEM((2, 4, rows, columns), BF16),
            pltpu.VMEM((2, 2, rows, columns), BF16),
            pltpu.VMEM((2, 2, rows, columns), BF16),
            dma((6,)),
            dma((6,)),
            dma((2, 4)),
            dma((2, 6)),
            dma((2, 6)),
        ]
        + [pltpu.VMEM(a.shape, a.dtype) for a in sources]
        + [dma((len(sources),))],
        compiler_params=pltpu.CompilerParams(
            collective_id=ident, has_side_effects=True, vmem_limit_bytes=60 * 1024 * 1024
        ),
        cost_estimate=pl.CostEstimate(
            flops=60_000_000_000, bytes_accessed=40_000_000, transcendentals=0
        ),
    )(*sources, small, mixed_part, caption_part, base)


def softmax_rows(queries, keys_in):
    scores = product(queries, keys_in, NT) * SCALE
    powers = jnp.exp(scores - jnp.max(scores, axis=-1, keepdims=True))
    return powers * (1.0 / jnp.sum(powers, axis=-1, keepdims=True))


def attend_forward_kernel(heads, separate, query_ref, pair_ref, out_ref):
    key_at = 0 if separate else heads
    for h in range(heads):
        queries = query_ref[:, h * HDIM : (h + 1) * HDIM]
        keys_in = pair_ref[:, (key_at + h) * HDIM : (key_at + h + 1) * HDIM]
        values_in = pair_ref[:, (key_at + heads + h) * HDIM : (key_at + heads + h + 1) * HDIM]
        probs = softmax_rows(queries, keys_in).astype(BF16)
        out_ref[:, h * HDIM : (h + 1) * HDIM] = product(probs, values_in).astype(BF16)


def attend_backward_kernel(heads, separate, query_ref, pair_ref, grad_ref, *outs):
    key_at = 0 if separate else heads
    query_out, pair_out = outs if separate else (outs[0], outs[0])
    for h in range(heads):
        own = slice(h * HDIM, (h + 1) * HDIM)
        key_slice = slice((key_at + h) * HDIM, (key_at + h + 1) * HDIM)
        value_slice = slice((key_at + heads + h) * HDIM, (key_at + heads + h + 1) * HDIM)
        queries, keys_in, values_in = query_ref[:, own], pair_ref[:, key_slice], pair_ref[:, value_slice]
        grad = grad_ref[:, own]
        probs = softmax_rows(queries, keys_in)
        pair_out[:, value_slice] = product(probs.astype(BF16), grad, TN).astype(BF16)
        grad_probs = product(grad, values_in, NT)
        centred = grad_probs - jnp.sum(probs * grad_probs, axis=-1, keepdims=True)
        grad_scores = (probs * centred * SCALE).astype(BF16)
        query_out[:, own] = product(grad_scores, keys_in).astype(BF16)
        pair_out[:, key_slice] = product(grad_scores, queries, TN).astype(BF16)


def image_blocks(images, *arrays):
    return [pl.BlockSpec((a.shape[0] // images, a.shape[1]), lambda i: (i, 0)) for a in arrays]


def attend_forward(images, heads, queries, pairs):
    separate = queries is not pairs
    out = jax.ShapeDtypeStruct((queries.shape[0], heads * HDIM), BF16)
    return pl.pallas_call(
        functools.partial(attend_forward_kernel, heads, separate),
        grid=(images,),
        out_shape=out,
        in_specs=image_blocks(images, queries, pairs),
        out_specs=image_blocks(images, out)[0],
        compiler_params=pltpu.CompilerParams(vmem_limit_bytes=VMEM_BYTES),
    )(queries, pairs)


def attend_backward(images, heads, queries, pairs, grad):
    separate = queries is not pairs
    outs = [jax.ShapeDtypeStruct(queries.shape, BF16)]
    if separate:
        outs.append(jax.ShapeDtypeStruct(pairs.shape, BF16))
    result = pl.pallas_call(
        functools.partial(attend_backward_kernel, heads, separate),
        grid=(images,),
        out_shape=outs,
        in_specs=image_blocks(images, queries, pairs, grad),
        out_specs=image_blocks(images, *outs),
        compiler_params=pltpu.CompilerParams(vmem_limit_bytes=VMEM_BYTES),
    )(queries, pairs, grad)
    return result if separate else result[0]


def gelu_exact(values_in):
    return jax.nn.gelu(values_in, approximate=False)


def body(
    square,
    tokens,
    caption,
    masked,
    out_grad,
    mask_embed,
    norm_gains,
    attention_in,
    attention_out,
    cross_query,
    cross_text,
    cross_out,
    feed_expand,
    feed_shrink,
):
    step = square_step if square else plain_step
    axis_count = lax.axis_size("mp")
    axis_place = lax.axis_index("mp")
    images, length = masked.shape
    rows_all = images * length
    share_rows = rows_all // axis_count
    model_width = tokens.shape[1]
    text_width = caption.shape[1]
    heads_here = attention_in.shape[2] // HDIM

    def own_rows(rows_in):
        return lax.dynamic_slice_in_dim(rows_in, axis_place * share_rows, share_rows, 0)

    gains = [norm_gains[k : k + 1] for k in range(3)]
    mask_column = (masked.reshape(rows_all, 1) > 0)

    def enter(rows_in, mask):
        return jnp.where(mask, mask_embed.astype(F32)[None, :], rows_in.astype(F32))

    own_mask = own_rows(mask_column)
    own_float = own_mask.astype(F32)
    own_entry = enter(own_rows(tokens), own_mask)
    first_unit, _ = norm_parts(enter(tokens, mask_column))
    first_normed = (first_unit * gains[0]).astype(BF16)
    weight_in = attention_in.reshape(model_width, -1)
    projected = product(first_normed, weight_in).astype(BF16)
    self_mixed = attend_forward(images, heads_here, projected, projected)
    own_self, second_normed = step(
        self_mixed, attention_out, NN, post_forward, gains[1], (own_entry,), F32, 0, True, 1
    )
    cross_queries = product(second_normed, cross_query).astype(BF16)
    weight_text = cross_text.reshape(text_width, -1)
    text_pairs = product(caption, weight_text).astype(BF16)
    cross_mixed = attend_forward(images, heads_here, cross_queries, text_pairs)
    own_cross, third_normed = step(
        cross_mixed, cross_out, NN, post_forward, gains[2], (own_self,), F32, 0, True, 2
    )

    feed_grad = jnp.where(mask_column, out_grad, jnp.zeros_like(out_grad))
    own_feed_grad = own_rows(feed_grad).astype(F32)
    hidden = product(third_normed, feed_expand)
    active = gelu_exact(hidden).astype(BF16)
    grad_active = product(feed_grad, feed_shrink, NT)
    _, gelu_pull = jax.vjp(gelu_exact, hidden)
    grad_hidden = gelu_pull(grad_active)[0].astype(BF16)
    own_before_feed, cross_grad, third_gain, shrink_sum = step(
        grad_hidden, feed_expand, NT, post_backward, gains[2], (own_feed_grad, own_cross), F32, 1, True, 3,
        (feed_grad, active), True,
    )

    grad_cross_mixed = product(cross_grad, cross_out, NT).astype(BF16)
    grad_cross_queries, grad_text_pairs = attend_backward(
        images, heads_here, cross_queries, text_pairs, grad_cross_mixed
    )
    caption_part = product(grad_text_pairs, weight_text, NT).astype(BF16)
    own_before_cross, self_grad, second_gain, expand_sum = step(
        grad_cross_queries, cross_query, NT, post_backward, gains[1], (own_before_feed, own_self), F32, 1, True, 4,
        (third_normed, grad_hidden),
    )

    self_grad, grad_text_pairs = lax.optimization_barrier((self_grad, grad_text_pairs))
    cross_text_sum = image_sum(rows_product(caption, grad_text_pairs))
    grad_self_mixed = product(self_grad, attention_out, NT).astype(BF16)
    grad_projected = attend_backward(images, heads_here, projected, projected, grad_self_mixed)
    tokens_grad, first_gain, embed_term = step(
        grad_projected, weight_in, NT, post_entry, gains[0],
        (own_before_cross, own_entry, own_float), F32, 2, False, 5,
    )
    terms = [first_gain, second_gain, third_gain, embed_term]
    if square:
        self_in_sum, self_out_sum, cross_query_sum, cross_out_sum, small_totals, mixed_out, caption_grad = line_sums(
            [first_normed, self_grad, second_normed, cross_grad],
            [grad_projected, self_mixed, grad_cross_queries, cross_mixed],
            ((0, 0, 0), (0, 0, 512), (0, 0, 1024), (1, 1, 0), (2, 2, 0), (3, 3, 0)),
            jnp.concatenate(terms + [jnp.zeros_like(embed_term)] * 4, axis=0),
            product(active, feed_shrink).astype(BF16),
            caption_part,
            own_cross,
            6,
        )
        slice_width = model_width // (lax.axis_size("img") * axis_count)
        slice_at = (lax.axis_index("img") * axis_count + axis_place) * slice_width
        small_sums = lax.dynamic_slice_in_dim(small_totals, slice_at, slice_width, 1)
    else:
        (mixed_out,) = step(
            active, feed_shrink, NN, post_plain, gains[0], (own_cross,), BF16, 0, False, 0
        )
        caption_grad = lax.psum_scatter(
            caption_part, "mp", scatter_dimension=1, tiled=True
        ).astype(F32)
        small_sums = lax.psum_scatter(
            jnp.concatenate(terms, axis=0), ("img", "mp"), scatter_dimension=1, tiled=True
        )
        self_in_sum = image_sum(rows_product(first_normed, grad_projected))
        self_out_sum = image_sum(rows_product(self_mixed, self_grad), 1)
        cross_query_sum = image_sum(rows_product(second_normed, grad_cross_queries))
        cross_out_sum = image_sum(rows_product(cross_mixed, cross_grad), 1)
    return (
        mixed_out,
        tokens_grad,
        caption_grad,
        small_sums[3],
        small_sums[0:3],
        self_in_sum.reshape(-1, 3, attention_in.shape[2]),
        self_out_sum,
        cross_query_sum,
        cross_text_sum.reshape(-1, 2, cross_text.shape[2]),
        cross_out_sum,
        expand_sum,
        shrink_sum,
    )


def solution(mesh):
    square = mesh.shape["mp"] == 4 and mesh.shape["img"] == 8
    return jax.shard_map(
        functools.partial(body, square),
        mesh=mesh,
        in_specs=(
            P("img", None),
            P("img", None),
            P("img", None),
            P("img", None),
            P(),
            P(),
            P(None, None, "mp"),
            P("mp", None),
            P(None, "mp"),
            P(None, None, "mp"),
            P("mp", None),
            P(None, "mp"),
            P("mp", None),
        ),
        out_specs=(
            P(("img", "mp"), None),
            P(("img", "mp"), None),
            P("img", "mp"),
            P(("img", "mp")),
            P(None, ("img", "mp")),
            P("img", None, "mp"),
            P("mp", "img"),
            P("img", "mp"),
            P("img", None, "mp"),
            P("mp", "img"),
            P("img", "mp"),
            P("mp", "img"),
        ),
        check_vma=False,
    )
```

```python
import dataclasses
import functools
import math
from typing import Any

import jax
import jax.numpy as jnp
from jax import lax
from jax.experimental import pallas as pl
from jax.experimental.pallas import tpu as pltpu
from jax.sharding import PartitionSpec as P

HDIM = 128
EPSILON = 1e-05
SCALE = 1.0 / math.sqrt(HDIM)
VMEM_BYTES = 58 * 1024 * 1024
MESH = pl.DeviceIdType.MESH
BF16 = jnp.bfloat16
F32 = jnp.float32

NN = (((1,), (0,)), ((), ()))
NT = (((1,), (1,)), ((), ()))
TN = (((0,), (0,)), ((), ()))


def product(left, right, dims=NN):
    return lax.dot_general(left, right, dims, preferred_element_type=F32)


def image_sum(part, dimension=0):
    return lax.psum_scatter(part, "img", scatter_dimension=dimension, tiled=True).astype(F32)


def rows_product(left, right):
    return product(left, right, TN).astype(BF16)


def norm_parts(rows_in):
    centre = rows_in - jnp.mean(rows_in, axis=-1, keepdims=True)
    root_inverse = lax.rsqrt(jnp.mean(centre * centre, axis=-1, keepdims=True) + EPSILON)
    return (centre * root_inverse, root_inverse)


def norm_back(grad_rows, unit_rows, root_inverse, gain_row):
    weighted = grad_rows * gain_row
    middle = jnp.mean(weighted, axis=-1, keepdims=True)
    along = jnp.mean(weighted * unit_rows, axis=-1, keepdims=True)
    return root_inverse * (weighted - middle - unit_rows * along)


def post_forward(total, rows_in, gain):
    fresh = rows_in[0] + total
    unit, _ = norm_parts(fresh)
    return fresh, (unit * gain).astype(BF16), ()


def post_backward(total, rows_in, gain):
    before, source = rows_in
    unit, root = norm_parts(source)
    grad = before + norm_back(total, unit, root, gain)
    return grad, grad.astype(BF16), (jnp.sum(total * unit, axis=0, keepdims=True),)


def post_entry(total, rows_in, gain):
    before, source, mask = rows_in
    unit, root = norm_parts(source)
    grad = before + norm_back(total, unit, root, gain)
    sums = (
        jnp.sum(total * unit, axis=0, keepdims=True),
        jnp.sum(grad * mask, axis=0, keepdims=True),
    )
    return grad * (1.0 - mask), None, sums


def remote(source, target, send, recv, device):
    return pltpu.make_async_remote_copy(
        src_ref=source,
        dst_ref=target,
        send_sem=send,
        recv_sem=recv,
        device_id=device,
        device_id_type=MESH,
    )


def greet(targets):
    barrier = pltpu.get_barrier_semaphore()
    for target in targets:
        pl.semaphore_signal(barrier, inc=1, device_id=target, device_id_type=MESH)
    pl.semaphore_wait(barrier, len(targets))


class Loader:
    def __init__(self, sources, targets, sem):
        self.targets = targets
        self.copies = [
            pltpu.make_async_copy(source, target, sem.at[i])
            for i, (source, target) in enumerate(zip(sources, targets))
        ]
        self.waiting = set()

    def start(self, i):
        self.copies[i].start()
        self.waiting.add(i)

    def got(self, i):
        if i in self.waiting:
            self.waiting.remove(i)
            self.copies[i].wait()
        return self.targets[i]


class Square:
    def __init__(self):
        self.spot = lax.axis_index("mp")
        up, across = lax.div(self.spot, 2), lax.rem(self.spot, 2)
        self.beside = up * 2 + (1 - across)
        self.above = (1 - up) * 2 + across
        self.corner = (1 - up) * 2 + (1 - across)
        self.peers = (self.beside, self.above)
        self.targets = [{"mp": self.beside}, {"mp": self.above}]


class LineSum:
    width = 512

    def __init__(self, loads, pieces, refs):
        self.loads, self.pieces = loads, pieces
        self.core_out, self.core_in, self.own, self.line_in = refs[:4]
        self.core_send, self.core_recv, self.line_send, self.line_recv = refs[4:]
        self.count = len(pieces)
        self.share = self.own.shape[2]
        self.place = lax.axis_index("img")
        self.line, self.core = lax.div(self.place, 2), lax.rem(self.place, 2)
        self.twin = self.line * 2 + (1 - self.core)
        self.others = [lax.rem(self.line + j, 4) * 2 + self.core for j in (1, 2, 3)]
        self.targets = [{"img": self.twin}] + [{"img": o} for o in self.others]

    @staticmethod
    def scratch(count, share):
        dma = pltpu.SemaphoreType.DMA
        width = LineSum.width
        return [
            pltpu.VMEM((count, 2, share, width), BF16),
            pltpu.VMEM((count, 2, share, width), BF16),
            pltpu.VMEM((count, 4, share, width), BF16),
            pltpu.VMEM((count, 2, 3, share, width), BF16),
            dma((count, 2)),
            dma((count, 2)),
            dma((count, 2, 3)),
            dma((count, 2, 3)),
        ]

    def core_copy(self, g, k):
        slot = lax.rem(k, 2)
        return remote(
            self.core_out.at[g, slot],
            self.core_in.at[g, slot],
            self.core_send.at[g, slot],
            self.core_recv.at[g, slot],
            {"img": self.twin},
        )

    def line_copy(self, g, way, s, chunk):
        return remote(
            self.own.at[g, chunk],
            self.line_in.at[g, way, s],
            self.line_send.at[g, way, s],
            self.line_recv.at[g, way, s],
            {"img": self.place + (2 if way == 0 else -2)},
        )

    def chunk_at(self, k):
        low = (3 - k) - lax.div(self.line + k, 3)
        high = k + lax.div(k, jnp.maximum(self.line, 1))
        chosen = jnp.where(self.line < 2, low, high)
        return jnp.where(k == 3, self.line, chosen)

    def distance(self, way):
        return self.line if way == 0 else 3 - self.line

    def multiply(self, g, k):
        lhs_at, rhs_at, column = self.pieces[g]
        left, right = self.loads.got(lhs_at), self.loads.got(rhs_at)
        chunk = self.chunk_at(k)

        @pl.when(k >= 2)
        def _():
            self.core_copy(g, k).wait_send()

        for mine in (False, True):
            part = self.core if mine else 1 - self.core
            at = pl.ds(pl.multiple_of((chunk * 2 + part) * self.share, 128), self.share)
            done = product(
                left[:, at],
                right[:, column : column + self.width],
                TN,
            ).astype(BF16)
            if mine:
                self.own[g, chunk] = done
            else:
                self.core_out[g, lax.rem(k, 2)] = done
                self.core_copy(g, k).start()

    def add(self, g, chunk, arrived):
        self.own[g, chunk] = (self.own[g, chunk].astype(F32) + arrived.astype(F32)).astype(BF16)

    def send_on(self, g, k):
        self.core_copy(g, k).wait_recv()
        self.add(g, self.chunk_at(k), self.core_in[g, lax.rem(k, 2)])
        for way in range(2):
            gone = self.distance(way)
            to = 3 - k + self.line if way == 0 else k - 3 + self.line

            @pl.when((gone <= k) & (k < 3))
            def _():
                @pl.when(gone >= 1)
                def _():
                    self.line_copy(g, way, k - 1, to).wait_recv()
                    self.add(g, to, self.line_in[g, way, k - 1])

                self.line_copy(g, way, k, to).start()

    def step(self, k):
        for g in range(self.count + 1):
            if g < self.count:
                self.multiply(g, k)
            if g > 0:
                self.send_on(g - 1, k)

    def steps(self, first, last):
        def one(k, carry):
            self.step(k)
            return carry

        lax.fori_loop(first, last, one, 0)

    def collect(self, g):
        for way in range(2):

            @pl.when(self.distance(way) >= 1)
            def _():
                self.line_copy(g, way, 2, self.line).wait_recv()
                self.add(g, self.line, self.line_in[g, way, 2])

        return self.own[g, self.line].astype(F32)

    def settle(self):
        for g in range(self.count):
            for k in (2, 3):
                self.core_copy(g, k).wait_send()

        def one(k, carry):
            for g in range(self.count):
                for way in range(2):

                    @pl.when(self.distance(way) <= k)
                    def _():
                        self.line_copy(g, way, k, self.line).wait_send()

            return carry

        lax.fori_loop(0, 3, one, 0)


def square_kernel(plan, *refs):
    gain_ref, refs = refs[0], refs[1:]
    given, refs = refs[: plan.given], refs[plan.given :]
    wide_ref, refs = refs[0], refs[1:]
    if plan.gather:
        full_ref, refs = refs[0], refs[1:]
    sum_refs, refs = refs[: plan.sums], refs[plan.sums :]
    weight_outs, refs = refs[: len(plan.grads)], refs[len(plan.grads) :]
    if plan.side:
        side_out, refs = refs[0], refs[1:]
    first_out, first_in, second_out, second_in, mine, send_sem, recv_sem = refs[:7]
    sources = [
        given[at] if span is None else given[at].at[:, span[0] : span[1]] for at, span in plan.loads
    ]
    loads = Loader(sources, refs[7 : 7 + len(sources)], refs[7 + len(sources)])
    refs = refs[8 + len(sources) :]
    pieces, gather, post, dims = plan.pieces, plan.gather, plan.post, plan.dims
    lhs_at, weight_at, row_at = 0, 1, range(2, 2 + plan.rows)
    for piece in pieces:
        for i in piece[:2]:
            if i not in loads.waiting:
                loads.start(i)
    for i in range(len(sources)):
        if i not in loads.waiting:
            loads.start(i)
    lhs_ref, weight_ref = loads.targets[:2]
    row_refs = loads.targets[2 : 2 + plan.rows]
    square = Square()
    spot, beside, above, corner, peers = (
        square.spot, square.beside, square.above, square.corner, square.peers
    )
    targets = square.targets
    if pieces:
        sums = LineSum(loads, pieces, refs)
        targets = targets + sums.targets
    share = mine.shape[0]
    half = mine.shape[1] // 2
    columns, tile = 256, 32
    greet(targets)

    def rows_of(owner):
        return pl.ds(pl.multiple_of(owner * share, 16), share)

    def copy_to(source, target, slot, peer):
        copy = remote(source, target, send_sem.at[slot], recv_sem.at[slot], {"mp": peer})
        copy.start()
        return copy

    def partial_into(owner, side, put):
        block = rows_of(owner)

        def step(j, carry):
            at = pl.multiple_of(j * columns, columns)
            there = pl.ds(pl.multiple_of(side * half + j * columns, columns), columns)
            if dims == NT:
                part = product(lhs_ref[block, :], weight_ref[there, :], NT)
            else:
                part = product(lhs_ref[block, :], weight_ref[:, there])
            put(pl.ds(at, columns), there, part)
            return carry

        lax.fori_loop(0, half // columns, step, 0)

    if pieces:
        sums.step(0)
    loads.got(lhs_at)
    loads.got(weight_at)
    copies = []
    for order, owners in ((0, (corner, corner)), (1, (beside, above))):
        for side in range(2):

            def put(at, there, part, side=side, order=order):
                first_out[side, order, :, at] = part.astype(BF16)

            partial_into(owners[side], side, put)
            copies.append(
                copy_to(
                    first_out.at[side, order], first_in.at[side, order], side * 2 + order, peers[side]
                )
            )

    def put_mine(at, there, part):
        mine[:, there] = part

    for side, owner in ((0, above), (1, beside)):

        def put_on(at, there, part, side=side):
            second_out[side, :, at] = part.astype(BF16)

        partial_into(owner, side, put_on)
    onward = []
    for side in range(2):
        copies[side].wait_recv()
        second_out[side] = (
            second_out[side].astype(F32) + first_in[side, 0].astype(F32)
        ).astype(BF16)
        onward.append(copy_to(second_out.at[side], second_in.at[side], 4 + side, peers[1 - side]))
    for side in range(2):
        partial_into(spot, side, put_mine)
    if pieces:
        sums.steps(1, 2)
    for side in range(2):
        copies[2 + side].wait_recv()
    for side in range(2):
        onward[side].wait_recv()
    for i in row_at:
        loads.got(i)

    for sum_ref in sum_refs:
        sum_ref[...] = jnp.zeros_like(sum_ref)

    def finish(t, carry):
        at = pl.ds(pl.multiple_of(t * tile, 16), tile)
        total = jnp.concatenate(
            [
                mine[at, side * half : (side + 1) * half]
                + first_in[side, 1, at, :].astype(F32)
                + second_in[side, at, :].astype(F32)
                for side in range(2)
            ],
            axis=1,
        )
        wide, narrow, terms = post(total, tuple(r[at, :] for r in row_refs), gain_ref[...])
        wide_ref[at, :] = wide
        if gather:
            full_ref[pl.ds(pl.multiple_of(spot * share + t * tile, 16), tile), :] = narrow
        for sum_ref, term in zip(sum_refs, terms):
            sum_ref[...] += term
        return carry

    lax.fori_loop(0, share // tile, finish, 0)

    def side_product():
        left, right = (loads.got(i) for i in plan.side[:2])

        def one(j, carry):
            at = pl.ds(pl.multiple_of(j * columns, columns), columns)
            if plan.side[2] == NT:
                part = product(left[...], right[at, :], NT)
            else:
                part = product(left[...], right[:, at])
            side_out[:, at] = part.astype(BF16)
            return carry

        lax.fori_loop(0, side_out.shape[1] // columns, one, 0)

    if gather:

        def spread(owner, side, slot, peer):
            where = full_ref.at[rows_of(owner), pl.ds(side * half, half)]
            return copy_to(where, where, slot, peer)

        first = [spread(spot, 0, 6, above), spread(spot, 1, 7, beside)]
        rest = [spread(spot, 0, 8, beside), spread(spot, 1, 9, above)]
        if plan.side:
            side_product()
        first[0].wait_recv()
        rest.append(spread(above, 0, 10, beside))
        first[1].wait_recv()
        rest.append(spread(beside, 1, 11, above))
        if pieces:
            sums.steps(2, 4)
        for copy in rest:
            copy.wait_recv()
        for copy in first + rest:
            copy.wait_send()
    else:
        if pieces:
            sums.steps(2, 3)
        if plan.side:
            side_product()
        if pieces:
            sums.steps(3, 4)
    for copy in copies + onward:
        copy.wait_send()
    if pieces:
        g = 0
        for out, (_, _, start, stop, flip) in zip(weight_outs, plan.grads):
            for column in range(0, stop - start, sums.width):
                at = slice(column, column + sums.width)
                if flip:
                    out[at, :] = sums.collect(g).T
                else:
                    out[:, at] = sums.collect(g)
                g += 1
        sums.settle()


@dataclasses.dataclass
class Plan:
    post: Any
    dims: Any
    rows: int
    sums: int
    gather: bool
    given: int
    loads: tuple
    pieces: tuple
    grads: tuple
    side: Any


def square_step(
    lhs, weight, dims, post, gain, rows_in, wide_type, sum_count, gather, ident, grads=(), side=None
):
    rows = lhs.shape[0]
    width = gain.shape[1]
    share = rows // 4
    given, loads, shapes = [], [], []

    def operand(array, span=None):
        at = next((i for i, a in enumerate(given) if a is array), None)
        if at is None:
            at = len(given)
            given.append(array)
        if span == (0, array.shape[1]):
            span = None
        for i, entry in enumerate(loads):
            if entry[0] == at and entry[1] in (span, None):
                return i, 0 if entry[1] == span else span[0]
        loads.append((at, span))
        stretch = array.shape[1] if span is None else span[1] - span[0]
        shapes.append(pltpu.VMEM((array.shape[0], stretch), array.dtype))
        return len(loads) - 1, 0

    for array in (lhs, weight, *rows_in):
        operand(array)
    outs = [jax.ShapeDtypeStruct((share, width), wide_type)]
    if gather:
        outs.append(jax.ShapeDtypeStruct((rows, width), BF16))
    outs += [jax.ShapeDtypeStruct((1, width), F32)] * sum_count
    side_plan = None
    if side:
        side_plan = (operand(side[0])[0], operand(side[1])[0], side[2])
    pieces, extra = [], []
    for left, right, start, stop, flip in grads:
        at, _ = operand(left)
        to, shift = operand(right, (start, stop))
        pieces += [(at, to, shift + c) for c in range(0, stop - start, LineSum.width)]
        kept = left.shape[1] // 8
        shape = (kept, stop - start)
        outs.append(jax.ShapeDtypeStruct(shape[::-1] if flip else shape, F32))
        extra = LineSum.scratch(len(pieces), kept)
    if side:
        wide = side[1].shape[0] if side[2] == NT else side[1].shape[1]
        outs.append(jax.ShapeDtypeStruct((side[0].shape[0], wide), BF16))
    plan = Plan(
        post, dims, len(rows_in), sum_count, gather, len(given), tuple(loads), tuple(pieces),
        tuple((0, 0) + tuple(g[2:]) for g in grads), side_plan,
    )
    half = width // 2
    vmem = pl.BlockSpec(memory_space=pltpu.VMEM)
    slots = 12 if gather else 6
    return pl.pallas_call(
        functools.partial(square_kernel, plan),
        out_shape=outs,
        in_specs=[vmem] + [pl.BlockSpec(memory_space=pl.ANY)] * len(given),
        out_specs=[vmem] * len(outs),
        scratch_shapes=[
            pltpu.VMEM((2, 2, share, half), BF16),
            pltpu.VMEM((2, 2, share, half), BF16),
            pltpu.VMEM((2, share, half), BF16),
            pltpu.VMEM((2, share, half), BF16),
            pltpu.VMEM((share, width), F32),
            pltpu.SemaphoreType.DMA((slots,)),
            pltpu.SemaphoreType.DMA((slots,)),
        ]
        + shapes
        + [pltpu.SemaphoreType.DMA((len(loads),))]
        + extra,
        compiler_params=pltpu.CompilerParams(
            collective_id=ident, has_side_effects=True, vmem_limit_bytes=VMEM_BYTES
        ),
        cost_estimate=pl.CostEstimate(
            flops=60_000_000_000,
            bytes_accessed=2 * (lhs.size + weight.size + 6 * share * width),
            transcendentals=0,
        ),
    )(gain, *given)


def plain_step(lhs, weight, dims, post, gain, rows_in, wide_type, sum_count, gather, ident, grads=(), side=None):
    part = product(lhs, weight, dims).astype(BF16)
    total = lax.psum_scatter(part, "mp", scatter_dimension=0, tiled=True).astype(F32)
    wide, narrow, sums = post(total, rows_in, gain)
    outs = [wide.astype(wide_type)]
    if gather:
        outs.append(lax.all_gather(narrow, "mp", axis=0, tiled=True))
    outs += list(sums)
    for left, right, start, stop, flip in grads:
        done = image_sum(rows_product(left, right[:, start:stop]))
        outs.append(done.T if flip else done)
    if side:
        outs.append(product(*side).astype(BF16))
    return outs


def line_kernel(pieces, lhs_count, rhs_count, *refs):
    sources, refs = refs[: lhs_count + rhs_count], refs[lhs_count + rhs_count :]
    loads = Loader(sources, refs[-len(sources) - 1 : -1], refs[-1])
    refs = refs[: -len(sources) - 1]
    for i in range(lhs_count):
        loads.start(i)
        loads.start(lhs_count + i)
    small_ref, mixed_ref, caption_ref, tokens_ref = refs[:4]
    in_out, self_out, query_out, cross_out, total_ref, mixed_out, caption_out, tokens_out = refs[4:12]
    line_refs, refs = refs[12:20], refs[20:]
    small_in, held, first_in, second_out, second_in = refs[:5]
    small_send, small_recv, load_sem, flat_send, flat_recv, move_sem, move_send, move_recv = refs[5:]
    square = Square()
    spot, beside, above, corner, peers = (
        square.spot, square.beside, square.above, square.corner, square.peers
    )
    sums = LineSum(loads, pieces, line_refs)
    targets = [sums.targets[0]] + square.targets + sums.targets[1:] + [{"mp": corner}]
    width = sums.width
    rows, columns = held.shape[2], held.shape[3]
    greet(targets)

    low = rows // 3

    def row_block(owner, j):
        return owner * 3 + j

    def block(job, owner, side, j):
        if job == 0:
            b = row_block(owner, j)
            at = pl.ds(pl.multiple_of((lax.rem(b, 4) * 3 + lax.div(b, 4)) * low, low), low)
            return mixed_ref.at[at, pl.ds(side * columns, columns)]
        at = pl.ds(pl.multiple_of(owner * columns, 128), columns)
        return caption_ref.at[pl.ds(side * rows + j * low, low), at]

    thirds = [pl.ds(j * low, low) for j in range(3)]

    def load(job, slot, owner, side):
        return [
            pltpu.make_async_copy(
                block(job, owner, side, j), held.at[job, slot, thirds[j]], load_sem.at[job, slot, j]
            )
            for j in range(3)
        ]

    def first_copy(job, side, order):
        owner = corner if order == 0 else peers[side]
        slot = side * 2 + order
        return [
            remote(
                block(job, owner, side, j),
                first_in.at[job, slot, thirds[j]],
                flat_send.at[job, slot, j],
                flat_recv.at[job, slot, j],
                {"mp": peers[side]},
            )
            for j in range(3)
        ]

    def second_copy(job, side):
        return remote(
            second_out.at[job, side],
            second_in.at[job, side],
            flat_send.at[job, 4 + side, 0],
            flat_recv.at[job, 4 + side, 0],
            {"mp": peers[1 - side]},
        )

    def flat_start(job):
        for order in range(2):
            for side in range(2):
                for copy in first_copy(job, side, order):
                    copy.start()
        for side in range(2):
            for copy in load(job, side, peers[1 - side], side) + load(job, 2 + side, spot, side):
                copy.start()

    def flat_forward(job):
        for side in range(2):
            for copy in load(job, side, peers[1 - side], side):
                copy.wait()
            for copy in first_copy(job, side, 0):
                copy.wait_recv()
            second_out[job, side] = (
                held[job, side].astype(F32) + first_in[job, side * 2].astype(F32)
            ).astype(BF16)
            second_copy(job, side).start()

    def flat_finish(job):
        for side in range(2):
            for copy in load(job, 2 + side, spot, side):
                copy.wait()
            for copy in first_copy(job, side, 1):
                copy.wait_recv()
            second_copy(job, side).wait_recv()
            total = (
                held[job, 2 + side].astype(F32)
                + first_in[job, side * 2 + 1].astype(F32)
                + second_in[job, side].astype(F32)
            )
            if job == 0:
                mixed_out[:, side * columns : (side + 1) * columns] = total.astype(BF16)
            else:
                caption_out[side * rows : (side + 1) * rows, :] = total
        for side in range(2):
            for order in range(2):
                for copy in first_copy(job, side, order):
                    copy.wait_send()
            second_copy(job, side).wait_send()

    def move(i):
        b = i * 4 + spot
        keeper, j = lax.div(b, 3), lax.rem(b, 3)
        target = tokens_out.at[pl.ds(pl.multiple_of(j * low, low), low)]
        away = remote(
            tokens_ref.at[i], target, move_send.at[i], move_recv.at[j], {"mp": keeper}
        )
        here = pltpu.make_async_copy(tokens_ref.at[i], target, move_sem.at[0])
        return keeper, away, here

    def move_start():
        for i in range(3):
            keeper, away, here = move(i)

            @pl.when(keeper != spot)
            def _():
                away.start()

            @pl.when(keeper == spot)
            def _():
                here.start()

    def move_finish():
        for i in range(3):
            keeper, away, here = move(i)

            @pl.when(keeper != spot)
            def _():
                away.wait_send()

            @pl.when(keeper == spot)
            def _():
                here.wait()

        for j in range(3):
            arrival = remote(
                tokens_ref.at[0], tokens_out.at[thirds[j]], move_send.at[0], move_recv.at[j], {"mp": corner}
            )

            @pl.when(lax.rem(row_block(spot, j), 4) != spot)
            def _():
                arrival.wait_recv()

    def small_step(slot, device):
        copy = remote(
            total_ref, small_in.at[slot], small_send.at[slot], small_recv.at[slot], device
        )
        copy.start()
        return copy

    total_ref[...] = small_ref[...]
    flat_start(0)
    flat_start(1)
    move_start()
    sums.step(0)
    flat_forward(0)
    sums.steps(1, 3)
    flat_forward(1)
    for slot, device in enumerate(targets[:3]):
        copy = small_step(slot, device)
        copy.wait()
        total_ref[...] += small_in[slot]
    wide = [small_step(3 + j, device) for j, device in enumerate(targets[3:6])]
    sums.steps(3, 4)
    flat_finish(0)
    flat_finish(1)
    move_finish()
    for copy in wide:
        copy.wait()
    total_ref[...] += small_in[3] + small_in[4] + small_in[5]

    places = ((in_out, 0), (in_out, 1), (in_out, 2), (self_out, None), (query_out, 0), (cross_out, None))
    for g, (target, column) in enumerate(places):
        done = sums.collect(g)
        if column is None:
            target[...] = done.T
        else:
            target[:, column * width : (column + 1) * width] = done
    sums.settle()


def line_sums(lhs_list, rhs_list, pieces, small, mixed_part, caption_part, tokens_rows, ident):
    width = 512
    share = lhs_list[0].shape[1] // 8
    count = len(pieces)
    sources = (*lhs_list, *rhs_list)
    images, low, full = tokens_rows.shape
    rows, columns = images * low, full // 2
    outs = [
        jax.ShapeDtypeStruct((share, 3 * width), F32),
        jax.ShapeDtypeStruct((width, share), F32),
        jax.ShapeDtypeStruct((share, width), F32),
        jax.ShapeDtypeStruct((width, share), F32),
        jax.ShapeDtypeStruct(small.shape, F32),
        jax.ShapeDtypeStruct((rows, full), BF16),
        jax.ShapeDtypeStruct((caption_part.shape[0], columns), F32),
        jax.ShapeDtypeStruct((rows, full), F32),
    ]
    vmem = pl.BlockSpec(memory_space=pltpu.VMEM)
    hbm = pl.BlockSpec(memory_space=pl.ANY)
    dma = pltpu.SemaphoreType.DMA
    return pl.pallas_call(
        functools.partial(line_kernel, pieces, len(lhs_list), len(rhs_list)),
        out_shape=outs,
        in_specs=[hbm] * len(sources) + [vmem, hbm, hbm, hbm],
        out_specs=[vmem] * len(outs),
        scratch_shapes=LineSum.scratch(count, share)
        + [
            pltpu.VMEM((6,) + small.shape, F32),
            pltpu.VMEM((2, 4, rows, columns), BF16),
            pltpu.VMEM((2, 4, rows, columns), BF16),
            pltpu.VMEM((2, 2, rows, columns), BF16),
            pltpu.VMEM((2, 2, rows, columns), BF16),
            dma((6,)),
            dma((6,)),
            dma((2, 4, 3)),
            dma((2, 6, 3)),
            dma((2, 6, 3)),
            dma((1,)),
            dma((3,)),
            dma((3,)),
        ]
        + [pltpu.VMEM(a.shape, a.dtype) for a in sources]
        + [dma((len(sources),))],
        compiler_params=pltpu.CompilerParams(
            collective_id=ident, has_side_effects=True, vmem_limit_bytes=60 * 1024 * 1024
        ),
        cost_estimate=pl.CostEstimate(
            flops=60_000_000_000, bytes_accessed=40_000_000, transcendentals=0
        ),
    )(*sources, small, mixed_part, caption_part, tokens_rows)


def softmax_rows(queries, keys_in):
    scores = product(queries, keys_in, NT) * SCALE
    powers = jnp.exp(scores - jnp.max(scores, axis=-1, keepdims=True))
    return powers * (1.0 / jnp.sum(powers, axis=-1, keepdims=True))


def image_rows(ref, i, columns=slice(None)):
    part = ref[:, i, :, columns]
    return part.reshape(part.shape[0] * part.shape[1], part.shape[2])


def put_image(ref, i, columns, value):
    ref[:, i, :, columns] = value.reshape(ref.shape[0], ref.shape[2], value.shape[1])


def tile_at(j, wide):
    return pl.ds(pl.multiple_of(j * wide, wide), wide)


def attend(queries, keys_in, values_in):
    probs = softmax_rows(queries, keys_in).astype(BF16)
    return product(probs, values_in).astype(BF16)


def attend_forward_kernel(heads, separate, query_ref, pair_ref, out_ref):
    key_at = 0 if separate else heads

    def one(h, carry):
        own, key, value = (tile_at(h + n, HDIM) for n in (0, key_at, key_at + heads))
        done = attend(image_rows(query_ref, 0, own), image_rows(pair_ref, 0, key), image_rows(pair_ref, 0, value))
        put_image(out_ref, 0, own, done)
        return carry

    lax.fori_loop(0, heads, one, 0)


def attend_backward_head(queries, keys_in, values_in, grad):
    probs = softmax_rows(queries, keys_in)
    grad_values = product(probs.astype(BF16), grad, TN).astype(BF16)
    grad_probs = product(grad, values_in, NT)
    centred = grad_probs - jnp.sum(probs * grad_probs, axis=-1, keepdims=True)
    grad_scores = (probs * centred * SCALE).astype(BF16)
    grad_queries = product(grad_scores, keys_in).astype(BF16)
    grad_keys = product(grad_scores, queries, TN).astype(BF16)
    return grad_queries, grad_keys, grad_values


def attend_backward_kernel(heads, separate, query_ref, pair_ref, grad_ref, *outs):
    key_at = 0 if separate else heads
    query_out, pair_out = outs if separate else (outs[0], outs[0])
    for h in range(heads):
        own, key, value = (slice((h + n) * HDIM, (h + n + 1) * HDIM) for n in (0, key_at, key_at + heads))
        done = attend_backward_head(
            image_rows(query_ref, 0, own),
            image_rows(pair_ref, 0, key),
            image_rows(pair_ref, 0, value),
            image_rows(grad_ref, 0, own),
        )
        put_image(query_out, 0, own, done[0])
        put_image(pair_out, 0, key, done[1])
        put_image(pair_out, 0, value, done[2])


def image_blocks(*arrays):
    return [
        pl.BlockSpec((a.shape[0], 1) + tuple(a.shape[2:]), lambda i: (0, i, 0, 0)) for a in arrays
    ]


def attend_forward(heads, queries, pairs):
    separate = queries is not pairs
    out = jax.ShapeDtypeStruct(queries.shape[:3] + (heads * HDIM,), BF16)
    return pl.pallas_call(
        functools.partial(attend_forward_kernel, heads, separate),
        grid=(queries.shape[1],),
        out_shape=out,
        in_specs=image_blocks(queries, pairs),
        out_specs=image_blocks(out)[0],
        compiler_params=pltpu.CompilerParams(vmem_limit_bytes=VMEM_BYTES),
    )(queries, pairs)


def attend_backward(heads, queries, pairs, grad):
    separate = queries is not pairs
    outs = [jax.ShapeDtypeStruct(queries.shape, BF16)]
    if separate:
        outs.append(jax.ShapeDtypeStruct(pairs.shape, BF16))
    result = pl.pallas_call(
        functools.partial(attend_backward_kernel, heads, separate),
        grid=(queries.shape[1],),
        out_shape=outs,
        in_specs=image_blocks(queries, pairs, grad),
        out_specs=image_blocks(*outs),
        compiler_params=pltpu.CompilerParams(vmem_limit_bytes=VMEM_BYTES),
    )(queries, pairs, grad)
    return result if separate else result[0]


class ImageSum:
    def __init__(self, square, part, first_in, second_out, second_in, send_sem, recv_sem):
        self.square, self.part = square, part
        self.first_in, self.second_out, self.second_in = first_in, second_out, second_in
        self.send_sem, self.recv_sem = send_sem, recv_sem
        self.half = part.shape[2] // 2
        self.summing, self.spreading = [], []

    def copy_to(self, kept, source, target, slot, peer):
        copy = remote(
            source, target, self.send_sem.at[slot], self.recv_sem.at[slot], {"mp": peer}
        )
        copy.start()
        kept.append(copy)

    def columns(self, side):
        return pl.ds(side * self.half, self.half)

    def start(self):
        square = self.square
        for order in range(2):
            for side in range(2):
                owner = square.peers[side] if order else square.corner
                self.copy_to(
                    self.summing,
                    self.part.at[owner, :, self.columns(side)],
                    self.first_in.at[side, order],
                    side * 2 + order,
                    square.peers[side],
                )

    def forward(self):
        square = self.square
        for side in range(2):
            self.summing[side].wait_recv()
            own = self.part[square.peers[1 - side], :, self.columns(side)]
            self.second_out[side] = (
                own.astype(F32) + self.first_in[side, 0].astype(F32)
            ).astype(BF16)
            self.copy_to(
                self.summing, self.second_out.at[side], self.second_in.at[side], 4 + side,
                square.peers[1 - side],
            )

    def arrived(self):
        for copy in self.summing[2:]:
            copy.wait_recv()

    def total(self, at):
        return jnp.concatenate(
            [
                self.part[self.square.spot, at, self.columns(side)].astype(F32)
                + self.first_in[side, 1, at, :].astype(F32)
                + self.second_in[side, at, :].astype(F32)
                for side in range(2)
            ],
            axis=1,
        )

    def sent(self):
        for copy in self.summing:
            copy.wait_send()

    def spread(self, full, owner, side, slot, peer):
        where = full.at[owner, :, self.columns(side)]
        self.copy_to(self.spreading, where, where, slot, peer)

    def gather(self, full):
        square = self.square
        for slot, side, peer in ((6, 0, 1), (7, 1, 0), (8, 0, 0), (9, 1, 1)):
            self.spread(full, square.spot, side, slot, square.peers[peer])

    def pass_on(self, full):
        square = self.square
        self.spreading[0].wait_recv()
        self.spread(full, square.above, 0, 10, square.beside)
        self.spreading[1].wait_recv()
        self.spread(full, square.beside, 1, 11, square.above)

    def gathered(self):
        for copy in self.spreading[2:]:
            copy.wait_recv()

    def spread_sent(self):
        for copy in self.spreading:
            copy.wait_send()

    @staticmethod
    def scratch(stages, images, block, width):
        dma = pltpu.SemaphoreType.DMA
        lead = (stages, images)
        return [
            pltpu.VMEM((images, 4, block, width), BF16),
            pltpu.VMEM(lead + (2, 2, block, width // 2), BF16),
            pltpu.VMEM(lead + (2, block, width // 2), BF16),
            pltpu.VMEM(lead + (2, block, width // 2), BF16),
            dma(lead + (12,)),
            dma(lead + (12,)),
        ]


def forward_kernel(*refs):
    gains_ref, refs = refs[0], refs[1:]
    given, refs = refs[:9], refs[9:]
    self_mixed, second_normed, queries_ref, cross_mixed, third_normed, active, grad_hidden = refs[:7]
    own_self, own_cross = refs[7:9]
    loads = Loader(given[:8], refs[9:17], refs[17])
    shrink_ref = given[8]
    tiles, tile_sem = refs[18:20]
    part, first_in, second_out, second_in, send_sem, recv_sem = refs[20:]
    images = own_self.shape[0]
    heads = self_mixed.shape[3] // HDIM
    for i in range(8):
        loads.start(i)
    square = Square()
    wide = 256

    def shrink_load(j):
        slot = lax.rem(j, 2)
        return pltpu.make_async_copy(
            shrink_ref.at[tile_at(j, wide), :], tiles.at[slot], tile_sem.at[slot]
        )

    shrink_load(0).start()
    greet(square.targets)
    jobs = [
        [
            ImageSum(
                square, part.at[i], first_in.at[t, i], second_out.at[t, i], second_in.at[t, i],
                send_sem.at[t, i], recv_sem.at[t, i],
            )
            for i in range(images)
        ]
        for t in range(2)
    ]

    def project(i, left, weight):
        def one(j, carry):
            at = tile_at(j, wide)
            done = product(left, weight[:, at]).astype(BF16)
            part[i, :, :, at] = done.reshape(part.shape[1], part.shape[2], wide)
            return carry

        lax.fori_loop(0, part.shape[3] // wide, one, 0)

    def self_stage(i):
        projected = loads.got(0)

        def one(h, carry):
            own, key, value = (tile_at(h + n * heads, HDIM) for n in range(3))
            done = attend(
                image_rows(projected, i, own),
                image_rows(projected, i, key),
                image_rows(projected, i, value),
            )
            put_image(self_mixed, i, own, done)
            return carry

        lax.fori_loop(0, heads, one, 0)
        project(i, image_rows(self_mixed, i), loads.got(1))
        jobs[0][i].start()

    def norm_stage(t, i, rows_ref, out_ref, full_ref):
        job = jobs[t][i]
        job.arrived()
        gain = gains_ref[t + 1 : t + 2, :]
        for start in range(0, out_ref.shape[1], 32):
            at = slice(start, start + 32)
            wide_rows, narrow, _ = post_forward(job.total(at), (rows_ref[i, at, :],), gain)
            out_ref[i, at, :] = wide_rows
            full_ref[square.spot, i, at, :] = narrow
        job.gather(full_ref.at[:, i])

    def cross_stage(i):
        jobs[0][i].gathered()
        jobs[0][i].sent()
        text = loads.got(4)
        queries_ref[:, i] = (
            product(image_rows(second_normed, i), loads.got(3)[...])
            .astype(BF16)
            .reshape(queries_ref.shape[0], queries_ref.shape[2], queries_ref.shape[3])
        )

        def one(h, carry):
            own, value = (tile_at(h + n * heads, HDIM) for n in range(2))
            done = attend(image_rows(queries_ref, i, own), text[i, :, own], text[i, :, value])
            put_image(cross_mixed, i, own, done)
            return carry

        lax.fori_loop(0, heads, one, 0)
        project(i, image_rows(cross_mixed, i), loads.got(5))
        jobs[1][i].start()

    def shrink_back(first, last):
        feed_grad = loads.got(6)
        count = shrink_ref.shape[0] // wide

        def one(j, carry):
            shrink_load(j).wait()

            @pl.when(j + 1 < count)
            def _():
                shrink_load(j + 1).start()

            for i in range(images):
                done = product(image_rows(feed_grad, i), tiles[lax.rem(j, 2)], NT)
                put_image(grad_hidden, i, tile_at(j, wide), done.astype(BF16))
            return carry

        lax.fori_loop(first, last, one, 0)

    def feed_stage(i):
        jobs[1][i].gathered()
        expand = loads.got(7)

        def one(j, carry):
            at = tile_at(j, wide)
            hidden = product(image_rows(third_normed, i), expand[:, at])
            spread = 0.5 + 0.5 * lax.erf(hidden * math.sqrt(0.5))
            slope = spread + hidden * jnp.exp(-0.5 * hidden * hidden) * (1.0 / math.sqrt(2.0 * math.pi))
            put_image(active, i, at, (hidden * spread).astype(BF16))
            grad = image_rows(grad_hidden, i, at).astype(F32) * slope
            put_image(grad_hidden, i, at, grad.astype(BF16))
            return carry

        lax.fori_loop(0, expand.shape[1] // wide, one, 0)

    count = shrink_ref.shape[0] // wide
    first, second = jobs
    self_stage(0)
    self_stage(1)
    first[0].forward()
    self_stage(2)
    first[1].forward()
    first[2].forward()
    shrink_back(0, count // 2)
    rows_ref = loads.got(2)
    for i in range(images):
        norm_stage(0, i, rows_ref, own_self, second_normed)
        if i:
            first[i - 1].pass_on(second_normed.at[:, i - 1])
    cross_stage(0)
    first[-1].pass_on(second_normed.at[:, images - 1])
    cross_stage(1)
    second[0].forward()
    cross_stage(2)
    second[1].forward()
    second[2].forward()
    shrink_back(count // 2, count)
    for i in range(images):
        norm_stage(1, i, own_self, own_cross, third_normed)
        if i:
            second[i - 1].pass_on(third_normed.at[:, i - 1])
    feed_stage(0)
    second[-1].pass_on(third_normed.at[:, images - 1])
    feed_stage(1)
    feed_stage(2)
    for job in first:
        job.spread_sent()
    for job in second:
        job.sent()
        job.spread_sent()


def forward_steps(gains, projected, attention_out, entry, cross_query, text, cross_out, feed_grad, expand, shrink, ident):
    quarters, images, block, _ = projected.shape
    width = attention_out.shape[1]
    ff = expand.shape[1]
    heads_wide = attention_out.shape[0]

    def rows(columns):
        return jax.ShapeDtypeStruct((quarters, images, block, columns), BF16)

    outs = [rows(heads_wide), rows(width), rows(heads_wide), rows(heads_wide), rows(width), rows(ff), rows(ff)]
    outs += [jax.ShapeDtypeStruct((images, block, width), F32)] * 2
    given = (projected, attention_out, entry, cross_query, text, cross_out, feed_grad, expand)
    vmem = pl.BlockSpec(memory_space=pltpu.VMEM)
    hbm = pl.BlockSpec(memory_space=pl.ANY)
    return pl.pallas_call(
        forward_kernel,
        out_shape=outs,
        in_specs=[vmem] + [hbm] * 9,
        out_specs=[vmem] * len(outs),
        scratch_shapes=[pltpu.VMEM(a.shape, a.dtype) for a in given]
        + [
            pltpu.SemaphoreType.DMA((len(given),)),
            pltpu.VMEM((2, 256, width), BF16),
            pltpu.SemaphoreType.DMA((2,)),
        ]
        + ImageSum.scratch(2, images, block, width),
        compiler_params=pltpu.CompilerParams(
            collective_id=ident, has_side_effects=True, vmem_limit_bytes=VMEM_BYTES
        ),
        cost_estimate=pl.CostEstimate(
            flops=60_000_000_000, bytes_accessed=80_000_000, transcendentals=0
        ),
    )(gains, *given, shrink)


def gelu_exact(values_in):
    return jax.nn.gelu(values_in, approximate=False)


def body(
    square,
    tokens,
    caption,
    masked,
    out_grad,
    mask_embed,
    norm_gains,
    attention_in,
    attention_out,
    cross_query,
    cross_text,
    cross_out,
    feed_expand,
    feed_shrink,
):
    step = square_step if square else plain_step
    axis_count = lax.axis_size("mp")
    axis_place = lax.axis_index("mp")
    images, length = masked.shape
    rows_all = images * length
    share_rows = rows_all // axis_count
    model_width = tokens.shape[1]
    text_width = caption.shape[1]
    heads_here = attention_in.shape[2] // HDIM

    quarters = axis_count if square else 1

    def own_rows(rows_in):
        return lax.dynamic_slice_in_dim(rows_in, axis_place * share_rows, share_rows, 0)

    def by_quarters(rows_in):
        parts = rows_in.reshape(images, quarters, length // quarters, -1)
        return parts.transpose(1, 0, 2, 3).reshape(rows_all, -1)

    def four(rows_in):
        return rows_in.reshape(quarters, images, -1, rows_in.shape[-1])

    def flat(parts):
        return parts.reshape(rows_all, parts.shape[-1])

    tokens, out_grad = by_quarters(tokens), by_quarters(out_grad)
    gains = [norm_gains[k : k + 1] for k in range(3)]
    mask_column = by_quarters(masked) > 0

    def enter(rows_in, mask):
        return jnp.where(mask, mask_embed.astype(F32)[None, :], rows_in.astype(F32))

    own_mask = own_rows(mask_column)
    own_float = own_mask.astype(F32)
    own_entry = enter(own_rows(tokens), own_mask)
    first_unit, _ = norm_parts(enter(tokens, mask_column))
    first_normed = (first_unit * gains[0]).astype(BF16)
    weight_in = attention_in.reshape(model_width, -1)
    projected = product(first_normed, weight_in).astype(BF16)
    weight_text = cross_text.reshape(text_width, -1)
    text_pairs = product(caption, weight_text).astype(BF16)
    text_four = text_pairs.reshape(1, images, -1, text_pairs.shape[1])
    feed_grad = jnp.where(mask_column, out_grad, jnp.zeros_like(out_grad))
    own_feed_grad = own_rows(feed_grad).astype(F32)
    ff = feed_expand.shape[1]
    if square:
        rows_out = forward_steps(
            norm_gains, four(projected), attention_out, own_entry.reshape(images, -1, model_width), cross_query,
            text_four[0], cross_out, four(feed_grad), feed_expand, feed_shrink, 1,
        )
        self_mixed, second_normed, cross_queries, cross_mixed, third_normed, active, grad_hidden = (
            flat(part) for part in rows_out[:7]
        )
        own_self, own_cross = (part.reshape(share_rows, model_width) for part in rows_out[7:])
    else:
        whole = four(projected)
        self_mixed = flat(attend_forward(heads_here, whole, whole))
        own_self, second_normed = step(
            self_mixed, attention_out, NN, post_forward, gains[1], (own_entry,), F32, 0, True, 1
        )
        cross_queries = product(second_normed, cross_query).astype(BF16)
        cross_mixed = flat(attend_forward(heads_here, four(cross_queries), text_four))
        own_cross, third_normed = step(
            cross_mixed, cross_out, NN, post_forward, gains[2], (own_self,), F32, 0, True, 2
        )
        hidden = product(third_normed, feed_expand)
        active = gelu_exact(hidden).astype(BF16)
        _, gelu_pull = jax.vjp(gelu_exact, hidden)
        grad_hidden = gelu_pull(product(feed_grad, feed_shrink, NT))[0].astype(BF16)
    wide = LineSum.width
    own_before_feed, cross_grad, third_gain, shrink_low = step(
        grad_hidden, feed_expand, NT, post_backward, gains[2], (own_feed_grad, own_cross), F32, 1, True, 3,
        ((feed_grad, active, 0, ff - wide, True),),
    )

    grad_cross_mixed = product(cross_grad, cross_out, NT).astype(BF16)
    grad_cross_queries, grad_text_pairs = attend_backward(
        heads_here, four(cross_queries), text_four, four(grad_cross_mixed)
    )
    grad_cross_queries = flat(grad_cross_queries)
    grad_text_pairs = grad_text_pairs.reshape(text_pairs.shape)
    own_before_cross, self_grad, second_gain, shrink_high, expand_low, mixed_part = step(
        grad_cross_queries, cross_query, NT, post_backward, gains[1], (own_before_feed, own_self), F32, 1, True, 4,
        ((feed_grad, active, ff - wide, ff, True), (third_normed, grad_hidden, 0, ff // 2, False)),
        (active, feed_shrink, NN),
    )

    self_grad, grad_text_pairs = lax.optimization_barrier((self_grad, grad_text_pairs))
    cross_text_sum = image_sum(rows_product(caption, grad_text_pairs))
    grad_self_mixed = product(self_grad, attention_out, NT).astype(BF16)
    four_projected = four(projected)
    grad_projected = flat(
        attend_backward(heads_here, four_projected, four_projected, four(grad_self_mixed))
    )
    tokens_rows, first_gain, embed_term, expand_high, caption_part = step(
        grad_projected, weight_in, NT, post_entry, gains[0],
        (own_before_cross, own_entry, own_float), F32, 2, False, 5,
        ((third_normed, grad_hidden, ff // 2, ff, False),), (grad_text_pairs, weight_text, NT),
    )
    terms = [first_gain, second_gain, third_gain, embed_term]
    if square:
        own_mixed = own_rows(mixed_part).astype(F32) + own_cross
        mixed_part = lax.dynamic_update_slice_in_dim(
            mixed_part, own_mixed.astype(BF16), axis_place * share_rows, 0
        )
        (
            self_in_sum, self_out_sum, cross_query_sum, cross_out_sum,
            small_totals, mixed_out, caption_grad, tokens_grad,
        ) = line_sums(
            [first_normed, self_grad, second_normed, cross_grad],
            [grad_projected, self_mixed, grad_cross_queries, cross_mixed],
            ((0, 4, 0), (0, 4, 512), (0, 4, 1024), (1, 5, 0), (2, 6, 0), (3, 7, 0)),
            jnp.concatenate(terms + [jnp.zeros_like(embed_term)] * 4, axis=0),
            mixed_part,
            caption_part,
            tokens_rows.reshape(images, -1, model_width),
            6,
        )
        slice_width = model_width // (lax.axis_size("img") * axis_count)
        slice_at = (lax.axis_index("img") * axis_count + axis_place) * slice_width
        small_sums = lax.dynamic_slice_in_dim(small_totals, slice_at, slice_width, 1)
    else:
        tokens_grad = tokens_rows
        mixed_sum = lax.psum_scatter(mixed_part, "mp", scatter_dimension=0, tiled=True)
        mixed_out = (own_cross + mixed_sum.astype(F32)).astype(BF16)
        caption_grad = lax.psum_scatter(
            caption_part, "mp", scatter_dimension=1, tiled=True
        ).astype(F32)
        small_sums = lax.psum_scatter(
            jnp.concatenate(terms, axis=0), ("img", "mp"), scatter_dimension=1, tiled=True
        )
        self_in_sum = image_sum(rows_product(first_normed, grad_projected))
        self_out_sum = image_sum(rows_product(self_mixed, self_grad), 1)
        cross_query_sum = image_sum(rows_product(second_normed, grad_cross_queries))
        cross_out_sum = image_sum(rows_product(cross_mixed, cross_grad), 1)
    return (
        mixed_out,
        tokens_grad,
        caption_grad,
        small_sums[3],
        small_sums[0:3],
        self_in_sum.reshape(-1, 3, attention_in.shape[2]),
        self_out_sum,
        cross_query_sum,
        cross_text_sum.reshape(-1, 2, cross_text.shape[2]),
        cross_out_sum,
        jnp.concatenate([expand_low, expand_high], axis=1),
        jnp.concatenate([shrink_low, shrink_high], axis=0),
    )


def solution(mesh):
    square = mesh.shape["mp"] == 4 and mesh.shape["img"] == 8
    return jax.shard_map(
        functools.partial(body, square),
        mesh=mesh,
        in_specs=(
            P("img", None),
            P("img", None),
            P("img", None),
            P("img", None),
            P(),
            P(),
            P(None, None, "mp"),
            P("mp", None),
            P(None, "mp"),
            P(None, None, "mp"),
            P("mp", None),
            P(None, "mp"),
            P("mp", None),
        ),
        out_specs=(
            P(("img", "mp"), None),
            P(("img", "mp"), None),
            P("img", "mp"),
            P(("img", "mp")),
            P(None, ("img", "mp")),
            P("img", None, "mp"),
            P("mp", "img"),
            P("img", "mp"),
            P("img", None, "mp"),
            P("mp", "img"),
            P("img", "mp"),
            P("mp", "img"),
        ),
        check_vma=False,
    )
```

```python
import dataclasses
import functools
import math
import types
from typing import Any

import jax
import jax.numpy as jnp
from jax import lax
from jax.experimental import pallas as pl
from jax.experimental.pallas import tpu as pltpu
from jax.sharding import PartitionSpec as P

HDIM = 128
EPSILON = 1e-05
SCALE = 1.0 / math.sqrt(HDIM)
VMEM_BYTES = 61 * 1024 * 1024
MESH = pl.DeviceIdType.MESH
BF16 = jnp.bfloat16
F32 = jnp.float32
WIDE = 512
TILE = 256

NN = (((1,), (0,)), ((), ()))
NT = (((1,), (1,)), ((), ()))
TN = (((0,), (0,)), ((), ()))


def product(left, right, dims=NN):
    return lax.dot_general(left, right, dims, preferred_element_type=F32)


def image_sum(part, dimension=0):
    return lax.psum_scatter(part, "img", scatter_dimension=dimension, tiled=True).astype(F32)


def rows_product(left, right):
    return product(left, right, TN).astype(BF16)


def norm_parts(rows_in):
    centre = rows_in - jnp.mean(rows_in, axis=-1, keepdims=True)
    root_inverse = lax.rsqrt(jnp.mean(centre * centre, axis=-1, keepdims=True) + EPSILON)
    return (centre * root_inverse, root_inverse)


def norm_back(grad_rows, unit_rows, root_inverse, gain_row):
    weighted = grad_rows * gain_row
    middle = jnp.mean(weighted, axis=-1, keepdims=True)
    along = jnp.mean(weighted * unit_rows, axis=-1, keepdims=True)
    return root_inverse * (weighted - middle - unit_rows * along)


def post_forward(total, rows_in, gain):
    fresh = rows_in[0] + total
    unit, _ = norm_parts(fresh)
    return fresh, (unit * gain).astype(BF16), ()


def post_backward(total, rows_in, gain):
    before, source = rows_in
    unit, root = norm_parts(source)
    grad = before + norm_back(total, unit, root, gain)
    return grad, grad.astype(BF16), (jnp.sum(total * unit, axis=0, keepdims=True),)


def post_entry(total, rows_in, gain):
    before, source, mask = rows_in
    unit, root = norm_parts(source)
    grad = before + norm_back(total, unit, root, gain)
    sums = (
        jnp.sum(total * unit, axis=0, keepdims=True),
        jnp.sum(grad * mask, axis=0, keepdims=True),
    )
    return grad * (1.0 - mask), None, sums


def remote(source, target, send, recv, device):
    return pltpu.make_async_remote_copy(
        src_ref=source,
        dst_ref=target,
        send_sem=send,
        recv_sem=recv,
        device_id=device,
        device_id_type=MESH,
    )


def greet(targets):
    barrier = pltpu.get_barrier_semaphore()
    for target in targets:
        pl.semaphore_signal(barrier, inc=1, device_id=target, device_id_type=MESH)
    pl.semaphore_wait(barrier, len(targets))


def tile_at(j, wide=TILE):
    return pl.ds(pl.multiple_of(j * wide, wide), wide)


def all_rows(ref, columns=slice(None)):
    part = ref[:, :, :, columns]
    return part.reshape(-1, part.shape[3])


def image_rows(ref, i, columns=slice(None)):
    part = ref[i, :, :, columns]
    return part.reshape(-1, part.shape[2])


def put_image(ref, i, columns, value):
    ref[i, :, :, columns] = value.reshape(ref.shape[1], ref.shape[2], value.shape[1])


class Loads:
    def __init__(self, names, sources, targets, sem):
        self.targets = dict(zip(names, targets))
        self.copies = {
            name: pltpu.make_async_copy(source, target, sem.at[i])
            for i, (name, source, target) in enumerate(zip(names, sources, targets))
        }
        self.waiting = set()

    def start(self, *names):
        for name in names:
            self.copies[name].start()
            self.waiting.add(name)

    def got(self, name):
        if name in self.waiting:
            self.waiting.remove(name)
            self.copies[name].wait()
        return self.targets[name]


class Stream:
    def __init__(self, source, tiles, sem, columns=False, passes=1):
        self.source, self.tiles, self.sem, self.columns = source, tiles, sem, columns
        self.count = source.shape[1 if columns else 0] // TILE
        self.total = passes * self.count

    def copy(self, j):
        slot, at = lax.rem(j, 2), tile_at(lax.rem(j, self.count))
        part = self.source.at[:, at] if self.columns else self.source.at[at, :]
        return pltpu.make_async_copy(part, self.tiles.at[slot], self.sem.at[slot])

    def start(self):
        self.copy(0).start()

    def run(self, first, last, use):
        def one(j, carry):
            self.copy(j).wait()

            @pl.when(j + 1 < self.total)
            def _():
                self.copy(j + 1).start()

            use(j, self.tiles[lax.rem(j, 2)])
            return carry

        lax.fori_loop(first, last, one, 0)

    @staticmethod
    def scratch(source, columns=False):
        shape = (source.shape[0], TILE) if columns else (TILE, source.shape[1])
        return pltpu.VMEM((2,) + shape, source.dtype), pltpu.SemaphoreType.DMA((2,))


class Saves:
    def __init__(self, names, sources, targets, sem):
        self.refs = {n: pair for n, pair in zip(names, zip(sources, targets))}
        self.sem, self.running, self.names = sem, [], names

    def save(self, name, i=None):
        source, target = self.refs[name]
        if i is not None:
            source, target = source.at[i], target.at[i]
        copy = pltpu.make_async_copy(source, target, self.sem.at[self.names.index(name), i or 0])
        copy.start()
        self.running.append(copy)

    def finish(self):
        for copy in self.running:
            copy.wait()


def launch(kernel, ident, vmem=(), loaded=(), hbm=(), outs=(), saved=(), hbm_outs=(), scratch=()):
    vmem, loaded, hbm, outs = dict(vmem), dict(loaded), dict(hbm), dict(outs)
    saved, hbm_outs, scratch = dict(saved), dict(hbm_outs), dict(scratch)
    names = [*vmem, *loaded, *hbm, *outs, *saved, *hbm_outs]
    buffers = [pltpu.VMEM(a.shape, a.dtype) for a in [*loaded.values(), *saved.values()]]

    def run(*refs):
        r = types.SimpleNamespace(**dict(zip(names, refs)))
        rest = refs[len(names) :]
        rest, buffer_refs = rest[: len(scratch)], rest[len(scratch) : len(scratch) + len(buffers)]
        for name, ref in zip(scratch, rest):
            setattr(r, name, ref)
        r.loads = Loads(list(loaded), [getattr(r, n) for n in loaded], buffer_refs[: len(loaded)], refs[-2])
        kept = buffer_refs[len(loaded) :]
        r.saves = Saves(list(saved), kept, [getattr(r, n) for n in saved], refs[-1])
        for name, ref in zip(saved, kept):
            setattr(r, name, ref)
        kernel(r)
        r.saves.finish()

    in_vmem = pl.BlockSpec(memory_space=pltpu.VMEM)
    in_hbm = pl.BlockSpec(memory_space=pl.ANY)
    result = pl.pallas_call(
        run,
        out_shape=[*outs.values(), *saved.values(), *hbm_outs.values()],
        in_specs=[in_vmem] * len(vmem) + [in_hbm] * (len(loaded) + len(hbm)),
        out_specs=[in_vmem] * len(outs) + [in_hbm] * (len(saved) + len(hbm_outs)),
        scratch_shapes=[
            *scratch.values(),
            *buffers,
            pltpu.SemaphoreType.DMA((max(len(loaded), 1),)),
            pltpu.SemaphoreType.DMA((max(len(saved), 1), 3)),
        ],
        compiler_params=pltpu.CompilerParams(
            collective_id=ident, has_side_effects=True, vmem_limit_bytes=VMEM_BYTES
        ),
        cost_estimate=pl.CostEstimate(
            flops=60_000_000_000, bytes_accessed=80_000_000, transcendentals=0
        ),
    )(*vmem.values(), *loaded.values(), *hbm.values())
    return types.SimpleNamespace(**dict(zip([*outs, *saved, *hbm_outs], result)))


def struct(shape, kind):
    return jax.ShapeDtypeStruct(tuple(shape), kind)


class Square:
    def __init__(self):
        self.spot = lax.axis_index("mp")
        up, across = lax.div(self.spot, 2), lax.rem(self.spot, 2)
        self.beside = up * 2 + (1 - across)
        self.above = (1 - up) * 2 + across
        self.corner = (1 - up) * 2 + (1 - across)
        self.peers = (self.beside, self.above)
        self.targets = [{"mp": self.beside}, {"mp": self.above}]


class LineSum:
    def __init__(self, r, lefts, pieces):
        self.r, self.lefts, self.pieces = r, lefts, pieces
        self.count, self.ticked = len(pieces), 0
        self.share = r.line_own.shape[2]
        self.place = lax.axis_index("img")
        self.line, self.core = lax.div(self.place, 2), lax.rem(self.place, 2)
        self.twin = self.line * 2 + (1 - self.core)
        self.others = [lax.rem(self.line + j, 4) * 2 + self.core for j in (1, 2, 3)]
        self.targets = [{"img": self.twin}] + [{"img": o} for o in self.others]

    @staticmethod
    def scratch(count, lefts, left):
        dma = pltpu.SemaphoreType.DMA
        share = left.shape[3] // 8
        return dict(
            line_left=pltpu.VMEM((lefts, 2) + tuple(left.shape[:3]) + (2 * share,), BF16),
            line_left_sem=dma((lefts, 2)),
            core_out=pltpu.VMEM((count, 2, share, WIDE), BF16),
            core_in=pltpu.VMEM((count, 2, share, WIDE), BF16),
            line_own=pltpu.VMEM((count, 4, share, WIDE), BF16),
            line_in=pltpu.VMEM((count, 5, share, WIDE), BF16),
            core_send=dma((count, 2)),
            core_recv=dma((count, 2)),
            line_send=dma((count, 2, 3)),
            line_recv=dma((count, 2, 3)),
        )

    def left_copy(self, n, k):
        slot = k % 2
        at = tile_at(self.chunk_at(k), 2 * self.share)
        return pltpu.make_async_copy(
            self.lefts[n].at[:, :, :, at], self.r.line_left.at[n, slot], self.r.line_left_sem.at[n, slot]
        )

    def begin(self):
        for n in range(len(self.lefts)):
            self.left_copy(n, 0).start()

    def core_copy(self, g, k):
        r, slot = self.r, k % 2
        return remote(
            r.core_out.at[g, slot], r.core_in.at[g, slot], r.core_send.at[g, slot],
            r.core_recv.at[g, slot], {"img": self.twin},
        )

    def slot_at(self, way, s, line):
        first = (line < 2) if way == 0 else (line >= 2)
        return jnp.where(first, s, s + 2)

    def line_copy(self, g, way, s, chunk):
        r, ahead = self.r, 1 if way == 0 else -1
        return remote(
            r.line_own.at[g, chunk],
            r.line_in.at[g, self.slot_at(way, s, self.line + ahead)],
            r.line_send.at[g, way, s],
            r.line_recv.at[g, way, s],
            {"img": self.place + 2 * ahead},
        )

    def chunk_at(self, k):
        if k == 3:
            return self.line
        low = 3 - k - jnp.where(self.line + k == 3, 1, 0)
        high = k + jnp.where(self.line == k, 1, 0)
        return jnp.where(self.line < 2, low, high)

    def distance(self, way):
        return self.line if way == 0 else 3 - self.line

    def multiply(self, g, k):
        r = self.r
        left, name, column = self.pieces[g]
        right = r.loads.got(name) if name in r.loads.targets else getattr(r, name)
        right = all_rows(right, slice(column, column + WIDE))
        chunk = self.chunk_at(k)

        if k >= 2:
            self.core_copy(g, k).wait_send()
        for mine in (False, True):
            part = self.core if mine else 1 - self.core
            block = r.line_left[left, k % 2, :, :, :, tile_at(part, self.share)]
            done = product(block.reshape(-1, self.share), right, TN).astype(BF16)
            if mine:
                r.line_own[g, chunk] = done
            else:
                r.core_out[g, k % 2] = done
                self.core_copy(g, k).start()

    def add(self, g, chunk, arrived):
        own = self.r.line_own
        own[g, chunk] = (own[g, chunk].astype(F32) + arrived.astype(F32)).astype(BF16)

    def take(self, g, way, s, chunk):
        self.line_copy(g, way, s, chunk).wait_recv()
        self.add(g, chunk, self.r.line_in[g, self.slot_at(way, s, self.line)])

    def send_on(self, g, k):
        self.core_copy(g, k).wait_recv()
        self.add(g, self.chunk_at(k), self.r.core_in[g, k % 2])
        for way in range(2) if k < 3 else ():
            gone = self.distance(way)
            to = 3 - k + self.line if way == 0 else k - 3 + self.line

            @pl.when(gone <= k)
            def _():
                if k >= 1:

                    @pl.when(gone >= 1)
                    def _():
                        self.take(g, way, k - 1, to)

                self.line_copy(g, way, k, to).start()

    def tick(self, count=None):
        everything = 4 * (self.count + 1)
        for at in range(self.ticked, everything if count is None else min(self.ticked + count, everything)):
            k, g = divmod(at, self.count + 1)
            if g == 0:
                for n in range(len(self.lefts)):
                    self.left_copy(n, k).wait()
                    if k < 3:
                        self.left_copy(n, k + 1).start()
            if g < self.count:
                self.multiply(g, k)
            if g > 0:
                self.send_on(g - 1, k)
            self.ticked = at + 1

    def collect(self, g):
        for way in range(2):

            @pl.when(self.distance(way) >= 1)
            def _():
                self.take(g, way, 2, self.line)

        return self.r.line_own[g, self.line]

    def settle(self):
        for g in range(self.count):
            for k in (2, 3):
                self.core_copy(g, k).wait_send()

        def one(k, carry):
            for g in range(self.count):
                for way in range(2):

                    @pl.when(self.distance(way) <= k)
                    def _():
                        self.line_copy(g, way, k, self.line).wait_send()

            return carry

        lax.fori_loop(0, 3, one, 0)


class ImageSum:
    def __init__(self, square, part, first_in, second_out, second_in, send_sem, recv_sem):
        self.square, self.part = square, part
        self.first_in, self.second_out, self.second_in = first_in, second_out, second_in
        self.send_sem, self.recv_sem = send_sem, recv_sem
        self.half = part.shape[2] // 2
        self.summing, self.spreading, self.firsts = [], [], ([], [])

    def copy_to(self, kept, source, target, slot, peer):
        copy = remote(
            source, target, self.send_sem.at[slot], self.recv_sem.at[slot], {"mp": peer}
        )
        copy.start()
        kept.append(copy)

    def columns(self, side):
        return pl.ds(side * self.half, self.half)

    def start(self):
        square = self.square
        for order in range(2):
            for side in range(2):
                owner = square.peers[side] if order else square.corner
                self.copy_to(
                    self.summing,
                    self.part.at[owner, :, self.columns(side)],
                    self.first_in.at[side, order],
                    side * 2 + order,
                    square.peers[side],
                )

    def start_side(self, side):
        square = self.square
        for order in range(2):
            owner = square.peers[side] if order else square.corner
            self.copy_to(
                self.firsts[side],
                self.part.at[owner, :, self.columns(side)],
                self.first_in.at[side, order],
                side * 2 + order,
                square.peers[side],
            )
        if side == 1:
            self.summing = [self.firsts[0][0], self.firsts[1][0], self.firsts[0][1], self.firsts[1][1]]

    def forward(self):
        square = self.square
        for side in range(2):
            self.summing[side].wait_recv()
            own = self.part[square.peers[1 - side], :, self.columns(side)]
            self.second_out[side] = (
                own.astype(F32) + self.first_in[side, 0].astype(F32)
            ).astype(BF16)
            self.copy_to(
                self.summing, self.second_out.at[side], self.second_in.at[side], 4 + side,
                square.peers[1 - side],
            )

    def arrived(self):
        for copy in self.summing[2:]:
            copy.wait_recv()

    def total(self, at):
        return jnp.concatenate(
            [
                self.part[self.square.spot, at, self.columns(side)].astype(F32)
                + self.first_in[side, 1, at, :].astype(F32)
                + self.second_in[side, at, :].astype(F32)
                for side in range(2)
            ],
            axis=1,
        )

    def sent(self):
        for copy in self.summing:
            copy.wait_send()

    def spread(self, full, owner, side, slot, peer):
        where = full.at[owner, :, self.columns(side)]
        self.copy_to(self.spreading, where, where, slot, peer)

    def gather(self, full):
        square = self.square
        for slot, side, peer in ((6, 0, 1), (7, 1, 0), (8, 0, 0), (9, 1, 1)):
            self.spread(full, square.spot, side, slot, square.peers[peer])

    def pass_on(self, full):
        square = self.square
        self.spreading[0].wait_recv()
        self.spread(full, square.above, 0, 10, square.beside)
        self.spreading[1].wait_recv()
        self.spread(full, square.beside, 1, 11, square.above)

    def gathered(self):
        for copy in self.spreading[2:]:
            copy.wait_recv()

    def spread_sent(self):
        for copy in self.spreading:
            copy.wait_send()

    @staticmethod
    def scratch(stages, like, width):
        images, _, block = like.shape[:3]
        dma = pltpu.SemaphoreType.DMA
        lead = (stages, images)
        return dict(
            part=pltpu.VMEM((images, 4, block, width), BF16),
            first_in=pltpu.VMEM(lead + (2, 2, block, width // 2), BF16),
            second_out=pltpu.VMEM(lead + (2, block, width // 2), BF16),
            second_in=pltpu.VMEM(lead + (2, block, width // 2), BF16),
            sum_send=dma(lead + (12,)),
            sum_recv=dma(lead + (12,)),
        )

    @staticmethod
    def stage(r, square, t):
        return [
            ImageSum(
                square, r.part.at[i], r.first_in.at[t, i], r.second_out.at[t, i], r.second_in.at[t, i],
                r.sum_send.at[t, i], r.sum_recv.at[t, i],
            )
            for i in range(r.part.shape[0])
        ]


def project(r, i, left, weight, dims=NN):
    def one(j, carry):
        at = tile_at(j)
        done = product(left, weight[at, :] if dims == NT else weight[:, at], dims)
        put_image(r.part, i, at, done.astype(BF16))
        return carry

    lax.fori_loop(0, r.part.shape[3] // TILE, one, 0)


def softmax_rows(queries, keys_in):
    scores = product(queries, keys_in, NT) * SCALE
    powers = jnp.exp(scores - jnp.max(scores, axis=-1, keepdims=True))
    return powers * (1.0 / jnp.sum(powers, axis=-1, keepdims=True))


def attend(queries, keys_in, values_in):
    probs = softmax_rows(queries, keys_in).astype(BF16)
    return product(probs, values_in).astype(BF16)


def attend_backward_head(queries, keys_in, values_in, grad):
    probs = softmax_rows(queries, keys_in)
    grad_values = product(probs.astype(BF16), grad, TN).astype(BF16)
    grad_probs = product(grad, values_in, NT)
    centred = grad_probs - jnp.sum(probs * grad_probs, axis=-1, keepdims=True)
    grad_scores = (probs * centred * SCALE).astype(BF16)
    grad_queries = product(grad_scores, keys_in).astype(BF16)
    grad_keys = product(grad_scores, queries, TN).astype(BF16)
    return grad_queries, grad_keys, grad_values


def backward_heads(heads, read, write):
    def one(h, carry):
        done = attend_backward_head(*(read(n, h) for n in range(4)))
        for n in range(3):
            write(n, h, done[n])
        return carry

    lax.fori_loop(0, heads, one, 0)


def forward_kernel(r):
    loads = r.loads
    images, heads = r.own_self.shape[0], r.self_mixed.shape[3] // HDIM
    loads.start("projected", "attention_out", "entry", "cross_query", "text", "cross_out", "feed_grad", "feed_expand")
    stream = Stream(r.feed_shrink, r.tiles, r.tile_sem)
    stream.start()
    square = Square()
    place = lax.axis_index("img")
    peers = [lax.rem(place + j, 8) for j in range(1, 8)]
    greet(square.targets + [{"img": peer} for peer in peers])
    jobs = [ImageSum.stage(r, square, t) for t in range(2)]

    def caption_columns(owner):
        return r.caption.at[:, tile_at(owner, WIDE)]

    moves = [
        remote(
            caption_columns(peer), r.captions.at[place], r.move_send.at[j], r.move_recv.at[j], {"img": peer}
        )
        for j, peer in enumerate(peers)
    ]
    stay = pltpu.make_async_copy(caption_columns(place), r.captions.at[place], r.stay_sem.at[0])

    def self_stage(i):
        projected = loads.got("projected")

        def one(h, carry):
            parts = [image_rows(projected, i, tile_at(h + n * heads, HDIM)) for n in range(3)]
            put_image(r.self_mixed, i, tile_at(h, HDIM), attend(*parts))
            return carry

        lax.fori_loop(0, heads, one, 0)
        project(r, i, image_rows(r.self_mixed, i), loads.got("attention_out"))
        jobs[0][i].start()
        r.saves.save("self_mixed", i)

    def norm_stage(t, i, rows_ref, out_ref, full_ref):
        job = jobs[t][i]
        job.arrived()
        gain = r.gains[t + 1 : t + 2, :]
        for start in range(0, out_ref.shape[1], 32):
            at = slice(start, start + 32)
            wide_rows, narrow, _ = post_forward(job.total(at), (rows_ref[i, at, :],), gain)
            out_ref[i, at, :] = wide_rows
            full_ref[i, square.spot, at, :] = narrow

    def gather_stage(t, full_ref):
        for i in range(images):
            if t == 0:
                norm_stage(0, i, loads.got("entry"), r.own_self, full_ref)
            else:
                norm_stage(1, i, r.own_self, r.own_cross, full_ref)
            if i:
                jobs[t][i - 1].pass_on(full_ref.at[i - 1])
            jobs[t][i].gather(full_ref.at[i])

    def cross_stage(i):
        jobs[0][i].gathered()
        jobs[0][i].sent()
        r.saves.save("second_normed", i)
        r.saves.save("own_self", i)
        text = loads.got("text")
        queries = product(image_rows(r.second_normed, i), loads.got("cross_query")[...]).astype(BF16)
        put_image(r.queries, i, slice(None), queries)

        def one(h, carry):
            own, value = (tile_at(h + n * heads, HDIM) for n in range(2))
            done = attend(image_rows(r.queries, i, own), text[i, :, own], text[i, :, value])
            put_image(r.cross_mixed, i, own, done)
            return carry

        lax.fori_loop(0, heads, one, 0)
        project(r, i, image_rows(r.cross_mixed, i), loads.got("cross_out"))
        jobs[1][i].start()
        r.saves.save("queries", i)
        r.saves.save("cross_mixed", i)

    def shrink_back(j, weight):
        feed_grad = loads.got("feed_grad")
        for i in range(images):
            done = product(image_rows(feed_grad, i), weight, NT)
            put_image(r.grad_hidden, i, tile_at(j), done.astype(BF16))

    def feed_stage(i):
        jobs[1][i].gathered()
        r.saves.save("third_normed", i)
        r.saves.save("own_cross", i)
        expand = loads.got("feed_expand")

        def one(j, carry):
            at = tile_at(j)
            hidden = product(image_rows(r.third_normed, i), expand[:, at])
            spread = 0.5 + 0.5 * lax.erf(hidden * math.sqrt(0.5))
            slope = spread + hidden * jnp.exp(-0.5 * hidden * hidden) * (1.0 / math.sqrt(2.0 * math.pi))
            put_image(r.active, i, at, (hidden * spread).astype(BF16))
            grad = image_rows(r.grad_hidden, i, at).astype(F32) * slope
            put_image(r.grad_hidden, i, at, grad.astype(BF16))
            return carry

        lax.fori_loop(0, expand.shape[1] // TILE, one, 0)
        r.saves.save("active", i)
        r.saves.save("grad_hidden", i)

    first, second = jobs
    self_stage(0)
    stay.start()
    for copy in moves:
        copy.start()
    self_stage(1)
    first[0].forward()
    self_stage(2)
    first[1].forward()
    first[2].forward()
    loads.got("feed_grad")
    stream.run(0, stream.count // 2, shrink_back)
    gather_stage(0, r.second_normed)
    cross_stage(0)
    first[2].pass_on(r.second_normed.at[2])
    cross_stage(1)
    second[0].forward()
    cross_stage(2)
    second[1].forward()
    second[2].forward()
    stream.run(stream.count // 2, stream.count, shrink_back)
    gather_stage(1, r.third_normed)
    feed_stage(0)
    second[2].pass_on(r.third_normed.at[2])
    feed_stage(1)
    feed_stage(2)
    for job in first:
        job.spread_sent()
    for job in second:
        job.sent()
        job.spread_sent()
    stay.wait()
    for copy in moves:
        copy.wait()


def forward_rows(gains, projected, attention_out, entry, cross_query, text, cross_out, feed_grad, feed_expand, feed_shrink, caption):
    lead = projected.shape[:3]
    width, ff, head_wide = attention_out.shape[1], feed_expand.shape[1], attention_out.shape[0]
    dma = pltpu.SemaphoreType.DMA
    tiles, tile_sem = Stream.scratch(feed_shrink)
    own = struct((lead[0], lead[2], width), F32)
    return launch(
        forward_kernel,
        1,
        vmem=dict(gains=gains),
        loaded=dict(
            projected=projected, attention_out=attention_out, entry=entry, cross_query=cross_query,
            text=text, cross_out=cross_out, feed_grad=feed_grad, feed_expand=feed_expand,
        ),
        hbm=dict(feed_shrink=feed_shrink, caption=caption),
        saved=dict(
            self_mixed=struct(lead + (head_wide,), BF16),
            second_normed=struct(lead + (width,), BF16),
            queries=struct(lead + (head_wide,), BF16),
            cross_mixed=struct(lead + (head_wide,), BF16),
            third_normed=struct(lead + (width,), BF16),
            active=struct(lead + (ff,), BF16),
            grad_hidden=struct(lead + (ff,), BF16),
            own_self=own,
            own_cross=own,
        ),
        hbm_outs=dict(captions=struct((8, caption.shape[0], caption.shape[1] // 8), BF16)),
        scratch=dict(
            tiles=tiles, tile_sem=tile_sem, move_send=dma((7,)), move_recv=dma((7,)), stay_sem=dma((1,)),
            **ImageSum.scratch(2, projected, width),
        ),
    )


def back_norm(r, job, i, t, before, source, sum_ref, full_ref, square):
    job.arrived()
    gain = r.gains[t : t + 1, :]
    for start in range(0, r.own_grad.shape[1], 32):
        at = slice(start, start + 32)
        grad, narrow, (term,) = post_backward(job.total(at), (before(at), source[i, at, :]), gain)
        r.own_grad[i, at, :] = grad
        full_ref[i, square.spot, at, :] = narrow
        sum_ref[...] += term


def middle_kernel(r):
    loads = r.loads
    images, heads = r.own_grad.shape[0], r.grad_queries.shape[3] // HDIM
    square = Square()
    pieces = [(0, "active", c) for c in range(0, r.active.shape[3], WIDE)] + [(1, "grad_hidden", 0)]
    sums = LineSum(r, (r.feed_grad, r.third_normed), pieces)
    sums.begin()
    loads.start("grad_hidden", "active", "own_feed", "own_cross", "cross_out", "queries", "text", "cross_query", "own_self")
    stream = Stream(r.feed_expand, r.tiles, r.tile_sem, passes=images)
    stream.start()
    greet(square.targets + sums.targets)
    third, second = [ImageSum.stage(r, square, t) for t in range(2)]
    r.third_gain[...] = jnp.zeros_like(r.third_gain)
    r.second_gain[...] = jnp.zeros_like(r.second_gain)
    grad_hidden = loads.got("grad_hidden")

    def expand_back(i):
        rows = image_rows(grad_hidden, i)

        def one(j, weight):
            at = tile_at(lax.rem(j, stream.count))
            put_image(r.part, i, at, product(rows, weight, NT).astype(BF16))

        for side in range(2):
            first = i * stream.count + side * stream.count // 2
            stream.run(first, first + stream.count // 2, one)
            third[i].start_side(side)

    expand_back(0)
    expand_back(1)
    sums.tick(3)
    third[0].forward()
    expand_back(2)
    third[1].forward()
    sums.tick(2)
    third[2].forward()
    sums.tick(1)

    def third_stage(i):
        feed, source = loads.got("own_feed"), loads.got("own_cross")
        back_norm(
            r, third[i], i, 2, lambda at: feed[i, at, :].astype(F32), source, r.third_gain, r.cross_grad, square
        )

    def cross_stage(i):
        third[i].gathered()
        third[i].sent()
        r.saves.save("cross_grad", i)
        queries, text = loads.got("queries"), loads.got("text")
        r.mixed_grad[...] = product(
            image_rows(r.cross_grad, i), loads.got("cross_out")[...], NT
        ).astype(BF16)

        def read(n, h):
            own, value = (tile_at(h + m * heads, HDIM) for m in range(2))
            if n == 0:
                return image_rows(queries, i, own)
            return r.mixed_grad[:, own] if n == 3 else text[i, :, own if n == 1 else value]

        def write(n, h, done):
            own, value = (tile_at(h + m * heads, HDIM) for m in range(2))
            if n == 0:
                put_image(r.grad_queries, i, own, done)
            else:
                r.grad_text[i, :, own if n == 1 else value] = done

        backward_heads(heads, read, write)
        project(r, i, image_rows(r.grad_queries, i), loads.got("cross_query"), NT)
        second[i].start()
        r.saves.save("grad_queries", i)
        r.saves.save("grad_text", i)

    def second_stage(i):
        back_norm(
            r, second[i], i, 1, lambda at: r.own_grad[i, at, :], loads.got("own_self"), r.second_gain,
            r.self_grad, square,
        )

    for i in range(images):
        third_stage(i)
        if i:
            third[i - 1].pass_on(r.cross_grad.at[i - 1])
        third[i].gather(r.cross_grad.at[i])
    sums.tick(2)
    cross_stage(0)
    third[2].pass_on(r.cross_grad.at[2])
    sums.tick(2)
    cross_stage(1)
    second[0].forward()
    sums.tick(2)
    cross_stage(2)
    second[1].forward()
    sums.tick(1)
    second[2].forward()
    sums.tick(1)
    for i in range(images):
        second_stage(i)
        r.saves.save("own_grad", i)
        if i:
            second[i - 1].pass_on(r.self_grad.at[i - 1])
        second[i].gather(r.self_grad.at[i])
    sums.tick(3)
    second[2].pass_on(r.self_grad.at[2])
    sums.tick()
    for i in range(images):
        second[i].gathered()
        r.saves.save("self_grad", i)
    for g in range(sums.count):
        done = sums.collect(g)
        if g + 1 < sums.count:
            r.shrink_sum[g * WIDE : (g + 1) * WIDE, :] = done.astype(F32).T.astype(BF16)
        else:
            r.expand_sum[...] = done
    for job in second:
        job.sent()
    for job in third + second:
        job.spread_sent()
    sums.settle()


def middle_rows(gains, feed_grad, own_feed, rows, text, cross_out, cross_query, feed_expand):
    lead = feed_grad.shape[:3]
    width, head_wide, ff = feed_grad.shape[3], cross_out.shape[0], feed_expand.shape[1]
    share = width // 8
    tiles, tile_sem = Stream.scratch(feed_expand)
    narrow = struct(lead + (width,), BF16)
    gain = struct((1, width), F32)
    return launch(
        middle_kernel,
        2,
        vmem=dict(gains=gains),
        loaded=dict(
            active=rows.active, grad_hidden=rows.grad_hidden, own_feed=own_feed, own_cross=rows.own_cross,
            cross_out=cross_out, queries=rows.queries, text=text, cross_query=cross_query,
            own_self=rows.own_self,
        ),
        hbm=dict(feed_grad=feed_grad, third_normed=rows.third_normed, feed_expand=feed_expand),
        saved=dict(
            cross_grad=narrow,
            self_grad=narrow,
            grad_queries=struct(lead + (head_wide,), BF16),
            grad_text=struct(text.shape, BF16),
            own_grad=struct((lead[0], lead[2], width), F32),
        ),
        outs=dict(
            third_gain=gain,
            second_gain=gain,
            shrink_sum=struct((ff, share), BF16),
            expand_sum=struct((share, WIDE), BF16),
        ),
        scratch=dict(
            tiles=tiles, tile_sem=tile_sem, mixed_grad=pltpu.VMEM((lead[1] * lead[2], head_wide), BF16),
            **ImageSum.scratch(2, feed_grad, width), **LineSum.scratch(ff // WIDE + 1, 2, feed_grad),
        ),
    )


def entry_kernel(r):
    loads = r.loads
    images, heads = r.own_out.shape[0], r.grad_projected.shape[3] // (3 * HDIM)
    square = Square()
    pieces = [(0, "grad_hidden", c) for c in range(0, r.grad_hidden.shape[3], WIDE)]
    pieces += [(1, "grad_queries", 0), (2, "cross_mixed", 0)]
    sums = LineSum(r, (r.third_normed, r.second_normed, r.cross_grad), pieces)
    sums.begin()
    loads.start("grad_hidden", "grad_queries", "cross_mixed", "self_grad", "attention_out", "projected", "weight_in")
    loads.start("own_grad", "entry", "grad_text")
    text = Stream(r.weight_text, r.text_tiles, r.text_sem)
    text.start()
    greet(square.targets + sums.targets)
    (jobs,) = [ImageSum.stage(r, square, t) for t in range(1)]
    r.first_gain[...] = jnp.zeros_like(r.first_gain)
    r.embed_term[...] = jnp.zeros_like(r.embed_term)

    def text_at(line):
        return r.texts.at[line * 2 + sums.core]

    def text_along(way, hop):
        ahead = 1 if way == 0 else -1
        source = text_at(sums.line - ahead * hop) if hop else r.grad_text
        return remote(
            source, text_at(sums.line - ahead * hop), r.text_send.at[way, hop], r.text_recv.at[way, hop],
            {"img": sums.place + 2 * ahead},
        )

    def text_across(way, hop):
        line = sums.line - (hop + 1) * (1 if way == 0 else -1)
        return remote(
            text_at(line), text_at(line), r.twin_send.at[way, hop], r.twin_recv.at[way, hop],
            {"img": sums.twin},
        )

    stay = pltpu.make_async_copy(r.grad_text, text_at(sums.line), r.stay_sem.at[0])
    over = remote(r.grad_text, text_at(sums.line), r.twin_send.at[0, 3], r.twin_recv.at[0, 3], {"img": sums.twin})

    def text_sends(way, hop):
        return (sums.distance(way) >= hop) & (sums.distance(1 - way) >= 1)

    def text_step(hop):
        for way in range(2):
            if hop:

                @pl.when(sums.distance(way) >= hop)
                def _():
                    text_along(way, hop - 1).wait_recv()
                    text_across(way, hop - 1).start()

            if hop < 3:

                @pl.when(text_sends(way, hop))
                def _():
                    text_along(way, hop).start()

    def text_settle():
        stay.wait()
        over.wait()
        for way in range(2):
            for hop in range(3):

                @pl.when(text_sends(way, hop))
                def _():
                    text_along(way, hop).wait_send()

                @pl.when(sums.distance(way) >= hop + 1)
                def _():
                    text_across(way, hop).wait()

    def self_stage(i):
        projected = loads.got("projected")
        r.mixed_grad[...] = product(
            image_rows(loads.got("self_grad"), i), loads.got("attention_out")[...], NT
        ).astype(BF16)

        def read(n, h):
            if n == 3:
                return r.mixed_grad[:, tile_at(h, HDIM)]
            return image_rows(projected, i, tile_at(h + n * heads, HDIM))

        def write(n, h, done):
            put_image(r.grad_projected, i, tile_at(h + n * heads, HDIM), done)

        backward_heads(heads, read, write)
        project(r, i, image_rows(r.grad_projected, i), loads.got("weight_in"))
        jobs[i].start()
        r.saves.save("grad_projected", i)

    def entry_stage(i):
        job = jobs[i]
        job.arrived()
        before, entry = loads.got("own_grad"), loads.got("entry")
        for start in range(0, before.shape[1], 32):
            at = slice(start, start + 32)
            wide_rows, _, terms = post_entry(
                job.total(at), (before[i, at, :], entry[i, at, :], r.mask[i, at, :]), r.gains[0:1, :]
            )
            r.own_out[i, at, :] = wide_rows
            r.first_gain[...] += terms[0]
            r.embed_term[...] += terms[1]
        r.saves.save("own_out", i)

    def caption_tile(j, weight):
        grad = loads.got("grad_text")[...]
        done = product(grad.reshape(-1, grad.shape[2]), weight, NT)
        r.caption_part[:, tile_at(j)] = done.astype(BF16)

    stay.start()
    over.start()
    sums.tick(3)
    text_step(0)
    sums.tick(1)
    self_stage(0)
    sums.tick(2)
    self_stage(1)
    jobs[0].forward()
    sums.tick(3)
    self_stage(2)
    jobs[1].forward()
    sums.tick(2)
    jobs[2].forward()
    text_step(1)
    loads.got("grad_text")
    text.run(0, text.count // 2, caption_tile)
    sums.tick(3)
    text.run(text.count // 2, text.count, caption_tile)
    r.saves.save("caption_part")
    sums.tick(2)
    entry_stage(0)
    entry_stage(1)
    sums.tick(2)
    text_step(2)
    entry_stage(2)
    sums.tick()
    text_step(3)
    for g in range(sums.count - 2):
        r.expand_sum[:, g * WIDE : (g + 1) * WIDE] = sums.collect(g)
    r.query_sum[...] = sums.collect(sums.count - 2)
    r.cross_sum[...] = sums.collect(sums.count - 1).astype(F32).T.astype(BF16)
    for job in jobs:
        job.sent()
    text_settle()
    sums.settle()


def entry_rows(gains, mask, rows, back, projected, entry, attention_out, weight_in, weight_text, grad_hidden):
    lead = projected.shape[:3]
    width = attention_out.shape[1]
    share = width // 8
    dma = pltpu.SemaphoreType.DMA
    text_tiles, text_sem = Stream.scratch(weight_text)
    text_rows = back.grad_text.shape[0] * back.grad_text.shape[1]
    gain = struct((1, width), F32)
    return launch(
        entry_kernel,
        3,
        vmem=dict(gains=gains, mask=mask),
        loaded=dict(
            grad_hidden=grad_hidden, self_grad=back.self_grad, attention_out=attention_out,
            projected=projected, weight_in=weight_in, own_grad=back.own_grad, entry=entry,
            grad_text=back.grad_text, grad_queries=back.grad_queries, cross_mixed=rows.cross_mixed,
        ),
        hbm=dict(
            third_normed=rows.third_normed, second_normed=rows.second_normed, cross_grad=back.cross_grad,
            weight_text=weight_text,
        ),
        saved=dict(
            grad_projected=struct(projected.shape, BF16),
            own_out=struct(back.own_grad.shape, F32),
            caption_part=struct((text_rows, weight_text.shape[0]), BF16),
        ),
        outs=dict(
            first_gain=gain,
            embed_term=gain,
            expand_sum=struct((share, grad_hidden.shape[3]), BF16),
            query_sum=struct((share, WIDE), BF16),
            cross_sum=struct((WIDE, share), BF16),
        ),
        hbm_outs=dict(texts=struct((8,) + back.grad_text.shape, BF16)),
        scratch=dict(
            text_tiles=text_tiles, text_sem=text_sem,
            mixed_grad=pltpu.VMEM((lead[1] * lead[2], attention_out.shape[0]), BF16),
            text_send=dma((2, 3)), text_recv=dma((2, 3)), twin_send=dma((2, 4)), twin_recv=dma((2, 4)),
            stay_sem=dma((1,)),
            **ImageSum.scratch(1, projected, width),
            **LineSum.scratch(grad_hidden.shape[3] // WIDE + 2, 3, rows.third_normed),
        ),
    )


def line_kernel(r):
    square = Square()
    spot, beside, above, corner, peers = (
        square.spot, square.beside, square.above, square.corner, square.peers
    )
    pieces = [(0, "grad_projected", c) for c in (0, WIDE, 2 * WIDE)]
    pieces += [(1, "self_mixed", 0)]
    sums = LineSum(r, (r.first_normed, r.self_grad), pieces)
    sums.begin()
    loads = r.loads
    loads.start("grad_projected", "self_mixed", "active", "own_cross")
    shrink = Stream(r.feed_shrink, r.tiles, r.tile_sem, True)
    shrink.start()

    def text_load(j):
        slot = lax.rem(j, 2)
        return (
            pltpu.make_async_copy(r.captions.at[j], r.caption_block.at[slot], r.block_sem.at[0, slot]),
            pltpu.make_async_copy(r.texts.at[j], r.text_block.at[slot], r.block_sem.at[1, slot]),
        )

    for copy in text_load(0):
        copy.start()
    targets = [sums.targets[0]] + square.targets + sums.targets[1:] + [{"mp": corner}]
    rows, columns = r.held.shape[2], r.held.shape[3]
    greet(targets)

    low = rows // 3

    def row_block(owner, j):
        return owner * 3 + j

    def block(job, owner, side, j):
        if job == 0:
            b = row_block(owner, j)
            return r.mixed_part.at[lax.div(b, 4), lax.rem(b, 4), :, pl.ds(side * columns, columns)]
        at = pl.ds(pl.multiple_of(owner * columns, 128), columns)
        return r.caption_part.at[pl.ds(side * rows + j * low, low), at]

    thirds = [pl.ds(j * low, low) for j in range(3)]

    def load(job, slot, owner, side):
        return [
            pltpu.make_async_copy(
                block(job, owner, side, j), r.held.at[job, slot, thirds[j]], r.load_sem.at[job, slot, j]
            )
            for j in range(3)
        ]

    def first_copy(job, side, order):
        owner = corner if order == 0 else peers[side]
        slot = side * 2 + order
        return [
            remote(
                block(job, owner, side, j),
                r.flat_first.at[job, slot, thirds[j]],
                r.flat_send.at[job, slot, j],
                r.flat_recv.at[job, slot, j],
                {"mp": peers[side]},
            )
            for j in range(3)
        ]

    def second_copy(job, side):
        return remote(
            r.flat_out.at[job, side],
            r.flat_second.at[job, side],
            r.flat_send.at[job, 4 + side, 0],
            r.flat_recv.at[job, 4 + side, 0],
            {"mp": peers[1 - side]},
        )

    def flat_start(job):
        for order in range(2):
            for side in range(2):
                for copy in first_copy(job, side, order):
                    copy.start()
        for side in range(2):
            for copy in load(job, side, peers[1 - side], side) + load(job, 2 + side, spot, side):
                copy.start()

    def flat_forward(job):
        for side in range(2):
            for copy in load(job, side, peers[1 - side], side):
                copy.wait()
            for copy in first_copy(job, side, 0):
                copy.wait_recv()
            r.flat_out[job, side] = (
                r.held[job, side].astype(F32) + r.flat_first[job, side * 2].astype(F32)
            ).astype(BF16)
            second_copy(job, side).start()

    def flat_finish(job):
        for side in range(2):
            for copy in load(job, 2 + side, spot, side):
                copy.wait()
            for copy in first_copy(job, side, 1):
                copy.wait_recv()
            second_copy(job, side).wait_recv()
            total = (
                r.held[job, 2 + side].astype(F32)
                + r.flat_first[job, side * 2 + 1].astype(F32)
                + r.flat_second[job, side].astype(F32)
            )
            if job == 0:
                r.mixed_out[:, side * columns : (side + 1) * columns] = total.astype(BF16)
            else:
                r.caption_out[side * rows : (side + 1) * rows, :] = total.astype(BF16)
        for side in range(2):
            for order in range(2):
                for copy in first_copy(job, side, order):
                    copy.wait_send()
            second_copy(job, side).wait_send()

    def move(i):
        b = i * 4 + spot
        keeper, j = lax.div(b, 3), lax.rem(b, 3)
        target = r.tokens_out.at[pl.ds(pl.multiple_of(j * low, low), low)]
        away = remote(
            r.own_out.at[i], target, r.move_send.at[i], r.move_recv.at[j], {"mp": keeper}
        )
        here = pltpu.make_async_copy(r.own_out.at[i], target, r.stay_sem.at[0])
        return keeper, away, here

    def move_start():
        for i in range(3):
            keeper, away, here = move(i)

            @pl.when(keeper != spot)
            def _():
                away.start()

            @pl.when(keeper == spot)
            def _():
                here.start()

    def move_finish():
        for i in range(3):
            keeper, away, here = move(i)

            @pl.when(keeper != spot)
            def _():
                away.wait_send()

            @pl.when(keeper == spot)
            def _():
                here.wait()

        for j in range(3):
            arrival = remote(
                r.own_out.at[0], r.tokens_out.at[thirds[j]], r.move_send.at[0], r.move_recv.at[j], {"mp": corner}
            )

            @pl.when(lax.rem(row_block(spot, j), 4) != spot)
            def _():
                arrival.wait_recv()

    def mixed_tile(j, weight):
        done = product(all_rows(loads.got("active")), weight).astype(BF16)
        at = tile_at(j)
        r.mixed_part[:, :, :, at] = done.reshape(r.mixed_part.shape[:3] + (TILE,))
        for i in range(3):
            own = r.mixed_part[i, spot, :, at].astype(F32) + loads.got("own_cross")[i, :, at]
            r.mixed_part[i, spot, :, at] = own.astype(BF16)

    def text_product(j, carry):
        for copy in text_load(j):
            copy.wait()

        @pl.when(j < 7)
        def _():
            for copy in text_load(j + 1):
                copy.start()

        left = r.caption_block[lax.rem(j, 2)]

        def one(n, inner):
            at = tile_at(n)
            right = r.text_block[lax.rem(j, 2), :, :, at]
            r.text_sum[:, at] += product(left, right.reshape(-1, TILE), TN)
            return inner

        return lax.fori_loop(0, r.text_sum.shape[1] // TILE, one, carry)

    def small_step(slot, device):
        copy = remote(
            r.small_out, r.small_in.at[slot], r.small_send.at[slot], r.small_recv.at[slot], device
        )
        copy.start()
        return copy

    r.small_out[...] = r.small[...]
    r.text_sum[...] = jnp.zeros_like(r.text_sum)

    def small_add(slot, copy):
        copy.wait()
        r.small_out[...] += r.small_in[slot]

    copy = small_step(0, targets[0])
    sums.tick(2)
    small_add(0, copy)
    copy = small_step(1, targets[1])
    sums.tick(1)
    small_add(1, copy)
    copy = small_step(2, targets[2])
    flat_start(1)
    move_start()
    sums.tick(2)
    small_add(2, copy)
    wide = [small_step(3 + j, device) for j, device in enumerate(targets[3:6])]
    loads.got("active")
    loads.got("own_cross")
    shrink.run(0, shrink.count, mixed_tile)
    flat_start(0)
    sums.tick(2)
    flat_forward(1)
    lax.fori_loop(0, 4, text_product, 0)
    sums.tick(2)
    lax.fori_loop(4, 8, text_product, 0)
    sums.tick(2)
    flat_forward(0)
    flat_finish(1)
    sums.tick(2)
    move_finish()
    sums.tick()
    flat_finish(0)
    for copy in wide:
        copy.wait()
    r.small_out[...] += r.small_in[3] + r.small_in[4] + r.small_in[5]
    for g in range(3):
        r.in_sum[:, g * WIDE : (g + 1) * WIDE] = sums.collect(g)
    r.self_sum[...] = sums.collect(3).astype(F32).T.astype(BF16)
    sums.settle()


def line_sums(first_normed, rows, back, entry, small, feed_shrink):
    images, low, full = entry.own_out.shape
    height, columns = images * low, full // 2
    share = full // 8
    dma = pltpu.SemaphoreType.DMA
    block = (height, columns)
    lead = first_normed.shape[:3]
    tiles, tile_sem = Stream.scratch(feed_shrink, True)
    captions, texts = rows.captions, entry.texts
    return launch(
        line_kernel,
        4,
        vmem=dict(small=small),
        loaded=dict(
            grad_projected=entry.grad_projected, self_mixed=rows.self_mixed, active=rows.active,
            own_cross=rows.own_cross,
        ),
        hbm=dict(
            first_normed=first_normed, self_grad=back.self_grad, caption_part=entry.caption_part,
            own_out=entry.own_out, feed_shrink=feed_shrink, captions=captions, texts=texts,
        ),
        outs=dict(
            in_sum=struct((share, 3 * WIDE), BF16),
            self_sum=struct((WIDE, share), BF16),
            text_sum=struct((captions.shape[2], texts.shape[3]), F32),
            small_out=struct(small.shape, F32),
            mixed_out=struct((height, full), BF16),
            caption_out=struct((entry.caption_part.shape[0], columns), BF16),
            tokens_out=struct((height, full), F32),
        ),
        scratch=dict(
            mixed_part=pltpu.VMEM(lead + (full,), BF16),
            tiles=tiles, tile_sem=tile_sem,
            caption_block=pltpu.VMEM((2,) + captions.shape[1:], BF16),
            text_block=pltpu.VMEM((2,) + texts.shape[1:], BF16),
            block_sem=dma((2, 2)),
            small_in=pltpu.VMEM((6,) + small.shape, F32),
            held=pltpu.VMEM((2, 4) + block, BF16),
            flat_first=pltpu.VMEM((2, 4) + block, BF16),
            flat_out=pltpu.VMEM((2, 2) + block, BF16),
            flat_second=pltpu.VMEM((2, 2) + block, BF16),
            small_send=dma((6,)),
            small_recv=dma((6,)),
            load_sem=dma((2, 4, 3)),
            flat_send=dma((2, 6, 3)),
            flat_recv=dma((2, 6, 3)),
            stay_sem=dma((1,)),
            move_send=dma((3,)),
            move_recv=dma((3,)),
            **LineSum.scratch(4, 2, first_normed),
        ),
    )


def plain_step(left, weight, dims, post, gain, rows_in):
    part = product(left, weight, dims).astype(BF16)
    total = lax.psum_scatter(part, "mp", scatter_dimension=0, tiled=True).astype(F32)
    wide, narrow, sums = post(total, rows_in, gain)
    if narrow is None:
        return (wide, *sums)
    return (wide, lax.all_gather(narrow, "mp", axis=0, tiled=True), *sums)


def plain_heads(array, images, parts=1):
    rows, columns = array.shape
    return array.reshape(images, rows // images, parts, -1, HDIM).transpose(2, 0, 3, 1, 4)


def plain_rows(array):
    images, heads, rows, _ = array.shape
    return array.transpose(0, 2, 1, 3).reshape(images * rows, heads * HDIM)


def per_head(function):
    return jax.vmap(jax.vmap(function))


def gelu_exact(values_in):
    return jax.nn.gelu(values_in, approximate=False)


def layer_plain(images, own_rows, gains, own_entry, own_float, first_normed, projected, text_pairs, feed_grad, weights):
    attention_out, cross_query, cross_out, feed_expand, feed_shrink, weight_in, weight_text, caption = weights
    queries, keys_in, values_in = plain_heads(projected, images, 3)
    text_keys, text_values = plain_heads(text_pairs, images, 2)
    self_mixed = plain_rows(per_head(attend)(queries, keys_in, values_in))
    own_self, second_normed = plain_step(
        self_mixed, attention_out, NN, post_forward, gains[1:2], (own_entry,)
    )
    cross_queries = plain_heads(product(second_normed, cross_query).astype(BF16), images)[0]
    cross_mixed = plain_rows(per_head(attend)(cross_queries, text_keys, text_values))
    own_cross, third_normed = plain_step(
        cross_mixed, cross_out, NN, post_forward, gains[2:3], (own_self,)
    )
    hidden = product(third_normed, feed_expand)
    active = gelu_exact(hidden).astype(BF16)
    mixed_sum = lax.psum_scatter(
        product(active, feed_shrink).astype(BF16), "mp", scatter_dimension=0, tiled=True
    )
    mixed_out = (own_cross + mixed_sum.astype(F32)).astype(BF16)
    _, gelu_pull = jax.vjp(gelu_exact, hidden)
    grad_hidden = gelu_pull(product(feed_grad, feed_shrink, NT))[0].astype(BF16)
    own_grad, cross_grad, third_gain = plain_step(
        grad_hidden, feed_expand, NT, post_backward, gains[2:3],
        (own_rows(feed_grad).astype(F32), own_cross),
    )
    grad_mixed = plain_heads(product(cross_grad, cross_out, NT).astype(BF16), images)[0]
    back = per_head(attend_backward_head)(cross_queries, text_keys, text_values, grad_mixed)
    grad_queries, grad_keys, grad_values = (plain_rows(part) for part in back)
    grad_text = jnp.concatenate([grad_keys, grad_values], axis=1)
    own_grad, self_grad, second_gain = plain_step(
        grad_queries, cross_query, NT, post_backward, gains[1:2], (own_grad, own_self)
    )
    grad_mixed = plain_heads(product(self_grad, attention_out, NT).astype(BF16), images)[0]
    back = per_head(attend_backward_head)(queries, keys_in, values_in, grad_mixed)
    grad_projected = jnp.concatenate([plain_rows(part) for part in back], axis=1)
    tokens_grad, first_gain, embed_term = plain_step(
        grad_projected, weight_in, NN, post_entry, gains[0:1], (own_grad, own_entry, own_float)
    )
    caption_grad = lax.psum_scatter(
        product(grad_text, weight_text, NT).astype(BF16), "mp", scatter_dimension=1, tiled=True
    )
    small = jnp.concatenate([first_gain, second_gain, third_gain, embed_term], axis=0)
    return (
        mixed_out,
        tokens_grad,
        caption_grad,
        lax.psum_scatter(small, ("img", "mp"), scatter_dimension=1, tiled=True),
        image_sum(rows_product(first_normed, grad_projected)),
        image_sum(rows_product(self_mixed, self_grad), 1),
        image_sum(rows_product(second_normed, grad_queries)),
        image_sum(rows_product(caption, grad_text)),
        image_sum(rows_product(cross_mixed, cross_grad), 1),
        image_sum(rows_product(third_normed, grad_hidden)),
        image_sum(rows_product(active, feed_grad), 1),
    )


def layer_square(images, own_mask, gains, own_entry, first_normed, projected, text_pairs, feed_grad, weights):
    attention_out, cross_query, cross_out, feed_expand, feed_shrink, weight_in, weight_text, caption = weights
    width = first_normed.shape[1]
    spot = lax.axis_index("mp")

    def four(rows_in):
        return rows_in.reshape(images, 4, -1, rows_in.shape[-1])

    text = text_pairs.reshape(images, -1, text_pairs.shape[1])
    four_grad, four_projected, four_normed = four(feed_grad), four(projected), four(first_normed)
    own_feed = lax.dynamic_index_in_dim(four_grad, spot, 1, False)
    rows = forward_rows(
        gains, four_projected, attention_out, own_entry, cross_query, text, cross_out, four_grad,
        feed_expand, feed_shrink, caption,
    )
    back = middle_rows(gains, four_grad, own_feed, rows, text, cross_out, cross_query, feed_expand)
    entry = entry_rows(
        gains, own_mask, rows, back, four_projected, own_entry, attention_out, weight_in, weight_text,
        rows.grad_hidden[:, :, :, WIDE:],
    )
    terms = [entry.first_gain, back.second_gain, back.third_gain, entry.embed_term]
    small = jnp.concatenate(terms + [jnp.zeros_like(entry.embed_term)] * 4, axis=0)
    late = line_sums(four_normed, rows, back, entry, small, feed_shrink)
    slice_width = width // 32
    at = (lax.axis_index("img") * 4 + spot) * slice_width
    return (
        late.mixed_out,
        late.tokens_out,
        late.caption_out,
        lax.dynamic_slice_in_dim(late.small_out, at, slice_width, 1),
        late.in_sum,
        late.self_sum,
        entry.query_sum,
        late.text_sum,
        entry.cross_sum,
        jnp.concatenate([back.expand_sum, entry.expand_sum], axis=1),
        back.shrink_sum,
    )


def body(
    square,
    tokens,
    caption,
    masked,
    out_grad,
    mask_embed,
    norm_gains,
    attention_in,
    attention_out,
    cross_query,
    cross_text,
    cross_out,
    feed_expand,
    feed_shrink,
):
    images, length = masked.shape
    rows_all = images * length
    count = lax.axis_size("mp")
    spot = lax.axis_index("mp")
    text_width = caption.shape[1]

    def own_rows(rows_in):
        return lax.dynamic_slice_in_dim(rows_in, spot * (rows_all // count), rows_all // count, 0)

    def own_quarters(rows_in):
        parts = rows_in.reshape(images, count, length // count, -1)
        return lax.dynamic_index_in_dim(parts, spot, 1, False)

    def enter(rows_in, mask):
        return jnp.where(mask, mask_embed.astype(F32), rows_in.astype(F32))

    own = own_quarters if square else own_rows
    mask_column = masked.reshape(rows_all, 1) > 0
    own_mask = own(mask_column)
    own_float = own_mask.astype(F32)
    own_entry = enter(own(tokens), own_mask)
    first_unit, _ = norm_parts(enter(tokens, mask_column))
    first_normed = (first_unit * norm_gains[0:1]).astype(BF16)
    weight_in = attention_in.transpose(1, 2, 0).reshape(-1, tokens.shape[1])
    projected = product(first_normed, weight_in, NT).astype(BF16)
    weight_text = cross_text.reshape(text_width, -1)
    text_pairs = product(caption, weight_text).astype(BF16)
    feed_grad = jnp.where(mask_column, out_grad, jnp.zeros_like(out_grad))
    weights = (
        attention_out, cross_query, cross_out, feed_expand, feed_shrink, weight_in, weight_text, caption,
    )
    if square:
        done = layer_square(
            images, own_float, norm_gains, own_entry, first_normed, projected, text_pairs, feed_grad, weights
        )
    else:
        done = layer_plain(
            images, own_rows, norm_gains, own_entry, own_float, first_normed, projected, text_pairs,
            feed_grad, weights,
        )
    mixed_out, tokens_grad, caption_grad, small_sums, self_in, *sums = done
    self_out, cross_query_sum, cross_text_sum, cross_out_sum, expand_sum, shrink_sum = (
        part.astype(F32) for part in sums
    )
    return (
        mixed_out,
        tokens_grad,
        caption_grad.astype(F32),
        small_sums[3],
        small_sums[0:3],
        self_in.astype(F32).reshape(-1, 3, attention_in.shape[2]),
        self_out,
        cross_query_sum,
        cross_text_sum.reshape(-1, 2, cross_text.shape[2]),
        cross_out_sum,
        expand_sum,
        shrink_sum,
    )


def solution(mesh):
    square = mesh.shape["mp"] == 4 and mesh.shape["img"] == 8
    return jax.shard_map(
        functools.partial(body, square),
        mesh=mesh,
        in_specs=(
            P("img", None),
            P("img", None),
            P("img", None),
            P("img", None),
            P(),
            P(),
            P(None, None, "mp"),
            P("mp", None),
            P(None, "mp"),
            P(None, None, "mp"),
            P("mp", None),
            P(None, "mp"),
            P("mp", None),
        ),
        out_specs=(
            P(("img", "mp"), None),
            P(("img", "mp"), None),
            P("img", "mp"),
            P(("img", "mp")),
            P(None, ("img", "mp")),
            P("img", None, "mp"),
            P("mp", "img"),
            P("img", "mp"),
            P("img", None, "mp"),
            P("mp", "img"),
            P("img", "mp"),
            P("mp", "img"),
        ),
        check_vma=False,
    )
```

```python
import dataclasses
import functools
import math
import types
from typing import Any

import jax
import jax.numpy as jnp
from jax import lax
from jax.experimental import pallas as pl
from jax.experimental.pallas import tpu as pltpu
from jax.sharding import PartitionSpec as P

HDIM = 128
EPSILON = 1e-05
SCALE = 1.0 / math.sqrt(HDIM)
VMEM_BYTES = 62 * 1024 * 1024
MESH = pl.DeviceIdType.MESH
BF16 = jnp.bfloat16
F32 = jnp.float32
WIDE = 512
TILE = 256

MIDDLE_TICKS = (1, 1, 1, 5, 0, 1, 0, 4, 2, 0, 2, 0, 0, 4, 1, 2, 0, 2, 1)
ENTRY_TICKS = (4, 0, 0, 0, 0, 0, 4, 4, 0, 2, 1, 2, 1, 1, 0, 0, 0, 0, 0, 1)

NN = (((1,), (0,)), ((), ()))
NT = (((1,), (1,)), ((), ()))
TN = (((0,), (0,)), ((), ()))


def product(left, right, dims=NN):
    return lax.dot_general(left, right, dims, preferred_element_type=F32)


def image_sum(part, dimension=0):
    return lax.psum_scatter(part, "img", scatter_dimension=dimension, tiled=True).astype(F32)


def rows_product(left, right):
    return product(left, right, TN).astype(BF16)


def norm_parts(rows_in):
    centre = rows_in - jnp.mean(rows_in, axis=-1, keepdims=True)
    root_inverse = lax.rsqrt(jnp.mean(centre * centre, axis=-1, keepdims=True) + EPSILON)
    return (centre * root_inverse, root_inverse)


def norm_back(grad_rows, unit_rows, root_inverse, gain_row):
    weighted = grad_rows * gain_row
    middle = jnp.mean(weighted, axis=-1, keepdims=True)
    along = jnp.mean(weighted * unit_rows, axis=-1, keepdims=True)
    return root_inverse * (weighted - middle - unit_rows * along)


def post_forward(total, rows_in, gain):
    fresh = rows_in[0] + total
    unit, _ = norm_parts(fresh)
    return fresh, (unit * gain).astype(BF16), ()


def post_backward(total, rows_in, gain):
    before, source = rows_in
    unit, root = norm_parts(source)
    grad = before + norm_back(total, unit, root, gain)
    return grad, grad.astype(BF16), (jnp.sum(total * unit, axis=0, keepdims=True),)


def post_entry(total, rows_in, gain):
    before, source, mask = rows_in
    unit, root = norm_parts(source)
    grad = before + norm_back(total, unit, root, gain)
    sums = (
        jnp.sum(total * unit, axis=0, keepdims=True),
        jnp.sum(grad * mask, axis=0, keepdims=True),
    )
    return grad * (1.0 - mask), None, sums


def remote(source, target, send, recv, device):
    return pltpu.make_async_remote_copy(
        src_ref=source,
        dst_ref=target,
        send_sem=send,
        recv_sem=recv,
        device_id=device,
        device_id_type=MESH,
    )


def greet(targets):
    barrier = pltpu.get_barrier_semaphore()
    for target in targets:
        pl.semaphore_signal(barrier, inc=1, device_id=target, device_id_type=MESH)
    pl.semaphore_wait(barrier, len(targets))


def tile_at(j, wide=TILE):
    return pl.ds(pl.multiple_of(j * wide, wide), wide)


def all_rows(ref, columns=slice(None)):
    part = ref[:, :, :, columns]
    return part.reshape(-1, part.shape[3])


def image_rows(ref, i, columns=slice(None)):
    part = ref[i, :, :, columns]
    return part.reshape(-1, part.shape[2])


def put_image(ref, i, columns, value):
    ref[i, :, :, columns] = value.reshape(ref.shape[1], ref.shape[2], value.shape[1])


class Loads:
    def __init__(self, names, sources, targets, sem):
        self.targets = dict(zip(names, targets))
        self.copies = {
            name: pltpu.make_async_copy(source, target, sem.at[i])
            for i, (name, source, target) in enumerate(zip(names, sources, targets))
        }
        self.waiting = set()

    def start(self, *names):
        for name in names:
            self.copies[name].start()
            self.waiting.add(name)

    def got(self, name):
        if name in self.waiting:
            self.waiting.remove(name)
            self.copies[name].wait()
        return self.targets[name]


class Stream:
    def __init__(self, source, tiles, sem, columns=False, passes=1):
        self.source, self.tiles, self.sem, self.columns = source, tiles, sem, columns
        self.count = source.shape[1 if columns else 0] // TILE
        self.total, self.depth = passes * self.count, tiles.shape[0]

    def copy(self, j):
        slot, at = lax.rem(j, self.depth), tile_at(lax.rem(j, self.count))
        part = self.source.at[:, at] if self.columns else self.source.at[at, :]
        return pltpu.make_async_copy(part, self.tiles.at[slot], self.sem.at[slot])

    def start(self):
        for j in range(self.depth - 1):
            self.copy(j).start()

    def run(self, first, last, use):
        def one(j, carry):
            self.copy(j).wait()
            later = j + self.depth - 1

            @pl.when(later < self.total)
            def _():
                self.copy(later).start()

            use(j, self.tiles[lax.rem(j, self.depth)])
            return carry

        lax.fori_loop(first, last, one, 0)

    @staticmethod
    def scratch(source, columns=False, depth=2):
        shape = (source.shape[0], TILE) if columns else (TILE, source.shape[1])
        return pltpu.VMEM((depth,) + shape, source.dtype), pltpu.SemaphoreType.DMA((depth,))


class Saves:
    def __init__(self, names, sources, targets, sem):
        self.refs = {n: pair for n, pair in zip(names, zip(sources, targets))}
        self.sem, self.running, self.names = sem, [], names

    def save(self, name, i=None):
        source, target = self.refs[name]
        if i is not None:
            source, target = source.at[i], target.at[i]
        copy = pltpu.make_async_copy(source, target, self.sem.at[self.names.index(name), i or 0])
        copy.start()
        self.running.append(copy)

    def finish(self):
        for copy in self.running:
            copy.wait()


def launch(kernel, ident, vmem=(), loaded=(), hbm=(), outs=(), saved=(), hbm_outs=(), scratch=()):
    vmem, loaded, hbm, outs = dict(vmem), dict(loaded), dict(hbm), dict(outs)
    starts = {n: a[1] if isinstance(a, tuple) else 0 for n, a in loaded.items()}
    loaded = {n: a[0] if isinstance(a, tuple) else a for n, a in loaded.items()}
    saved, hbm_outs, scratch = dict(saved), dict(hbm_outs), dict(scratch)
    names = [*vmem, *loaded, *hbm, *outs, *saved, *hbm_outs]
    buffers = [
        pltpu.VMEM(a.shape[:-1] + (a.shape[-1] - starts.get(n, 0),), a.dtype)
        for n, a in [*loaded.items(), *saved.items()]
    ]

    def source(ref, start):
        return ref.at[:, :, :, start:] if start else ref

    def run(*refs):
        r = types.SimpleNamespace(**dict(zip(names, refs)))
        rest = refs[len(names) :]
        rest, buffer_refs = rest[: len(scratch)], rest[len(scratch) : len(scratch) + len(buffers)]
        for name, ref in zip(scratch, rest):
            setattr(r, name, ref)
        sources = [source(getattr(r, n), starts[n]) for n in loaded]
        r.loads = Loads(list(loaded), sources, buffer_refs[: len(loaded)], refs[-2])
        kept = buffer_refs[len(loaded) :]
        r.saves = Saves(list(saved), kept, [getattr(r, n) for n in saved], refs[-1])
        for name, ref in zip(saved, kept):
            setattr(r, name, ref)
        kernel(r)
        r.saves.finish()

    in_vmem = pl.BlockSpec(memory_space=pltpu.VMEM)
    in_hbm = pl.BlockSpec(memory_space=pl.ANY)
    result = pl.pallas_call(
        run,
        out_shape=[*outs.values(), *saved.values(), *hbm_outs.values()],
        in_specs=[in_vmem] * len(vmem) + [in_hbm] * (len(loaded) + len(hbm)),
        out_specs=[in_vmem] * len(outs) + [in_hbm] * (len(saved) + len(hbm_outs)),
        scratch_shapes=[
            *scratch.values(),
            *buffers,
            pltpu.SemaphoreType.DMA((max(len(loaded), 1),)),
            pltpu.SemaphoreType.DMA((max(len(saved), 1), 3)),
        ],
        compiler_params=pltpu.CompilerParams(
            collective_id=ident, has_side_effects=True, vmem_limit_bytes=VMEM_BYTES
        ),
        cost_estimate=pl.CostEstimate(
            flops=60_000_000_000, bytes_accessed=80_000_000, transcendentals=0
        ),
    )(*vmem.values(), *loaded.values(), *hbm.values())
    return types.SimpleNamespace(**dict(zip([*outs, *saved, *hbm_outs], result)))


def struct(shape, kind):
    return jax.ShapeDtypeStruct(tuple(shape), kind)


class Square:
    def __init__(self):
        self.spot = lax.axis_index("mp")
        up, across = lax.div(self.spot, 2), lax.rem(self.spot, 2)
        self.beside = up * 2 + (1 - across)
        self.above = (1 - up) * 2 + across
        self.corner = (1 - up) * 2 + (1 - across)
        self.peers = (self.beside, self.above)
        self.targets = [{"mp": self.beside}, {"mp": self.above}]


class LineSum:
    def __init__(self, r, lefts, pieces):
        self.r, self.lefts, self.pieces = r, lefts, pieces
        self.count, self.ticked = len(pieces), 0
        self.share = r.line_own.shape[2]
        self.place = lax.axis_index("img")
        self.line, self.core = lax.div(self.place, 2), lax.rem(self.place, 2)
        self.twin = self.line * 2 + (1 - self.core)
        self.others = [lax.rem(self.line + j, 4) * 2 + self.core for j in (1, 2, 3)]
        self.targets = [{"img": self.twin}] + [{"img": o} for o in self.others]

    @staticmethod
    def scratch(count, lefts, left):
        dma = pltpu.SemaphoreType.DMA
        share = left.shape[3] // 8
        return dict(
            line_left=pltpu.VMEM((lefts, 2) + tuple(left.shape[:3]) + (2 * share,), BF16),
            line_left_sem=dma((lefts, 2)),
            core_out=pltpu.VMEM((count, 2, share, WIDE), BF16),
            core_in=pltpu.VMEM((count, 2, share, WIDE), BF16),
            line_own=pltpu.VMEM((count, 4, share, WIDE), BF16),
            line_in=pltpu.VMEM((count, 5, share, WIDE), BF16),
            core_send=dma((count, 2)),
            core_recv=dma((count, 2)),
            line_send=dma((count, 2, 3)),
            line_recv=dma((count, 2, 3)),
        )

    def left_copy(self, n, k):
        slot = k % 2
        at = tile_at(self.chunk_at(k), 2 * self.share)
        return pltpu.make_async_copy(
            self.lefts[n].at[:, :, :, at], self.r.line_left.at[n, slot], self.r.line_left_sem.at[n, slot]
        )

    def begin(self):
        for n in range(len(self.lefts)):
            self.left_copy(n, 0).start()

    def core_copy(self, g, k):
        r, slot = self.r, k % 2
        return remote(
            r.core_out.at[g, slot], r.core_in.at[g, slot], r.core_send.at[g, slot],
            r.core_recv.at[g, slot], {"img": self.twin},
        )

    def slot_at(self, way, s, line):
        first = (line < 2) if way == 0 else (line >= 2)
        return jnp.where(first, s, s + 2)

    def line_copy(self, g, way, s, chunk):
        r, ahead = self.r, 1 if way == 0 else -1
        return remote(
            r.line_own.at[g, chunk],
            r.line_in.at[g, self.slot_at(way, s, self.line + ahead)],
            r.line_send.at[g, way, s],
            r.line_recv.at[g, way, s],
            {"img": self.place + 2 * ahead},
        )

    def chunk_at(self, k):
        if k == 3:
            return self.line
        low = 3 - k - jnp.where(self.line + k == 3, 1, 0)
        high = k + jnp.where(self.line == k, 1, 0)
        return jnp.where(self.line < 2, low, high)

    def distance(self, way):
        return self.line if way == 0 else 3 - self.line

    def multiply(self, g, k):
        r = self.r
        left, name, column = self.pieces[g]
        right = r.loads.got(name) if name in r.loads.targets else getattr(r, name)
        right = all_rows(right, slice(column, column + WIDE))
        chunk = self.chunk_at(k)

        if k >= 2:
            self.core_copy(g, k).wait_send()
        for mine in (False, True):
            part = self.core if mine else 1 - self.core
            block = r.line_left[left, k % 2, :, :, :, tile_at(part, self.share)]
            done = product(block.reshape(-1, self.share), right, TN).astype(BF16)
            if mine:
                r.line_own[g, chunk] = done
            else:
                r.core_out[g, k % 2] = done
                self.core_copy(g, k).start()

    def add(self, g, chunk, arrived):
        own = self.r.line_own
        own[g, chunk] = (own[g, chunk].astype(F32) + arrived.astype(F32)).astype(BF16)

    def take(self, g, way, s, chunk):
        self.line_copy(g, way, s, chunk).wait_recv()
        self.add(g, chunk, self.r.line_in[g, self.slot_at(way, s, self.line)])

    def send_on(self, g, k):
        self.core_copy(g, k).wait_recv()
        self.add(g, self.chunk_at(k), self.r.core_in[g, k % 2])
        for way in range(2) if k < 3 else ():
            gone = self.distance(way)
            to = 3 - k + self.line if way == 0 else k - 3 + self.line

            @pl.when(gone <= k)
            def _():
                if k >= 1:

                    @pl.when(gone >= 1)
                    def _():
                        self.take(g, way, k - 1, to)

                self.line_copy(g, way, k, to).start()

    def tick(self, count=None):
        everything = 4 * (self.count + 1)
        for at in range(self.ticked, everything if count is None else min(self.ticked + count, everything)):
            k, g = divmod(at, self.count + 1)
            if g == 0:
                for n in range(len(self.lefts)):
                    self.left_copy(n, k).wait()
                    if k < 3:
                        self.left_copy(n, k + 1).start()
            if g < self.count:
                self.multiply(g, k)
            if g > 0:
                self.send_on(g - 1, k)
            self.ticked = at + 1

    def pace(self, counts):
        counts = iter(counts)
        return lambda: self.tick(next(counts))

    def collect(self, g):
        for way in range(2):

            @pl.when(self.distance(way) >= 1)
            def _():
                self.take(g, way, 2, self.line)

        return self.r.line_own[g, self.line]

    def settle(self):
        for g in range(self.count):
            for k in (2, 3):
                self.core_copy(g, k).wait_send()

        def one(k, carry):
            for g in range(self.count):
                for way in range(2):

                    @pl.when(self.distance(way) <= k)
                    def _():
                        self.line_copy(g, way, k, self.line).wait_send()

            return carry

        lax.fori_loop(0, 3, one, 0)


class ImageSum:
    def __init__(self, square, part, first_in, second_out, second_in, send_sem, recv_sem):
        self.square, self.part = square, part
        self.first_in, self.second_out, self.second_in = first_in, second_out, second_in
        self.send_sem, self.recv_sem = send_sem, recv_sem
        self.half = part.shape[2] // 2
        self.summing, self.spreading, self.firsts = [], [], ([], [])

    def copy_to(self, kept, source, target, slot, peer):
        copy = remote(
            source, target, self.send_sem.at[slot], self.recv_sem.at[slot], {"mp": peer}
        )
        copy.start()
        kept.append(copy)

    def columns(self, side):
        return pl.ds(side * self.half, self.half)

    def start(self):
        square = self.square
        for order in range(2):
            for side in range(2):
                owner = square.peers[side] if order else square.corner
                self.copy_to(
                    self.summing,
                    self.part.at[owner, :, self.columns(side)],
                    self.first_in.at[side, order],
                    side * 2 + order,
                    square.peers[side],
                )

    def start_side(self, side):
        square = self.square
        for order in range(2):
            owner = square.peers[side] if order else square.corner
            self.copy_to(
                self.firsts[side],
                self.part.at[owner, :, self.columns(side)],
                self.first_in.at[side, order],
                side * 2 + order,
                square.peers[side],
            )
        if side == 1:
            self.summing = [self.firsts[0][0], self.firsts[1][0], self.firsts[0][1], self.firsts[1][1]]

    def forward(self):
        square = self.square
        for side in range(2):
            self.summing[side].wait_recv()
            own = self.part[square.peers[1 - side], :, self.columns(side)]
            self.second_out[side] = (
                own.astype(F32) + self.first_in[side, 0].astype(F32)
            ).astype(BF16)
            self.copy_to(
                self.summing, self.second_out.at[side], self.second_in.at[side], 4 + side,
                square.peers[1 - side],
            )

    def arrived(self):
        for copy in self.summing[2:]:
            copy.wait_recv()

    def total(self, at):
        return jnp.concatenate(
            [
                self.part[self.square.spot, at, self.columns(side)].astype(F32)
                + self.first_in[side, 1, at, :].astype(F32)
                + self.second_in[side, at, :].astype(F32)
                for side in range(2)
            ],
            axis=1,
        )

    def sent(self):
        for copy in self.summing:
            copy.wait_send()

    def spread(self, full, owner, side, slot, peer):
        where = full.at[owner, :, self.columns(side)]
        self.copy_to(self.spreading, where, where, slot, peer)

    def gather(self, full):
        square = self.square
        for slot, side, peer in ((6, 0, 1), (7, 1, 0), (8, 0, 0), (9, 1, 1)):
            self.spread(full, square.spot, side, slot, square.peers[peer])

    def pass_on(self, full):
        square = self.square
        self.spreading[0].wait_recv()
        self.spread(full, square.above, 0, 10, square.beside)
        self.spreading[1].wait_recv()
        self.spread(full, square.beside, 1, 11, square.above)

    def gathered(self):
        for copy in self.spreading[2:]:
            copy.wait_recv()

    def spread_sent(self):
        for copy in self.spreading:
            copy.wait_send()

    @staticmethod
    def scratch(stages, like, width):
        images, _, block = like.shape[:3]
        dma = pltpu.SemaphoreType.DMA
        return dict(
            part=pltpu.VMEM((images, 4, block, width), BF16),
            first_in=pltpu.VMEM((images, 2, 2, block, width // 2), BF16),
            second_out=pltpu.VMEM((images, 2, block, width // 2), BF16),
            second_in=pltpu.VMEM((images, 2, block, width // 2), BF16),
            sum_send=dma((stages, images, 12)),
            sum_recv=dma((stages, images, 12)),
        )

    @staticmethod
    def stage(r, square, t):
        return [
            ImageSum(
                square, r.part.at[i], r.first_in.at[i], r.second_out.at[i], r.second_in.at[i],
                r.sum_send.at[t, i], r.sum_recv.at[t, i],
            )
            for i in range(r.part.shape[0])
        ]


def project(r, i, left, weight, dims=NN):
    def one(j, carry):
        at = tile_at(j)
        done = product(left, weight[at, :] if dims == NT else weight[:, at], dims)
        put_image(r.part, i, at, done.astype(BF16))
        return carry

    lax.fori_loop(0, r.part.shape[3] // TILE, one, 0)


def softmax_rows(queries, keys_in):
    scores = product(queries, keys_in, NT) * SCALE
    powers = jnp.exp(scores - jnp.max(scores, axis=-1, keepdims=True))
    return powers * (1.0 / jnp.sum(powers, axis=-1, keepdims=True))


def attend(queries, keys_in, values_in):
    probs = softmax_rows(queries, keys_in).astype(BF16)
    return product(probs, values_in).astype(BF16)


def attend_backward_head(queries, keys_in, values_in, grad):
    probs = softmax_rows(queries, keys_in)
    grad_values = product(probs.astype(BF16), grad, TN).astype(BF16)
    grad_probs = product(grad, values_in, NT)
    centred = grad_probs - jnp.sum(probs * grad_probs, axis=-1, keepdims=True)
    grad_scores = (probs * centred * SCALE).astype(BF16)
    grad_queries = product(grad_scores, keys_in).astype(BF16)
    grad_keys = product(grad_scores, queries, TN).astype(BF16)
    return grad_queries, grad_keys, grad_values


def backward_heads(heads, read, write):
    def one(h, carry):
        done = attend_backward_head(*(read(n, h) for n in range(4)))
        for n in range(3):
            write(n, h, done[n])
        return carry

    lax.fori_loop(0, heads, one, 0)


def forward_kernel(r):
    loads = r.loads
    images, heads = r.own_self.shape[0], r.self_mixed.shape[3] // HDIM
    loads.start("projected", "attention_out", "entry", "cross_query", "caption", "cross_out", "feed_grad", "feed_expand")
    stream = Stream(r.feed_shrink, r.tiles, r.tile_sem)
    stream.start()
    text = Stream(r.weight_text, r.text_tiles, r.text_sem, True)
    text.start()
    square = Square()
    place = lax.axis_index("img")
    peers = [lax.rem(place + j, 8) for j in range(1, 8)]
    greet(square.targets + [{"img": peer} for peer in peers])
    jobs = [ImageSum.stage(r, square, t) for t in range(2)]

    def caption_columns(owner):
        return r.caption.at[:, tile_at(owner, WIDE)]

    moves = [
        remote(
            caption_columns(peer), r.captions.at[place], r.move_send.at[j], r.move_recv.at[j], {"img": peer}
        )
        for j, peer in enumerate(peers)
    ]
    stay = pltpu.make_async_copy(caption_columns(place), r.captions.at[place], r.stay_sem.at[0])

    def self_stage(i):
        projected = loads.got("projected")

        def one(h, carry):
            parts = [image_rows(projected, i, tile_at(h + n * heads, HDIM)) for n in range(3)]
            put_image(r.self_mixed, i, tile_at(h, HDIM), attend(*parts))
            return carry

        lax.fori_loop(0, heads, one, 0)
        project(r, i, image_rows(r.self_mixed, i), loads.got("attention_out"))
        jobs[0][i].start()
        r.saves.save("self_mixed", i)

    def norm_stage(t, i, rows_ref, out_ref, full_ref):
        job = jobs[t][i]
        job.arrived()
        gain = r.gains[t + 1 : t + 2, :]
        for start in range(0, out_ref.shape[1], 32):
            at = slice(start, start + 32)
            wide_rows, narrow, _ = post_forward(job.total(at), (rows_ref[i, at, :],), gain)
            out_ref[i, at, :] = wide_rows
            full_ref[i, square.spot, at, :] = narrow

    def gather_stage(t, full_ref):
        for i in range(images):
            if t == 0:
                norm_stage(0, i, loads.got("entry"), r.own_self, full_ref)
            else:
                norm_stage(1, i, r.own_self, r.own_cross, full_ref)
            if i:
                jobs[t][i - 1].pass_on(full_ref.at[i - 1])
            jobs[t][i].gather(full_ref.at[i])

    def cross_stage(i):
        jobs[0][i].gathered()
        jobs[0][i].sent()
        r.saves.save("second_normed", i)
        r.saves.save("own_self", i)
        queries = product(image_rows(r.second_normed, i), loads.got("cross_query")[...]).astype(BF16)
        put_image(r.queries, i, slice(None), queries)

        def one(h, carry):
            own, value = (tile_at(h + n * heads, HDIM) for n in range(2))
            done = attend(image_rows(r.queries, i, own), r.text[i, :, own], r.text[i, :, value])
            put_image(r.cross_mixed, i, own, done)
            return carry

        lax.fori_loop(0, heads, one, 0)
        project(r, i, image_rows(r.cross_mixed, i), loads.got("cross_out"))
        jobs[1][i].start()
        r.saves.save("queries", i)
        r.saves.save("cross_mixed", i)

    def text_tile(j, weight):
        done = product(loads.got("caption")[...], weight).astype(BF16)
        r.text[:, :, tile_at(j)] = done.reshape(r.text.shape[0], -1, TILE)

    def shrink_back(j, weight):
        feed_grad = loads.got("feed_grad")
        for i in range(images):
            done = product(image_rows(feed_grad, i), weight, NT)
            put_image(r.grad_hidden, i, tile_at(j), done.astype(BF16))

    def feed_stage(i):
        jobs[1][i].gathered()
        r.saves.save("third_normed", i)
        r.saves.save("own_cross", i)
        expand = loads.got("feed_expand")

        def one(j, carry):
            at = tile_at(j)
            hidden = product(image_rows(r.third_normed, i), expand[:, at])
            spread = 0.5 + 0.5 * lax.erf(hidden * math.sqrt(0.5))
            slope = spread + hidden * jnp.exp(-0.5 * hidden * hidden) * (1.0 / math.sqrt(2.0 * math.pi))
            put_image(r.active, i, at, (hidden * spread).astype(BF16))
            grad = image_rows(r.grad_hidden, i, at).astype(F32) * slope
            put_image(r.grad_hidden, i, at, grad.astype(BF16))
            return carry

        lax.fori_loop(0, expand.shape[1] // TILE, one, 0)
        r.saves.save("active", i)
        r.saves.save("grad_hidden", i)

    first, second = jobs
    self_stage(0)
    stay.start()
    for copy in moves:
        copy.start()
    self_stage(1)
    first[0].forward()
    self_stage(2)
    first[1].forward()
    first[2].forward()
    loads.got("caption")
    text.run(0, text.count, text_tile)
    r.saves.save("text")
    loads.got("feed_grad")
    gather_stage(0, r.second_normed)
    cross_stage(0)
    first[2].pass_on(r.second_normed.at[2])
    stream.run(0, stream.count // 2, shrink_back)
    cross_stage(1)
    second[0].forward()
    cross_stage(2)
    second[1].forward()
    second[2].forward()
    stream.run(stream.count // 2, stream.count, shrink_back)
    gather_stage(1, r.third_normed)
    feed_stage(0)
    second[2].pass_on(r.third_normed.at[2])
    feed_stage(1)
    feed_stage(2)
    for job in first:
        job.spread_sent()
    for job in second:
        job.sent()
        job.spread_sent()
    stay.wait()
    for copy in moves:
        copy.wait()


def forward_rows(
    gains, projected, attention_out, entry, cross_query, weight_text, cross_out, feed_grad, feed_expand,
    feed_shrink, caption,
):
    lead = projected.shape[:3]
    width, ff, head_wide = attention_out.shape[1], feed_expand.shape[1], attention_out.shape[0]
    dma = pltpu.SemaphoreType.DMA
    tiles, tile_sem = Stream.scratch(feed_shrink)
    text_tiles, text_sem = Stream.scratch(weight_text, True)
    own = struct((lead[0], lead[2], width), F32)
    return launch(
        forward_kernel,
        1,
        vmem=dict(gains=gains),
        loaded=dict(
            projected=projected, attention_out=attention_out, entry=entry, cross_query=cross_query,
            caption=caption, cross_out=cross_out, feed_grad=feed_grad, feed_expand=feed_expand,
        ),
        hbm=dict(feed_shrink=feed_shrink, weight_text=weight_text),
        saved=dict(
            self_mixed=struct(lead + (head_wide,), BF16),
            second_normed=struct(lead + (width,), BF16),
            queries=struct(lead + (head_wide,), BF16),
            cross_mixed=struct(lead + (head_wide,), BF16),
            third_normed=struct(lead + (width,), BF16),
            active=struct(lead + (ff,), BF16),
            grad_hidden=struct(lead + (ff,), BF16),
            own_self=own,
            own_cross=own,
            text=struct((lead[0], caption.shape[0] // lead[0], weight_text.shape[1]), BF16),
        ),
        hbm_outs=dict(captions=struct((8, caption.shape[0], caption.shape[1] // 8), BF16)),
        scratch=dict(
            tiles=tiles, tile_sem=tile_sem, text_tiles=text_tiles, text_sem=text_sem, move_send=dma((7,)), move_recv=dma((7,)), stay_sem=dma((1,)),
            **ImageSum.scratch(2, projected, width),
        ),
    )


def back_norm(r, job, i, t, before, source, sum_ref, full_ref, square):
    job.arrived()
    gain = r.gains[t : t + 1, :]
    for start in range(0, r.own_grad.shape[1], 32):
        at = slice(start, start + 32)
        grad, narrow, (term,) = post_backward(job.total(at), (before(at), source[i, at, :]), gain)
        r.own_grad[i, at, :] = grad
        full_ref[i, square.spot, at, :] = narrow
        sum_ref[...] += term


def middle_kernel(r):
    loads = r.loads
    images, heads = r.own_grad.shape[0], r.grad_queries.shape[3] // HDIM
    square = Square()
    pieces = [(0, "active", c) for c in range(0, r.active.shape[3], WIDE)] + [(1, "grad_hidden", 0), (1, "grad_hidden", WIDE)]
    sums = LineSum(r, (r.feed_grad, r.third_normed), pieces)
    sums.begin()
    loads.start("grad_hidden", "active", "own_feed", "own_cross", "cross_out", "queries", "text", "cross_query")
    stream = Stream(r.feed_expand, r.tiles, r.tile_sem, passes=2)
    stream.start()
    greet(square.targets + sums.targets)
    third, second = [ImageSum.stage(r, square, t) for t in range(2)]

    def text_copy(way):
        peer = sums.twin if way == 2 else sums.place + (2 if way == 0 else -2)
        return remote(r.grad_text, r.near.at[way], r.near_send.at[way], r.near_recv.at[way], {"img": peer})

    r.third_gain[...] = jnp.zeros_like(r.third_gain)
    r.second_gain[...] = jnp.zeros_like(r.second_gain)
    grad_hidden = loads.got("grad_hidden")

    def expand_back(turn, members):
        rows = [image_rows(grad_hidden, i) for i in members]

        def one(j, weight):
            at = tile_at(lax.rem(j, stream.count))
            for i, row in zip(members, rows):
                put_image(r.part, i, at, product(row, weight, NT).astype(BF16))

        for side in range(2):
            first = turn * stream.count + side * stream.count // 2
            stream.run(first, first + stream.count // 2, one)
            for i in members:
                third[i].start_side(side)
            if turn:
                tick()

    tick = sums.pace(MIDDLE_TICKS)
    expand_back(0, range(1))
    tick()
    expand_back(1, range(1, images))
    for job in third:
        job.forward()
        tick()

    def third_stage(i):
        feed, source = loads.got("own_feed"), loads.got("own_cross")
        back_norm(
            r, third[i], i, 2, lambda at: feed[i, at, :].astype(F32), source, r.third_gain, r.cross_grad, square
        )

    def cross_stage(i):
        third[i].gathered()
        third[i].sent()
        r.saves.save("cross_grad", i)
        queries, text = loads.got("queries"), loads.got("text")
        r.mixed_grad[...] = product(
            image_rows(r.cross_grad, i), loads.got("cross_out")[...], NT
        ).astype(BF16)

        def read(n, h):
            own, value = (tile_at(h + m * heads, HDIM) for m in range(2))
            if n == 0:
                return image_rows(queries, i, own)
            return r.mixed_grad[:, own] if n == 3 else text[i, :, own if n == 1 else value]

        def write(n, h, done):
            own, value = (tile_at(h + m * heads, HDIM) for m in range(2))
            if n == 0:
                put_image(r.grad_queries, i, own, done)
            else:
                r.grad_text[i, :, own if n == 1 else value] = done

        backward_heads(heads, read, write)
        project(r, i, image_rows(r.grad_queries, i), loads.got("cross_query"), NT)
        second[i].start()
        r.saves.save("grad_queries", i)
        r.saves.save("grad_text", i)

    def second_stage(i):
        back_norm(
            r, second[i], i, 1, lambda at: r.own_grad[i, at, :], loads.targets["own_cross"], r.second_gain,
            r.self_grad, square,
        )

    for i in range(images):
        third_stage(i)
        if i:
            third[i - 1].pass_on(r.cross_grad.at[i - 1])
        third[i].gather(r.cross_grad.at[i])
        tick()
    late = pltpu.make_async_copy(r.own_self, loads.targets["own_cross"], r.late_sem.at[0])
    late.start()
    for i in range(images):
        cross_stage(i)
        tick()
        if i == 0:
            third[-1].pass_on(r.cross_grad.at[images - 1])
        else:
            second[i - 1].forward()
        if i == images - 1:
            text_copy(2).start()
            for way in range(2):

                @pl.when(sums.distance(1 - way) >= 1)
                def _():
                    text_copy(way).start()

        tick()
    second[-1].forward()
    tick()
    late.wait()
    for i in range(images):
        second_stage(i)
        r.saves.save("own_grad", i)
        if i:
            second[i - 1].pass_on(r.self_grad.at[i - 1])
        second[i].gather(r.self_grad.at[i])
        tick()
    second[-1].pass_on(r.self_grad.at[images - 1])
    sums.tick()
    for i in range(images):
        second[i].gathered()
        r.saves.save("self_grad", i)
    for g in range(sums.count):
        done = sums.collect(g)
        if g + 2 < sums.count:
            r.shrink_sum[g * WIDE : (g + 1) * WIDE, :] = done.astype(F32).T.astype(BF16)
        else:
            at = g + 2 - sums.count
            r.expand_sum[:, at * WIDE : (at + 1) * WIDE] = done
    for job in second:
        job.sent()
    for job in third + second:
        job.spread_sent()
    text_copy(2).wait()
    for way in range(2):

        @pl.when(sums.distance(1 - way) >= 1)
        def _():
            text_copy(way).wait_send()

        @pl.when(sums.distance(way) >= 1)
        def _():
            text_copy(way).wait_recv()

    sums.settle()


def middle_rows(gains, feed_grad, own_feed, rows, text, cross_out, cross_query, feed_expand):
    lead = feed_grad.shape[:3]
    width, head_wide, ff = feed_grad.shape[3], cross_out.shape[0], feed_expand.shape[1]
    share = width // 8
    tiles, tile_sem = Stream.scratch(feed_expand, depth=3)
    narrow = struct(lead + (width,), BF16)
    gain = struct((1, width), F32)
    return launch(
        middle_kernel,
        2,
        vmem=dict(gains=gains),
        loaded=dict(
            active=rows.active, grad_hidden=rows.grad_hidden, own_feed=own_feed, own_cross=rows.own_cross,
            cross_out=cross_out, queries=rows.queries, text=text, cross_query=cross_query,
        ),
        hbm=dict(own_self=rows.own_self, feed_grad=feed_grad, third_normed=rows.third_normed, feed_expand=feed_expand),
        saved=dict(
            cross_grad=narrow,
            self_grad=narrow,
            grad_queries=struct(lead + (head_wide,), BF16),
            grad_text=struct(text.shape, BF16),
            own_grad=struct((lead[0], lead[2], width), F32),
        ),
        outs=dict(
            third_gain=gain,
            second_gain=gain,
            shrink_sum=struct((ff, share), BF16),
            expand_sum=struct((share, 2 * WIDE), BF16),
        ),
        hbm_outs=dict(near=struct((3,) + text.shape, BF16)),
        scratch=dict(
            late_sem=pltpu.SemaphoreType.DMA((1,)),
            near_send=pltpu.SemaphoreType.DMA((3,)), near_recv=pltpu.SemaphoreType.DMA((3,)),
            tiles=tiles, tile_sem=tile_sem, mixed_grad=pltpu.VMEM((lead[1] * lead[2], head_wide), BF16),
            **ImageSum.scratch(2, feed_grad, width), **LineSum.scratch(ff // WIDE + 2, 2, feed_grad),
        ),
    )


def entry_kernel(r):
    loads = r.loads
    images, heads = r.own_out.shape[0], r.grad_projected.shape[3] // (3 * HDIM)
    square = Square()
    pieces = [(0, "grad_hidden", c) for c in range(0, r.loads.targets["grad_hidden"].shape[3], WIDE)]
    pieces += [(1, "grad_queries", 0), (2, "cross_mixed", 0)]
    sums = LineSum(r, (r.third_normed, r.second_normed, r.cross_grad), pieces)
    sums.begin()
    loads.start("grad_hidden", "grad_queries", "cross_mixed", "self_grad", "attention_out", "projected", "weight_in")
    loads.start("own_grad", "entry", "grad_text")
    text = Stream(r.weight_text, r.text_tiles, r.text_sem)
    text.start()
    greet(square.targets + sums.targets)
    (jobs,) = [ImageSum.stage(r, square, t) for t in range(1)]
    r.first_gain[...] = jnp.zeros_like(r.first_gain)
    r.embed_term[...] = jnp.zeros_like(r.embed_term)

    def text_at(line):
        return r.texts.at[line * 2 + sums.core]

    def behind(way, hop):
        return sums.line - (hop if way == 0 else -hop)

    def text_along(way, hop):
        source = r.near.at[way] if hop == 1 else text_at(behind(way, hop))
        return remote(
            source, text_at(behind(way, hop)), r.text_send.at[way, hop], r.text_recv.at[way, hop],
            {"img": sums.place + (2 if way == 0 else -2)},
        )

    def text_across(way, hop):
        line = behind(way, hop + 1)
        source = r.near.at[way] if hop == 0 else text_at(line)
        return remote(
            source, text_at(line), r.twin_send.at[way, hop], r.twin_recv.at[way, hop], {"img": sums.twin}
        )

    def text_here(way):
        return pltpu.make_async_copy(r.near.at[way], text_at(behind(way, 1)), r.stay_sem.at[way])

    stay = [
        pltpu.make_async_copy(r.text_own, text_at(sums.line), r.stay_sem.at[2]),
        pltpu.make_async_copy(r.near.at[2], r.texts.at[sums.twin], r.stay_sem.at[3]),
    ]

    def text_sends(way, hop):
        return (sums.distance(way) >= hop) & (sums.distance(1 - way) >= 1)

    def text_step(hop):
        for way in range(2):

            @pl.when(sums.distance(way) >= hop)
            def _():
                if hop > 1:
                    text_along(way, hop - 1).wait_recv()
                else:
                    text_here(way).start()
                text_across(way, hop - 1).start()

            if hop < 3:

                @pl.when(text_sends(way, hop))
                def _():
                    text_along(way, hop).start()

    def text_settle():
        for copy in stay:
            copy.wait()
        for way in range(2):
            for hop in range(3):
                if hop:

                    @pl.when(text_sends(way, hop))
                    def _():
                        text_along(way, hop).wait_send()

                @pl.when(sums.distance(way) >= hop + 1)
                def _():
                    if hop == 0:
                        text_here(way).wait()
                    text_across(way, hop).wait()

    def self_stage(i):
        projected = loads.got("projected")
        r.mixed_grad[...] = product(
            image_rows(loads.got("self_grad"), i), loads.got("attention_out")[...], NT
        ).astype(BF16)
        tick()

        def read(n, h):
            if n == 3:
                return r.mixed_grad[:, tile_at(h, HDIM)]
            return image_rows(projected, i, tile_at(h + n * heads, HDIM))

        def write(n, h, done):
            put_image(r.grad_projected, i, tile_at(h + n * heads, HDIM), done)

        backward_heads(heads, read, write)
        tick()
        project(r, i, image_rows(r.grad_projected, i), loads.got("weight_in"))
        jobs[i].start()
        r.saves.save("grad_projected", i)
        tick()

    def entry_stage(i):
        job = jobs[i]
        job.arrived()
        before, entry = loads.got("own_grad"), loads.got("entry")
        for start in range(0, before.shape[1], 32):
            at = slice(start, start + 32)
            wide_rows, _, terms = post_entry(
                job.total(at), (before[i, at, :], entry[i, at, :], r.mask[i, at, :]), r.gains[0:1, :]
            )
            r.own_out[i, at, :] = wide_rows
            r.first_gain[...] += terms[0]
            r.embed_term[...] += terms[1]
        r.saves.save("own_out", i)

    def caption_tile(j, weight):
        grad = loads.got("grad_text")[...]
        done = product(grad.reshape(-1, grad.shape[2]), weight, NT)
        r.caption_part[:, tile_at(j)] = done.astype(BF16)

    for copy in stay:
        copy.start()
    tick = sums.pace(ENTRY_TICKS)
    tick()
    text_step(1)
    tick()
    for i in range(images):
        self_stage(i)
        if i:
            jobs[i - 1].forward()
    text_step(2)
    tick()
    jobs[-1].forward()
    tick()
    loads.got("grad_text")
    for quarter in range(4):
        text.run(quarter * text.count // 4, (quarter + 1) * text.count // 4, caption_tile)
        tick()
    r.saves.save("caption_part")
    text_step(3)
    for i in range(images):
        entry_stage(i)
        tick()
    sums.tick()
    for g in range(sums.count - 2):
        r.expand_sum[:, g * WIDE : (g + 1) * WIDE] = sums.collect(g)
    r.query_sum[...] = sums.collect(sums.count - 2)
    r.cross_sum[...] = sums.collect(sums.count - 1).astype(F32).T.astype(BF16)
    for job in jobs:
        job.sent()
    text_settle()
    sums.settle()


def entry_rows(gains, mask, rows, back, projected, entry, attention_out, weight_in, weight_text):
    lead = projected.shape[:3]
    width = attention_out.shape[1]
    share = width // 8
    dma = pltpu.SemaphoreType.DMA
    text_tiles, text_sem = Stream.scratch(weight_text, depth=4)
    left = rows.grad_hidden.shape[3] - 2 * WIDE
    text_rows = back.grad_text.shape[0] * back.grad_text.shape[1]
    gain = struct((1, width), F32)
    return launch(
        entry_kernel,
        3,
        vmem=dict(gains=gains, mask=mask),
        loaded=dict(
            grad_hidden=(rows.grad_hidden, 2 * WIDE), self_grad=back.self_grad, attention_out=attention_out,
            projected=projected, weight_in=weight_in, own_grad=back.own_grad, entry=entry,
            grad_text=back.grad_text, grad_queries=back.grad_queries, cross_mixed=rows.cross_mixed,
        ),
        hbm=dict(
            third_normed=rows.third_normed, second_normed=rows.second_normed, cross_grad=back.cross_grad,
            weight_text=weight_text, near=back.near, text_own=back.grad_text,
        ),
        saved=dict(
            grad_projected=struct(projected.shape, BF16),
            own_out=struct(back.own_grad.shape, F32),
            caption_part=struct((text_rows, weight_text.shape[0]), BF16),
        ),
        outs=dict(
            first_gain=gain,
            embed_term=gain,
            expand_sum=struct((share, left), BF16),
            query_sum=struct((share, WIDE), BF16),
            cross_sum=struct((WIDE, share), BF16),
        ),
        hbm_outs=dict(texts=struct((8,) + back.grad_text.shape, BF16)),
        scratch=dict(
            text_tiles=text_tiles, text_sem=text_sem,
            mixed_grad=pltpu.VMEM((lead[1] * lead[2], attention_out.shape[0]), BF16),
            text_send=dma((2, 3)), text_recv=dma((2, 3)), twin_send=dma((2, 4)), twin_recv=dma((2, 4)),
            stay_sem=dma((4,)),
            **ImageSum.scratch(1, projected, width),
            **LineSum.scratch(left // WIDE + 2, 3, rows.third_normed),
        ),
    )


def line_kernel(r):
    square = Square()
    spot, beside, above, corner, peers = (
        square.spot, square.beside, square.above, square.corner, square.peers
    )
    pieces = [(0, "grad_projected", c) for c in (0, WIDE, 2 * WIDE)]
    pieces += [(1, "self_mixed", 0)]
    sums = LineSum(r, (r.first_normed, r.self_grad), pieces)
    sums.begin()
    loads = r.loads
    loads.start("grad_projected", "self_mixed", "active", "own_cross")
    shrink = Stream(r.feed_shrink, r.tiles, r.tile_sem, True)
    shrink.start()

    def text_load(j):
        slot = lax.rem(j, 2)
        return (
            pltpu.make_async_copy(r.captions.at[j], r.caption_block.at[slot], r.block_sem.at[0, slot]),
            pltpu.make_async_copy(r.texts.at[j], r.text_block.at[slot], r.block_sem.at[1, slot]),
        )

    for copy in text_load(0):
        copy.start()
    targets = [sums.targets[0]] + square.targets + sums.targets[1:] + [{"mp": corner}]
    rows, columns = r.held.shape[2], r.held.shape[3]
    greet(targets)

    low = rows // 3

    def row_block(owner, j):
        return owner * 3 + j

    def block(job, owner, side, j):
        if job == 0:
            b = row_block(owner, j)
            return r.mixed_part.at[lax.div(b, 4), lax.rem(b, 4), :, pl.ds(side * columns, columns)]
        at = pl.ds(pl.multiple_of(owner * columns, 128), columns)
        return r.caption_part.at[pl.ds(side * rows + j * low, low), at]

    thirds = [pl.ds(j * low, low) for j in range(3)]

    def load(job, slot, owner, side):
        return [
            pltpu.make_async_copy(
                block(job, owner, side, j), r.held.at[job, slot, thirds[j]], r.load_sem.at[job, slot, j]
            )
            for j in range(3)
        ]

    def first_copy(job, side, order):
        owner = corner if order == 0 else peers[side]
        slot = side * 2 + order
        return [
            remote(
                block(job, owner, side, j),
                r.flat_first.at[job, slot, thirds[j]],
                r.flat_send.at[job, slot, j],
                r.flat_recv.at[job, slot, j],
                {"mp": peers[side]},
            )
            for j in range(3)
        ]

    def second_copy(job, side):
        return remote(
            r.flat_out.at[job, side],
            r.flat_second.at[job, side],
            r.flat_send.at[job, 4 + side, 0],
            r.flat_recv.at[job, 4 + side, 0],
            {"mp": peers[1 - side]},
        )

    def flat_start(job):
        for order in range(2):
            for side in range(2):
                for copy in first_copy(job, side, order):
                    copy.start()
        for side in range(2):
            for copy in load(job, side, peers[1 - side], side) + load(job, 2 + side, spot, side):
                copy.start()

    def flat_forward(job):
        for side in range(2):
            for copy in load(job, side, peers[1 - side], side):
                copy.wait()
            for copy in first_copy(job, side, 0):
                copy.wait_recv()
            r.flat_out[job, side] = (
                r.held[job, side].astype(F32) + r.flat_first[job, side * 2].astype(F32)
            ).astype(BF16)
            second_copy(job, side).start()

    def flat_finish(job):
        for side in range(2):
            for copy in load(job, 2 + side, spot, side):
                copy.wait()
            for copy in first_copy(job, side, 1):
                copy.wait_recv()
            second_copy(job, side).wait_recv()
            total = (
                r.held[job, 2 + side].astype(F32)
                + r.flat_first[job, side * 2 + 1].astype(F32)
                + r.flat_second[job, side].astype(F32)
            )
            if job == 0:
                r.mixed_out[:, side * columns : (side + 1) * columns] = total.astype(BF16)
            else:
                r.caption_out[side * rows : (side + 1) * rows, :] = total.astype(BF16)
        for side in range(2):
            for order in range(2):
                for copy in first_copy(job, side, order):
                    copy.wait_send()
            second_copy(job, side).wait_send()

    def move(i):
        b = i * 4 + spot
        keeper, j = lax.div(b, 3), lax.rem(b, 3)
        target = r.tokens_out.at[pl.ds(pl.multiple_of(j * low, low), low)]
        away = remote(
            r.own_out.at[i], target, r.move_send.at[i], r.move_recv.at[j], {"mp": keeper}
        )
        here = pltpu.make_async_copy(r.own_out.at[i], target, r.stay_sem.at[0])
        return keeper, away, here

    def move_start():
        for i in range(3):
            keeper, away, here = move(i)

            @pl.when(keeper != spot)
            def _():
                away.start()

            @pl.when(keeper == spot)
            def _():
                here.start()

    def move_finish():
        for i in range(3):
            keeper, away, here = move(i)

            @pl.when(keeper != spot)
            def _():
                away.wait_send()

            @pl.when(keeper == spot)
            def _():
                here.wait()

        for j in range(3):
            arrival = remote(
                r.own_out.at[0], r.tokens_out.at[thirds[j]], r.move_send.at[0], r.move_recv.at[j], {"mp": corner}
            )

            @pl.when(lax.rem(row_block(spot, j), 4) != spot)
            def _():
                arrival.wait_recv()

    def mixed_tile(j, weight):
        done = product(all_rows(loads.got("active")), weight).astype(BF16)
        at = tile_at(j)
        r.mixed_part[:, :, :, at] = done.reshape(r.mixed_part.shape[:3] + (TILE,))
        for i in range(3):
            own = r.mixed_part[i, spot, :, at].astype(F32) + loads.got("own_cross")[i, :, at]
            r.mixed_part[i, spot, :, at] = own.astype(BF16)

    def text_product(j, carry):
        for copy in text_load(j):
            copy.wait()

        @pl.when(j < 7)
        def _():
            for copy in text_load(j + 1):
                copy.start()

        left = r.caption_block[lax.rem(j, 2)]

        def one(n, inner):
            at = tile_at(n)
            right = r.text_block[lax.rem(j, 2), :, :, at]
            r.text_sum[:, at] += product(left, right.reshape(-1, TILE), TN)
            return inner

        return lax.fori_loop(0, r.text_sum.shape[1] // TILE, one, carry)

    def small_step(slot, device):
        copy = remote(
            r.small_out, r.small_in.at[slot], r.small_send.at[slot], r.small_recv.at[slot], device
        )
        copy.start()
        return copy

    r.small_out[...] = r.small[...]
    r.text_sum[...] = jnp.zeros_like(r.text_sum)

    def small_add(slot, copy):
        copy.wait()
        r.small_out[...] += r.small_in[slot]

    copy = small_step(0, targets[0])
    sums.tick(2)
    small_add(0, copy)
    copy = small_step(1, targets[1])
    sums.tick(1)
    small_add(1, copy)
    copy = small_step(2, targets[2])
    flat_start(1)
    move_start()
    sums.tick(2)
    small_add(2, copy)
    wide = [small_step(3 + j, device) for j, device in enumerate(targets[3:6])]
    loads.got("active")
    loads.got("own_cross")
    shrink.run(0, shrink.count // 2, mixed_tile)
    sums.tick(2)
    shrink.run(shrink.count // 2, shrink.count, mixed_tile)
    flat_start(0)
    sums.tick(2)
    flat_forward(1)
    lax.fori_loop(0, 2, text_product, 0)
    sums.tick(2)
    lax.fori_loop(2, 4, text_product, 0)
    sums.tick(1)
    lax.fori_loop(4, 5, text_product, 0)
    sums.tick(1)
    flat_forward(0)
    lax.fori_loop(5, 6, text_product, 0)
    sums.tick(1)
    lax.fori_loop(6, 8, text_product, 0)
    sums.tick(1)
    flat_finish(1)
    sums.tick()
    move_finish()
    flat_finish(0)
    for copy in wide:
        copy.wait()
    r.small_out[...] += r.small_in[3] + r.small_in[4] + r.small_in[5]
    for g in range(3):
        r.in_sum[:, g * WIDE : (g + 1) * WIDE] = sums.collect(g)
    r.self_sum[...] = sums.collect(3).astype(F32).T.astype(BF16)
    sums.settle()


def line_sums(first_normed, rows, back, entry, small, feed_shrink):
    images, low, full = entry.own_out.shape
    height, columns = images * low, full // 2
    share = full // 8
    dma = pltpu.SemaphoreType.DMA
    block = (height, columns)
    lead = first_normed.shape[:3]
    tiles, tile_sem = Stream.scratch(feed_shrink, True, 3)
    captions, texts = rows.captions, entry.texts
    return launch(
        line_kernel,
        4,
        vmem=dict(small=small),
        loaded=dict(
            grad_projected=entry.grad_projected, self_mixed=rows.self_mixed, active=rows.active,
            own_cross=rows.own_cross,
        ),
        hbm=dict(
            first_normed=first_normed, self_grad=back.self_grad, caption_part=entry.caption_part,
            own_out=entry.own_out, feed_shrink=feed_shrink, captions=captions, texts=texts,
        ),
        outs=dict(
            in_sum=struct((share, 3 * WIDE), BF16),
            self_sum=struct((WIDE, share), BF16),
            text_sum=struct((captions.shape[2], texts.shape[3]), F32),
            small_out=struct(small.shape, F32),
            mixed_out=struct((height, full), BF16),
            caption_out=struct((entry.caption_part.shape[0], columns), BF16),
            tokens_out=struct((height, full), F32),
        ),
        scratch=dict(
            mixed_part=pltpu.VMEM(lead + (full,), BF16),
            tiles=tiles, tile_sem=tile_sem,
            caption_block=pltpu.VMEM((2,) + captions.shape[1:], BF16),
            text_block=pltpu.VMEM((2,) + texts.shape[1:], BF16),
            block_sem=dma((2, 2)),
            small_in=pltpu.VMEM((6,) + small.shape, F32),
            held=pltpu.VMEM((2, 4) + block, BF16),
            flat_first=pltpu.VMEM((2, 4) + block, BF16),
            flat_out=pltpu.VMEM((2, 2) + block, BF16),
            flat_second=pltpu.VMEM((2, 2) + block, BF16),
            small_send=dma((6,)),
            small_recv=dma((6,)),
            load_sem=dma((2, 4, 3)),
            flat_send=dma((2, 6, 3)),
            flat_recv=dma((2, 6, 3)),
            stay_sem=dma((1,)),
            move_send=dma((3,)),
            move_recv=dma((3,)),
            **LineSum.scratch(4, 2, first_normed),
        ),
    )


def plain_step(left, weight, dims, post, gain, rows_in):
    part = product(left, weight, dims).astype(BF16)
    total = lax.psum_scatter(part, "mp", scatter_dimension=0, tiled=True).astype(F32)
    wide, narrow, sums = post(total, rows_in, gain)
    if narrow is None:
        return (wide, *sums)
    return (wide, lax.all_gather(narrow, "mp", axis=0, tiled=True), *sums)


def plain_heads(array, images, parts=1):
    rows, columns = array.shape
    return array.reshape(images, rows // images, parts, -1, HDIM).transpose(2, 0, 3, 1, 4)


def plain_rows(array):
    images, heads, rows, _ = array.shape
    return array.transpose(0, 2, 1, 3).reshape(images * rows, heads * HDIM)


def per_head(function):
    return jax.vmap(jax.vmap(function))


def gelu_exact(values_in):
    return jax.nn.gelu(values_in, approximate=False)


def layer_plain(images, own_rows, gains, own_entry, own_float, first_normed, projected, feed_grad, weights):
    attention_out, cross_query, cross_out, feed_expand, feed_shrink, weight_in, weight_text, caption = weights
    queries, keys_in, values_in = plain_heads(projected, images, 3)
    text_pairs = product(caption, weight_text).astype(BF16)
    text_keys, text_values = plain_heads(text_pairs, images, 2)
    self_mixed = plain_rows(per_head(attend)(queries, keys_in, values_in))
    own_self, second_normed = plain_step(
        self_mixed, attention_out, NN, post_forward, gains[1:2], (own_entry,)
    )
    cross_queries = plain_heads(product(second_normed, cross_query).astype(BF16), images)[0]
    cross_mixed = plain_rows(per_head(attend)(cross_queries, text_keys, text_values))
    own_cross, third_normed = plain_step(
        cross_mixed, cross_out, NN, post_forward, gains[2:3], (own_self,)
    )
    hidden = product(third_normed, feed_expand)
    active = gelu_exact(hidden).astype(BF16)
    mixed_sum = lax.psum_scatter(
        product(active, feed_shrink).astype(BF16), "mp", scatter_dimension=0, tiled=True
    )
    mixed_out = (own_cross + mixed_sum.astype(F32)).astype(BF16)
    _, gelu_pull = jax.vjp(gelu_exact, hidden)
    grad_hidden = gelu_pull(product(feed_grad, feed_shrink, NT))[0].astype(BF16)
    own_grad, cross_grad, third_gain = plain_step(
        grad_hidden, feed_expand, NT, post_backward, gains[2:3],
        (own_rows(feed_grad).astype(F32), own_cross),
    )
    grad_mixed = plain_heads(product(cross_grad, cross_out, NT).astype(BF16), images)[0]
    back = per_head(attend_backward_head)(cross_queries, text_keys, text_values, grad_mixed)
    grad_queries, grad_keys, grad_values = (plain_rows(part) for part in back)
    grad_text = jnp.concatenate([grad_keys, grad_values], axis=1)
    own_grad, self_grad, second_gain = plain_step(
        grad_queries, cross_query, NT, post_backward, gains[1:2], (own_grad, own_self)
    )
    grad_mixed = plain_heads(product(self_grad, attention_out, NT).astype(BF16), images)[0]
    back = per_head(attend_backward_head)(queries, keys_in, values_in, grad_mixed)
    grad_projected = jnp.concatenate([plain_rows(part) for part in back], axis=1)
    tokens_grad, first_gain, embed_term = plain_step(
        grad_projected, weight_in, NN, post_entry, gains[0:1], (own_grad, own_entry, own_float)
    )
    caption_grad = lax.psum_scatter(
        product(grad_text, weight_text, NT).astype(BF16), "mp", scatter_dimension=1, tiled=True
    )
    small = jnp.concatenate([first_gain, second_gain, third_gain, embed_term], axis=0)
    return (
        mixed_out,
        tokens_grad,
        caption_grad,
        lax.psum_scatter(small, ("img", "mp"), scatter_dimension=1, tiled=True),
        image_sum(rows_product(first_normed, grad_projected)),
        image_sum(rows_product(self_mixed, self_grad), 1),
        image_sum(rows_product(second_normed, grad_queries)),
        image_sum(rows_product(caption, grad_text)),
        image_sum(rows_product(cross_mixed, cross_grad), 1),
        image_sum(rows_product(third_normed, grad_hidden)),
        image_sum(rows_product(active, feed_grad), 1),
    )


def layer_square(images, own_mask, gains, own_entry, first_normed, projected, feed_grad, weights):
    attention_out, cross_query, cross_out, feed_expand, feed_shrink, weight_in, weight_text, caption = weights
    width = first_normed.shape[1]
    spot = lax.axis_index("mp")

    def four(rows_in):
        return rows_in.reshape(images, 4, -1, rows_in.shape[-1])

    four_grad, four_projected, four_normed = four(feed_grad), four(projected), four(first_normed)
    own_feed = lax.dynamic_index_in_dim(four_grad, spot, 1, False)
    rows = forward_rows(
        gains, four_projected, attention_out, own_entry, cross_query, weight_text, cross_out, four_grad,
        feed_expand, feed_shrink, caption,
    )
    back = middle_rows(gains, four_grad, own_feed, rows, rows.text, cross_out, cross_query, feed_expand)
    entry = entry_rows(
        gains, own_mask, rows, back, four_projected, own_entry, attention_out, weight_in, weight_text,
    )
    terms = [entry.first_gain, back.second_gain, back.third_gain, entry.embed_term]
    small = jnp.concatenate(terms + [jnp.zeros_like(entry.embed_term)] * 4, axis=0)
    late = line_sums(four_normed, rows, back, entry, small, feed_shrink)
    slice_width = width // 32
    at = (lax.axis_index("img") * 4 + spot) * slice_width
    return (
        late.mixed_out,
        late.tokens_out,
        late.caption_out,
        lax.dynamic_slice_in_dim(late.small_out, at, slice_width, 1),
        late.in_sum,
        late.self_sum,
        entry.query_sum,
        late.text_sum,
        entry.cross_sum,
        jnp.concatenate([back.expand_sum, entry.expand_sum], axis=1),
        back.shrink_sum,
    )


def body(
    square,
    tokens,
    caption,
    masked,
    out_grad,
    mask_embed,
    norm_gains,
    attention_in,
    attention_out,
    cross_query,
    cross_text,
    cross_out,
    feed_expand,
    feed_shrink,
):
    images, length = masked.shape
    rows_all = images * length
    count = lax.axis_size("mp")
    spot = lax.axis_index("mp")
    text_width = caption.shape[1]

    def own_rows(rows_in):
        return lax.dynamic_slice_in_dim(rows_in, spot * (rows_all // count), rows_all // count, 0)

    def own_quarters(rows_in):
        parts = rows_in.reshape(images, count, length // count, -1)
        return lax.dynamic_index_in_dim(parts, spot, 1, False)

    def enter(rows_in, mask):
        return jnp.where(mask, mask_embed.astype(F32), rows_in.astype(F32))

    own = own_quarters if square else own_rows
    mask_column = masked.reshape(rows_all, 1) > 0
    own_mask = own(mask_column)
    own_float = own_mask.astype(F32)
    own_entry = enter(own(tokens), own_mask)
    first_unit, _ = norm_parts(enter(tokens, mask_column))
    first_normed = (first_unit * norm_gains[0:1]).astype(BF16)
    weight_in = attention_in.transpose(1, 2, 0).reshape(-1, tokens.shape[1])
    projected = product(first_normed, weight_in, NT).astype(BF16)
    weight_text = cross_text.reshape(text_width, -1)
    feed_grad = jnp.where(mask_column, out_grad, jnp.zeros_like(out_grad))
    weights = (
        attention_out, cross_query, cross_out, feed_expand, feed_shrink, weight_in, weight_text, caption,
    )
    if square:
        done = layer_square(
            images, own_float, norm_gains, own_entry, first_normed, projected, feed_grad, weights
        )
    else:
        done = layer_plain(
            images, own_rows, norm_gains, own_entry, own_float, first_normed, projected,
            feed_grad, weights,
        )
    mixed_out, tokens_grad, caption_grad, small_sums, self_in, *sums = done
    self_out, cross_query_sum, cross_text_sum, cross_out_sum, expand_sum, shrink_sum = (
        part.astype(F32) for part in sums
    )
    return (
        mixed_out,
        tokens_grad,
        caption_grad.astype(F32),
        small_sums[3],
        small_sums[0:3],
        self_in.astype(F32).reshape(-1, 3, attention_in.shape[2]),
        self_out,
        cross_query_sum,
        cross_text_sum.reshape(-1, 2, cross_text.shape[2]),
        cross_out_sum,
        expand_sum,
        shrink_sum,
    )


def solution(mesh):
    square = mesh.shape["mp"] == 4 and mesh.shape["img"] == 8
    return jax.shard_map(
        functools.partial(body, square),
        mesh=mesh,
        in_specs=(
            P("img", None),
            P("img", None),
            P("img", None),
            P("img", None),
            P(),
            P(),
            P(None, None, "mp"),
            P("mp", None),
            P(None, "mp"),
            P(None, None, "mp"),
            P("mp", None),
            P(None, "mp"),
            P("mp", None),
        ),
        out_specs=(
            P(("img", "mp"), None),
            P(("img", "mp"), None),
            P("img", "mp"),
            P(("img", "mp")),
            P(None, ("img", "mp")),
            P("img", None, "mp"),
            P("mp", "img"),
            P("img", "mp"),
            P("img", None, "mp"),
            P("mp", "img"),
            P("img", "mp"),
            P("mp", "img"),
        ),
        check_vma=False,
    )
```

```python
import dataclasses
import functools
import math
import types
from typing import Any

import jax
import jax.numpy as jnp
from jax import lax
from jax.experimental import pallas as pl
from jax.experimental.pallas import tpu as pltpu
from jax.sharding import PartitionSpec as P

HDIM = 128
EPSILON = 1e-05
SCALE = 1.0 / math.sqrt(HDIM)
VMEM_BYTES = 62 * 1024 * 1024
MESH = pl.DeviceIdType.MESH
BF16 = jnp.bfloat16
F32 = jnp.float32
WIDE = 512
TILE = 256

MIDDLE_TICKS = (1, 1, 1, 5, 0, 1, 0, 4, 2, 0, 2, 0, 0, 4, 1, 2, 0, 2, 1)
ENTRY_TICKS = (3, 0, 0, 0, 1, 0, 3, 4, 0, 1, 0, 2, 0, 1, 0, 0, 2, 1, 0, 1)

NN = (((1,), (0,)), ((), ()))
NT = (((1,), (1,)), ((), ()))
TN = (((0,), (0,)), ((), ()))


def product(left, right, dims=NN):
    return lax.dot_general(left, right, dims, preferred_element_type=F32)


def image_sum(part, dimension=0):
    return lax.psum_scatter(part, "img", scatter_dimension=dimension, tiled=True).astype(F32)


def rows_product(left, right):
    return product(left, right, TN).astype(BF16)


def norm_parts(rows_in):
    centre = rows_in - jnp.mean(rows_in, axis=-1, keepdims=True)
    root_inverse = lax.rsqrt(jnp.mean(centre * centre, axis=-1, keepdims=True) + EPSILON)
    return (centre * root_inverse, root_inverse)


def norm_back(grad_rows, unit_rows, root_inverse, gain_row):
    weighted = grad_rows * gain_row
    middle = jnp.mean(weighted, axis=-1, keepdims=True)
    along = jnp.mean(weighted * unit_rows, axis=-1, keepdims=True)
    return root_inverse * (weighted - middle - unit_rows * along)


def post_forward(total, rows_in, gain):
    fresh = rows_in[0] + total
    unit, _ = norm_parts(fresh)
    return fresh, (unit * gain).astype(BF16), ()


def post_backward(total, rows_in, gain):
    before, source = rows_in
    unit, root = norm_parts(source)
    grad = before + norm_back(total, unit, root, gain)
    return grad, grad.astype(BF16), (jnp.sum(total * unit, axis=0, keepdims=True),)


def post_entry(total, rows_in, gain):
    before, source, mask = rows_in
    unit, root = norm_parts(source)
    grad = before + norm_back(total, unit, root, gain)
    sums = (
        jnp.sum(total * unit, axis=0, keepdims=True),
        jnp.sum(grad * mask, axis=0, keepdims=True),
    )
    return grad * (1.0 - mask), None, sums


def remote(source, target, send, recv, device):
    return pltpu.make_async_remote_copy(
        src_ref=source,
        dst_ref=target,
        send_sem=send,
        recv_sem=recv,
        device_id=device,
        device_id_type=MESH,
    )


def greet(targets):
    barrier = pltpu.get_barrier_semaphore()
    for target in targets:
        pl.semaphore_signal(barrier, inc=1, device_id=target, device_id_type=MESH)
    pl.semaphore_wait(barrier, len(targets))


def tile_at(j, wide=TILE):
    return pl.ds(pl.multiple_of(j * wide, wide), wide)


def all_rows(ref, columns=slice(None)):
    part = ref[:, :, :, columns]
    return part.reshape(-1, part.shape[3])


def image_rows(ref, i, columns=slice(None)):
    part = ref[i, :, :, columns]
    return part.reshape(-1, part.shape[2])


def put_image(ref, i, columns, value):
    ref[i, :, :, columns] = value.reshape(ref.shape[1], ref.shape[2], value.shape[1])


class Loads:
    def __init__(self, names, sources, targets, sem):
        self.targets = dict(zip(names, targets))
        self.copies = {
            name: pltpu.make_async_copy(source, target, sem.at[i])
            for i, (name, source, target) in enumerate(zip(names, sources, targets))
        }
        self.waiting = set()

    def start(self, *names):
        for name in names:
            self.copies[name].start()
            self.waiting.add(name)

    def got(self, name):
        if name in self.waiting:
            self.waiting.remove(name)
            self.copies[name].wait()
        return self.targets[name]


class Stream:
    def __init__(self, source, tiles, sem, columns=False, passes=1):
        self.source, self.tiles, self.sem, self.columns = source, tiles, sem, columns
        self.count = source.shape[1 if columns else 0] // TILE
        self.total, self.depth = passes * self.count, tiles.shape[0]

    def copy(self, j):
        slot, at = lax.rem(j, self.depth), tile_at(lax.rem(j, self.count))
        part = self.source.at[:, at] if self.columns else self.source.at[at, :]
        return pltpu.make_async_copy(part, self.tiles.at[slot], self.sem.at[slot])

    def start(self):
        for j in range(self.depth - 1):
            self.copy(j).start()

    def run(self, first, last, use):
        def one(j, carry):
            self.copy(j).wait()
            later = j + self.depth - 1

            @pl.when(later < self.total)
            def _():
                self.copy(later).start()

            use(j, self.tiles[lax.rem(j, self.depth)])
            return carry

        lax.fori_loop(first, last, one, 0)

    @staticmethod
    def scratch(source, columns=False, depth=2):
        shape = (source.shape[0], TILE) if columns else (TILE, source.shape[1])
        return pltpu.VMEM((depth,) + shape, source.dtype), pltpu.SemaphoreType.DMA((depth,))


class Saves:
    def __init__(self, names, sources, targets, sem):
        self.refs = {n: pair for n, pair in zip(names, zip(sources, targets))}
        self.sem, self.running, self.names = sem, [], names

    def save(self, name, i=None):
        source, target = self.refs[name]
        if i is not None:
            source, target = source.at[i], target.at[i]
        copy = pltpu.make_async_copy(source, target, self.sem.at[self.names.index(name), i or 0])
        copy.start()
        self.running.append(copy)

    def finish(self):
        for copy in self.running:
            copy.wait()


def launch(kernel, ident, vmem=(), loaded=(), hbm=(), outs=(), saved=(), hbm_outs=(), scratch=()):
    vmem, loaded, hbm, outs = dict(vmem), dict(loaded), dict(hbm), dict(outs)
    starts = {n: a[1] if isinstance(a, tuple) else 0 for n, a in loaded.items()}
    loaded = {n: a[0] if isinstance(a, tuple) else a for n, a in loaded.items()}
    saved, hbm_outs, scratch = dict(saved), dict(hbm_outs), dict(scratch)
    names = [*vmem, *loaded, *hbm, *outs, *saved, *hbm_outs]
    buffers = [
        pltpu.VMEM(a.shape[:-1] + (a.shape[-1] - starts.get(n, 0),), a.dtype)
        for n, a in [*loaded.items(), *saved.items()]
    ]

    def source(ref, start):
        return ref.at[:, :, :, start:] if start else ref

    def run(*refs):
        r = types.SimpleNamespace(**dict(zip(names, refs)))
        rest = refs[len(names) :]
        rest, buffer_refs = rest[: len(scratch)], rest[len(scratch) : len(scratch) + len(buffers)]
        for name, ref in zip(scratch, rest):
            setattr(r, name, ref)
        sources = [source(getattr(r, n), starts[n]) for n in loaded]
        r.loads = Loads(list(loaded), sources, buffer_refs[: len(loaded)], refs[-2])
        kept = buffer_refs[len(loaded) :]
        r.saves = Saves(list(saved), kept, [getattr(r, n) for n in saved], refs[-1])
        for name, ref in zip(saved, kept):
            setattr(r, name, ref)
        kernel(r)
        r.saves.finish()

    in_vmem = pl.BlockSpec(memory_space=pltpu.VMEM)
    in_hbm = pl.BlockSpec(memory_space=pl.ANY)
    result = pl.pallas_call(
        run,
        out_shape=[*outs.values(), *saved.values(), *hbm_outs.values()],
        in_specs=[in_vmem] * len(vmem) + [in_hbm] * (len(loaded) + len(hbm)),
        out_specs=[in_vmem] * len(outs) + [in_hbm] * (len(saved) + len(hbm_outs)),
        scratch_shapes=[
            *scratch.values(),
            *buffers,
            pltpu.SemaphoreType.DMA((max(len(loaded), 1),)),
            pltpu.SemaphoreType.DMA((max(len(saved), 1), 3)),
        ],
        compiler_params=pltpu.CompilerParams(
            collective_id=ident, has_side_effects=True, vmem_limit_bytes=VMEM_BYTES
        ),
        cost_estimate=pl.CostEstimate(
            flops=60_000_000_000, bytes_accessed=80_000_000, transcendentals=0
        ),
    )(*vmem.values(), *loaded.values(), *hbm.values())
    return types.SimpleNamespace(**dict(zip([*outs, *saved, *hbm_outs], result)))


def struct(shape, kind):
    return jax.ShapeDtypeStruct(tuple(shape), kind)


class Square:
    def __init__(self):
        self.spot = lax.axis_index("mp")
        up, across = lax.div(self.spot, 2), lax.rem(self.spot, 2)
        self.beside = up * 2 + (1 - across)
        self.above = (1 - up) * 2 + across
        self.corner = (1 - up) * 2 + (1 - across)
        self.peers = (self.beside, self.above)
        self.targets = [{"mp": self.beside}, {"mp": self.above}]


class LineSum:
    def __init__(self, r, lefts, pieces):
        self.r, self.lefts, self.pieces = r, lefts, pieces
        self.count, self.ticked = len(pieces), 0
        self.share = r.line_own.shape[2]
        self.place = lax.axis_index("img")
        self.line, self.core = lax.div(self.place, 2), lax.rem(self.place, 2)
        self.twin = self.line * 2 + (1 - self.core)
        self.others = [lax.rem(self.line + j, 4) * 2 + self.core for j in (1, 2, 3)]
        self.targets = [{"img": self.twin}] + [{"img": o} for o in self.others]

    @staticmethod
    def scratch(count, lefts, left):
        dma = pltpu.SemaphoreType.DMA
        share = left.shape[3] // 8
        return dict(
            line_left=pltpu.VMEM((lefts, 2) + tuple(left.shape[:3]) + (2 * share,), BF16),
            line_left_sem=dma((lefts, 2)),
            core_out=pltpu.VMEM((count, 2, share, WIDE), BF16),
            core_in=pltpu.VMEM((count, 2, share, WIDE), BF16),
            line_own=pltpu.VMEM((count, 4, share, WIDE), BF16),
            line_in=pltpu.VMEM((count, 5, share, WIDE), BF16),
            core_send=dma((count, 2)),
            core_recv=dma((count, 2)),
            line_send=dma((count, 2, 3)),
            line_recv=dma((count, 2, 3)),
        )

    def left_copy(self, n, k):
        slot = k % 2
        at = tile_at(self.chunk_at(k), 2 * self.share)
        return pltpu.make_async_copy(
            self.lefts[n].at[:, :, :, at], self.r.line_left.at[n, slot], self.r.line_left_sem.at[n, slot]
        )

    def begin(self):
        for n in range(len(self.lefts)):
            self.left_copy(n, 0).start()

    def core_copy(self, g, k):
        r, slot = self.r, k % 2
        return remote(
            r.core_out.at[g, slot], r.core_in.at[g, slot], r.core_send.at[g, slot],
            r.core_recv.at[g, slot], {"img": self.twin},
        )

    def slot_at(self, way, s, line):
        first = (line < 2) if way == 0 else (line >= 2)
        return jnp.where(first, s, s + 2)

    def line_copy(self, g, way, s, chunk):
        r, ahead = self.r, 1 if way == 0 else -1
        return remote(
            r.line_own.at[g, chunk],
            r.line_in.at[g, self.slot_at(way, s, self.line + ahead)],
            r.line_send.at[g, way, s],
            r.line_recv.at[g, way, s],
            {"img": self.place + 2 * ahead},
        )

    def chunk_at(self, k):
        if k == 3:
            return self.line
        low = 3 - k - jnp.where(self.line + k == 3, 1, 0)
        high = k + jnp.where(self.line == k, 1, 0)
        return jnp.where(self.line < 2, low, high)

    def distance(self, way):
        return self.line if way == 0 else 3 - self.line

    def multiply(self, g, k):
        r = self.r
        left, name, column = self.pieces[g]
        right = r.loads.got(name) if name in r.loads.targets else getattr(r, name)
        right = all_rows(right, slice(column, column + WIDE))
        chunk = self.chunk_at(k)

        if k >= 2:
            self.core_copy(g, k).wait_send()
        for mine in (False, True):
            part = self.core if mine else 1 - self.core
            block = r.line_left[left, k % 2, :, :, :, tile_at(part, self.share)]
            done = product(block.reshape(-1, self.share), right, TN).astype(BF16)
            if mine:
                r.line_own[g, chunk] = done
            else:
                r.core_out[g, k % 2] = done
                self.core_copy(g, k).start()

    def add(self, g, chunk, arrived):
        own = self.r.line_own
        own[g, chunk] = (own[g, chunk].astype(F32) + arrived.astype(F32)).astype(BF16)

    def take(self, g, way, s, chunk):
        self.line_copy(g, way, s, chunk).wait_recv()
        self.add(g, chunk, self.r.line_in[g, self.slot_at(way, s, self.line)])

    def send_on(self, g, k):
        self.core_copy(g, k).wait_recv()
        self.add(g, self.chunk_at(k), self.r.core_in[g, k % 2])
        for way in range(2) if k < 3 else ():
            gone = self.distance(way)
            to = 3 - k + self.line if way == 0 else k - 3 + self.line

            @pl.when(gone <= k)
            def _():
                if k >= 1:

                    @pl.when(gone >= 1)
                    def _():
                        self.take(g, way, k - 1, to)

                self.line_copy(g, way, k, to).start()

    def tick(self, count=None):
        everything = 4 * (self.count + 1)
        for at in range(self.ticked, everything if count is None else min(self.ticked + count, everything)):
            k, g = divmod(at, self.count + 1)
            if g == 0:
                for n in range(len(self.lefts)):
                    self.left_copy(n, k).wait()
                    if k < 3:
                        self.left_copy(n, k + 1).start()
            if g < self.count:
                self.multiply(g, k)
            if g > 0:
                self.send_on(g - 1, k)
            self.ticked = at + 1

    def pace(self, counts):
        counts = iter(counts)
        return lambda: self.tick(next(counts))

    def collect(self, g):
        for way in range(2):

            @pl.when(self.distance(way) >= 1)
            def _():
                self.take(g, way, 2, self.line)

        return self.r.line_own[g, self.line]

    def settle(self):
        for g in range(self.count):
            for k in (2, 3):
                self.core_copy(g, k).wait_send()

        def one(k, carry):
            for g in range(self.count):
                for way in range(2):

                    @pl.when(self.distance(way) <= k)
                    def _():
                        self.line_copy(g, way, k, self.line).wait_send()

            return carry

        lax.fori_loop(0, 3, one, 0)


class ImageSum:
    def __init__(self, square, part, first_in, second_out, second_in, send_sem, recv_sem):
        self.square, self.part = square, part
        self.first_in, self.second_out, self.second_in = first_in, second_out, second_in
        self.send_sem, self.recv_sem = send_sem, recv_sem
        self.half = part.shape[2] // 2
        self.summing, self.spreading, self.firsts = [], [], ([], [])

    def copy_to(self, kept, source, target, slot, peer):
        copy = remote(
            source, target, self.send_sem.at[slot], self.recv_sem.at[slot], {"mp": peer}
        )
        copy.start()
        kept.append(copy)

    def columns(self, side):
        return pl.ds(side * self.half, self.half)

    def start(self):
        square = self.square
        for order in range(2):
            for side in range(2):
                owner = square.peers[side] if order else square.corner
                self.copy_to(
                    self.summing,
                    self.part.at[owner, :, self.columns(side)],
                    self.first_in.at[side, order],
                    side * 2 + order,
                    square.peers[side],
                )

    def start_side(self, side):
        square = self.square
        for order in range(2):
            owner = square.peers[side] if order else square.corner
            self.copy_to(
                self.firsts[side],
                self.part.at[owner, :, self.columns(side)],
                self.first_in.at[side, order],
                side * 2 + order,
                square.peers[side],
            )
        if side == 1:
            self.summing = [self.firsts[0][0], self.firsts[1][0], self.firsts[0][1], self.firsts[1][1]]

    def forward(self):
        square = self.square
        for side in range(2):
            self.summing[side].wait_recv()
            own = self.part[square.peers[1 - side], :, self.columns(side)]
            self.second_out[side] = (
                own.astype(F32) + self.first_in[side, 0].astype(F32)
            ).astype(BF16)
            self.copy_to(
                self.summing, self.second_out.at[side], self.second_in.at[side], 4 + side,
                square.peers[1 - side],
            )

    def arrived(self):
        for copy in self.summing[2:]:
            copy.wait_recv()

    def total(self, at):
        return jnp.concatenate(
            [
                self.part[self.square.spot, at, self.columns(side)].astype(F32)
                + self.first_in[side, 1, at, :].astype(F32)
                + self.second_in[side, at, :].astype(F32)
                for side in range(2)
            ],
            axis=1,
        )

    def sent(self):
        for copy in self.summing:
            copy.wait_send()

    def spread(self, full, owner, side, slot, peer):
        where = full.at[owner, :, self.columns(side)]
        self.copy_to(self.spreading, where, where, slot, peer)

    def gather(self, full):
        square = self.square
        for slot, side, peer in ((6, 0, 1), (7, 1, 0), (8, 0, 0), (9, 1, 1)):
            self.spread(full, square.spot, side, slot, square.peers[peer])

    def pass_on(self, full):
        square = self.square
        self.spreading[0].wait_recv()
        self.spread(full, square.above, 0, 10, square.beside)
        self.spreading[1].wait_recv()
        self.spread(full, square.beside, 1, 11, square.above)

    def gathered(self):
        for copy in self.spreading[2:]:
            copy.wait_recv()

    def spread_sent(self):
        for copy in self.spreading:
            copy.wait_send()

    @staticmethod
    def scratch(stages, like, width):
        images, _, block = like.shape[:3]
        dma = pltpu.SemaphoreType.DMA
        return dict(
            part=pltpu.VMEM((images, 4, block, width), BF16),
            first_in=pltpu.VMEM((images, 2, 2, block, width // 2), BF16),
            second_out=pltpu.VMEM((images, 2, block, width // 2), BF16),
            second_in=pltpu.VMEM((images, 2, block, width // 2), BF16),
            sum_send=dma((stages, images, 12)),
            sum_recv=dma((stages, images, 12)),
        )

    @staticmethod
    def stage(r, square, t):
        return [
            ImageSum(
                square, r.part.at[i], r.first_in.at[i], r.second_out.at[i], r.second_in.at[i],
                r.sum_send.at[t, i], r.sum_recv.at[t, i],
            )
            for i in range(r.part.shape[0])
        ]


def project(r, i, left, weight, dims=NN):
    def one(j, carry):
        at = tile_at(j)
        done = product(left, weight[at, :] if dims == NT else weight[:, at], dims)
        put_image(r.part, i, at, done.astype(BF16))
        return carry

    lax.fori_loop(0, r.part.shape[3] // TILE, one, 0)


def softmax_rows(queries, keys_in):
    scores = product(queries, keys_in, NT) * SCALE
    powers = jnp.exp(scores - jnp.max(scores, axis=-1, keepdims=True))
    return powers * (1.0 / jnp.sum(powers, axis=-1, keepdims=True))


def attend(queries, keys_in, values_in):
    probs = softmax_rows(queries, keys_in).astype(BF16)
    return product(probs, values_in).astype(BF16)


def attend_backward_head(queries, keys_in, values_in, grad):
    probs = softmax_rows(queries, keys_in)
    grad_values = product(probs.astype(BF16), grad, TN).astype(BF16)
    grad_probs = product(grad, values_in, NT)
    centred = grad_probs - jnp.sum(probs * grad_probs, axis=-1, keepdims=True)
    grad_scores = (probs * centred * SCALE).astype(BF16)
    grad_queries = product(grad_scores, keys_in).astype(BF16)
    grad_keys = product(grad_scores, queries, TN).astype(BF16)
    return grad_queries, grad_keys, grad_values


def backward_heads(heads, read, write):
    def one(h, carry):
        done = attend_backward_head(*(read(n, h) for n in range(4)))
        for n in range(3):
            write(n, h, done[n])
        return carry

    lax.fori_loop(0, heads, one, 0)


def forward_kernel(r):
    loads = r.loads
    images, heads = r.own_self.shape[0], r.self_mixed.shape[3] // HDIM
    loads.start("projected", "attention_out", "entry", "cross_query", "caption", "cross_out", "feed_grad", "feed_expand")
    stream = Stream(r.feed_shrink, r.tiles, r.tile_sem)
    stream.start()
    text = Stream(r.weight_text, r.text_tiles, r.text_sem, True)
    text.start()
    square = Square()
    place = lax.axis_index("img")
    peers = [lax.rem(place + j, 8) for j in range(1, 8)]
    greet(square.targets + [{"img": peer} for peer in peers])
    jobs = [ImageSum.stage(r, square, t) for t in range(2)]

    def caption_columns(owner):
        return r.caption.at[:, tile_at(owner, WIDE)]

    moves = [
        remote(
            caption_columns(peer), r.captions.at[place], r.move_send.at[j], r.move_recv.at[j], {"img": peer}
        )
        for j, peer in enumerate(peers)
    ]
    stay = pltpu.make_async_copy(caption_columns(place), r.captions.at[place], r.stay_sem.at[0])

    def self_stage(i):
        projected = loads.got("projected")

        def one(h, carry):
            parts = [image_rows(projected, i, tile_at(h + n * heads, HDIM)) for n in range(3)]
            put_image(r.self_mixed, i, tile_at(h, HDIM), attend(*parts))
            return carry

        lax.fori_loop(0, heads, one, 0)
        project(r, i, image_rows(r.self_mixed, i), loads.got("attention_out"))
        jobs[0][i].start()
        r.saves.save("self_mixed", i)

    def norm_stage(t, i, rows_ref, out_ref, full_ref):
        job = jobs[t][i]
        job.arrived()
        gain = r.gains[t + 1 : t + 2, :]
        for start in range(0, out_ref.shape[1], 32):
            at = slice(start, start + 32)
            wide_rows, narrow, _ = post_forward(job.total(at), (rows_ref[i, at, :],), gain)
            out_ref[i, at, :] = wide_rows
            full_ref[i, square.spot, at, :] = narrow

    def gather_stage(t, full_ref):
        for i in range(images):
            if t == 0:
                norm_stage(0, i, loads.got("entry"), r.own_self, full_ref)
            else:
                norm_stage(1, i, r.own_self, r.own_cross, full_ref)
            if i:
                jobs[t][i - 1].pass_on(full_ref.at[i - 1])
            jobs[t][i].gather(full_ref.at[i])

    def cross_stage(i):
        jobs[0][i].gathered()
        jobs[0][i].sent()
        r.saves.save("second_normed", i)
        r.saves.save("own_self", i)
        queries = product(image_rows(r.second_normed, i), loads.got("cross_query")[...]).astype(BF16)
        put_image(r.queries, i, slice(None), queries)

        def one(h, carry):
            own, value = (tile_at(h + n * heads, HDIM) for n in range(2))
            done = attend(image_rows(r.queries, i, own), r.text[i, :, own], r.text[i, :, value])
            put_image(r.cross_mixed, i, own, done)
            return carry

        lax.fori_loop(0, heads, one, 0)
        project(r, i, image_rows(r.cross_mixed, i), loads.got("cross_out"))
        jobs[1][i].start()
        r.saves.save("queries", i)
        r.saves.save("cross_mixed", i)

    def text_tile(j, weight):
        done = product(loads.got("caption")[...], weight).astype(BF16)
        r.text[:, :, tile_at(j)] = done.reshape(r.text.shape[0], -1, TILE)

    def shrink_back(j, weight):
        feed_grad = loads.got("feed_grad")
        for i in range(images):
            done = product(image_rows(feed_grad, i), weight, NT)
            put_image(r.grad_hidden, i, tile_at(j), done.astype(BF16))

    def feed_stage(i):
        jobs[1][i].gathered()
        r.saves.save("third_normed", i)
        r.saves.save("own_cross", i)
        expand = loads.got("feed_expand")

        def one(j, carry):
            at = tile_at(j)
            hidden = product(image_rows(r.third_normed, i), expand[:, at])
            spread = 0.5 + 0.5 * lax.erf(hidden * math.sqrt(0.5))
            slope = spread + hidden * jnp.exp(-0.5 * hidden * hidden) * (1.0 / math.sqrt(2.0 * math.pi))
            put_image(r.active, i, at, (hidden * spread).astype(BF16))
            grad = image_rows(r.grad_hidden, i, at).astype(F32) * slope
            put_image(r.grad_hidden, i, at, grad.astype(BF16))
            return carry

        lax.fori_loop(0, expand.shape[1] // TILE, one, 0)
        r.saves.save("active", i)
        r.saves.save("grad_hidden", i)

    first, second = jobs
    self_stage(0)
    stay.start()
    for copy in moves:
        copy.start()
    self_stage(1)
    first[0].forward()
    self_stage(2)
    first[1].forward()
    first[2].forward()
    loads.got("caption")
    text.run(0, text.count // 2, text_tile)
    loads.got("feed_grad")
    gather_stage(0, r.second_normed)
    text.run(text.count // 2, text.count, text_tile)
    r.saves.save("text")
    quarter = stream.count // 4
    cross_stage(0)
    first[2].pass_on(r.second_normed.at[2])
    stream.run(0, quarter, shrink_back)
    cross_stage(1)
    stream.run(quarter, 2 * quarter, shrink_back)
    second[0].forward()
    cross_stage(2)
    second[1].forward()
    stream.run(2 * quarter, 3 * quarter, shrink_back)
    second[2].forward()
    stream.run(3 * quarter, stream.count, shrink_back)
    gather_stage(1, r.third_normed)
    feed_stage(0)
    second[2].pass_on(r.third_normed.at[2])
    feed_stage(1)
    feed_stage(2)
    for job in first:
        job.spread_sent()
    for job in second:
        job.sent()
        job.spread_sent()
    stay.wait()
    for copy in moves:
        copy.wait()


def forward_rows(
    gains, projected, attention_out, entry, cross_query, weight_text, cross_out, feed_grad, feed_expand,
    feed_shrink, caption,
):
    lead = projected.shape[:3]
    width, ff, head_wide = attention_out.shape[1], feed_expand.shape[1], attention_out.shape[0]
    dma = pltpu.SemaphoreType.DMA
    tiles, tile_sem = Stream.scratch(feed_shrink)
    text_tiles, text_sem = Stream.scratch(weight_text, True)
    own = struct((lead[0], lead[2], width), F32)
    return launch(
        forward_kernel,
        1,
        vmem=dict(gains=gains),
        loaded=dict(
            projected=projected, attention_out=attention_out, entry=entry, cross_query=cross_query,
            caption=caption, cross_out=cross_out, feed_grad=feed_grad, feed_expand=feed_expand,
        ),
        hbm=dict(feed_shrink=feed_shrink, weight_text=weight_text),
        saved=dict(
            self_mixed=struct(lead + (head_wide,), BF16),
            second_normed=struct(lead + (width,), BF16),
            queries=struct(lead + (head_wide,), BF16),
            cross_mixed=struct(lead + (head_wide,), BF16),
            third_normed=struct(lead + (width,), BF16),
            active=struct(lead + (ff,), BF16),
            grad_hidden=struct(lead + (ff,), BF16),
            own_self=own,
            own_cross=own,
            text=struct((lead[0], caption.shape[0] // lead[0], weight_text.shape[1]), BF16),
        ),
        hbm_outs=dict(captions=struct((8, caption.shape[0], caption.shape[1] // 8), BF16)),
        scratch=dict(
            tiles=tiles, tile_sem=tile_sem, text_tiles=text_tiles, text_sem=text_sem, move_send=dma((7,)), move_recv=dma((7,)), stay_sem=dma((1,)),
            **ImageSum.scratch(2, projected, width),
        ),
    )


def back_norm(r, job, i, t, before, source, sum_ref, full_ref, square):
    job.arrived()
    gain = r.gains[t : t + 1, :]
    for start in range(0, r.own_grad.shape[1], 32):
        at = slice(start, start + 32)
        grad, narrow, (term,) = post_backward(job.total(at), (before(at), source[i, at, :]), gain)
        r.own_grad[i, at, :] = grad
        full_ref[i, square.spot, at, :] = narrow
        sum_ref[...] += term


def middle_kernel(r):
    loads = r.loads
    images, heads = r.own_grad.shape[0], r.grad_queries.shape[3] // HDIM
    square = Square()
    pieces = [(0, "active", c) for c in range(0, r.active.shape[3], WIDE)] + [(1, "grad_hidden", 0), (1, "grad_hidden", WIDE)]
    sums = LineSum(r, (r.feed_grad, r.third_normed), pieces)
    sums.begin()
    own_feed = pltpu.make_async_copy(r.feed_grad.at[:, square.spot], r.own_feed, r.late_sem.at[1])
    own_feed.start()
    loads.start("grad_hidden", "active", "own_cross", "cross_out", "queries", "text", "cross_query")
    stream = Stream(r.feed_expand, r.tiles, r.tile_sem, passes=2)
    stream.start()
    greet(square.targets + sums.targets)
    third, second = [ImageSum.stage(r, square, t) for t in range(2)]

    def text_copy(way):
        peer = sums.twin if way == 2 else sums.place + (2 if way == 0 else -2)
        return remote(r.grad_text, r.near.at[way], r.near_send.at[way], r.near_recv.at[way], {"img": peer})

    r.third_gain[...] = jnp.zeros_like(r.third_gain)
    r.second_gain[...] = jnp.zeros_like(r.second_gain)
    grad_hidden = loads.got("grad_hidden")

    def expand_back(turn, members):
        rows = [image_rows(grad_hidden, i) for i in members]

        def one(j, weight):
            at = tile_at(lax.rem(j, stream.count))
            for i, row in zip(members, rows):
                put_image(r.part, i, at, product(row, weight, NT).astype(BF16))

        for side in range(2):
            first = turn * stream.count + side * stream.count // 2
            stream.run(first, first + stream.count // 2, one)
            for i in members:
                third[i].start_side(side)
            if turn:
                tick()

    tick = sums.pace(MIDDLE_TICKS)
    expand_back(0, range(1))
    tick()
    expand_back(1, range(1, images))
    for job in third:
        job.forward()
        tick()

    def third_stage(i):
        source = loads.got("own_cross")
        back_norm(
            r, third[i], i, 2, lambda at: r.own_feed[i, at, :].astype(F32), source, r.third_gain, r.cross_grad, square
        )

    def cross_stage(i):
        third[i].gathered()
        third[i].sent()
        r.saves.save("cross_grad", i)
        queries, text = loads.got("queries"), loads.got("text")
        r.mixed_grad[...] = product(
            image_rows(r.cross_grad, i), loads.got("cross_out")[...], NT
        ).astype(BF16)

        def read(n, h):
            own, value = (tile_at(h + m * heads, HDIM) for m in range(2))
            if n == 0:
                return image_rows(queries, i, own)
            return r.mixed_grad[:, own] if n == 3 else text[i, :, own if n == 1 else value]

        def write(n, h, done):
            own, value = (tile_at(h + m * heads, HDIM) for m in range(2))
            if n == 0:
                put_image(r.grad_queries, i, own, done)
            else:
                r.grad_text[i, :, own if n == 1 else value] = done

        backward_heads(heads, read, write)
        project(r, i, image_rows(r.grad_queries, i), loads.got("cross_query"), NT)
        second[i].start()
        r.saves.save("grad_queries", i)
        r.saves.save("grad_text", i)

    def second_stage(i):
        back_norm(
            r, second[i], i, 1, lambda at: r.own_grad[i, at, :], loads.targets["own_cross"], r.second_gain,
            r.self_grad, square,
        )

    own_feed.wait()
    for i in range(images):
        third_stage(i)
        if i:
            third[i - 1].pass_on(r.cross_grad.at[i - 1])
        third[i].gather(r.cross_grad.at[i])
        tick()
    late = pltpu.make_async_copy(r.own_self, loads.targets["own_cross"], r.late_sem.at[0])
    late.start()
    for i in range(images):
        cross_stage(i)
        tick()
        if i == 0:
            third[-1].pass_on(r.cross_grad.at[images - 1])
        else:
            second[i - 1].forward()
        if i == images - 1:
            text_copy(2).start()
            for way in range(2):

                @pl.when(sums.distance(1 - way) >= 1)
                def _():
                    text_copy(way).start()

        tick()
    second[-1].forward()
    tick()
    late.wait()
    for i in range(images):
        second_stage(i)
        r.saves.save("own_grad", i)
        if i:
            second[i - 1].pass_on(r.self_grad.at[i - 1])
        second[i].gather(r.self_grad.at[i])
        tick()
    second[-1].pass_on(r.self_grad.at[images - 1])
    sums.tick()
    for i in range(images):
        second[i].gathered()
        r.saves.save("self_grad", i)
    for g in range(sums.count):
        done = sums.collect(g)
        if g + 2 < sums.count:
            r.shrink_sum[g * WIDE : (g + 1) * WIDE, :] = done.astype(F32).T.astype(BF16)
        else:
            at = g + 2 - sums.count
            r.expand_sum[:, at * WIDE : (at + 1) * WIDE] = done
    for job in second:
        job.sent()
    for job in third + second:
        job.spread_sent()
    text_copy(2).wait()
    for way in range(2):

        @pl.when(sums.distance(1 - way) >= 1)
        def _():
            text_copy(way).wait_send()

        @pl.when(sums.distance(way) >= 1)
        def _():
            text_copy(way).wait_recv()

    sums.settle()


def middle_rows(gains, feed_grad, rows, text, cross_out, cross_query, feed_expand):
    lead = feed_grad.shape[:3]
    width, head_wide, ff = feed_grad.shape[3], cross_out.shape[0], feed_expand.shape[1]
    share = width // 8
    tiles, tile_sem = Stream.scratch(feed_expand, depth=3)
    narrow = struct(lead + (width,), BF16)
    gain = struct((1, width), F32)
    return launch(
        middle_kernel,
        2,
        vmem=dict(gains=gains),
        loaded=dict(
            active=rows.active, grad_hidden=rows.grad_hidden, own_cross=rows.own_cross,
            cross_out=cross_out, queries=rows.queries, text=text, cross_query=cross_query,
        ),
        hbm=dict(own_self=rows.own_self, feed_grad=feed_grad, third_normed=rows.third_normed, feed_expand=feed_expand),
        saved=dict(
            cross_grad=narrow,
            self_grad=narrow,
            grad_queries=struct(lead + (head_wide,), BF16),
            grad_text=struct(text.shape, BF16),
            own_grad=struct((lead[0], lead[2], width), F32),
        ),
        outs=dict(
            third_gain=gain,
            second_gain=gain,
            shrink_sum=struct((ff, share), BF16),
            expand_sum=struct((share, 2 * WIDE), BF16),
        ),
        hbm_outs=dict(near=struct((3,) + text.shape, BF16)),
        scratch=dict(
            late_sem=pltpu.SemaphoreType.DMA((2,)), own_feed=pltpu.VMEM((lead[0], lead[2], width), BF16),
            near_send=pltpu.SemaphoreType.DMA((3,)), near_recv=pltpu.SemaphoreType.DMA((3,)),
            tiles=tiles, tile_sem=tile_sem, mixed_grad=pltpu.VMEM((lead[1] * lead[2], head_wide), BF16),
            **ImageSum.scratch(2, feed_grad, width), **LineSum.scratch(ff // WIDE + 2, 2, feed_grad),
        ),
    )


def entry_kernel(r):
    loads = r.loads
    images, heads = r.own_out.shape[0], r.grad_projected.shape[3] // (3 * HDIM)
    square = Square()
    pieces = [(0, "grad_hidden", c) for c in range(0, r.loads.targets["grad_hidden"].shape[3], WIDE)]
    pieces += [(1, "grad_queries", 0), (2, "cross_mixed", 0)]
    sums = LineSum(r, (r.third_normed, r.second_normed, r.cross_grad), pieces)
    sums.begin()
    loads.start("grad_hidden", "grad_queries", "cross_mixed", "self_grad", "attention_out", "projected", "weight_in")
    loads.start("own_grad", "entry", "grad_text")
    text = Stream(r.weight_text, r.text_tiles, r.text_sem)
    text.start()
    greet(square.targets + sums.targets)
    (jobs,) = [ImageSum.stage(r, square, t) for t in range(1)]
    r.first_gain[...] = jnp.zeros_like(r.first_gain)
    r.embed_term[...] = jnp.zeros_like(r.embed_term)

    def text_at(line):
        return r.texts.at[line * 2 + sums.core]

    def behind(way, hop):
        return sums.line - (hop if way == 0 else -hop)

    def text_along(way, hop):
        source = r.near.at[way] if hop == 1 else text_at(behind(way, hop))
        return remote(
            source, text_at(behind(way, hop)), r.text_send.at[way, hop], r.text_recv.at[way, hop],
            {"img": sums.place + (2 if way == 0 else -2)},
        )

    def text_across(way, hop):
        line = behind(way, hop + 1)
        source = r.near.at[way] if hop == 0 else text_at(line)
        return remote(
            source, text_at(line), r.twin_send.at[way, hop], r.twin_recv.at[way, hop], {"img": sums.twin}
        )

    def text_in(way):
        return pltpu.make_async_copy(r.near.at[way], r.bounce.at[way], r.in_sem.at[way])

    def text_out(way):
        target = r.texts.at[sums.twin] if way == 2 else text_at(behind(way, 1))
        return pltpu.make_async_copy(r.bounce.at[way], target, r.stay_sem.at[way])

    def text_own():
        return pltpu.make_async_copy(loads.targets["grad_text"], text_at(sums.line), r.stay_sem.at[3])

    def text_sends(way, hop):
        return (sums.distance(way) >= hop) & (sums.distance(1 - way) >= 1)

    def text_step(hop):
        for way in range(2):

            @pl.when(sums.distance(way) >= hop)
            def _():
                if hop > 1:
                    text_along(way, hop - 1).wait_recv()
                else:
                    text_in(way).start()
                text_across(way, hop - 1).start()

            if hop < 3:

                @pl.when(text_sends(way, hop))
                def _():
                    text_along(way, hop).start()

    def text_settle():
        text_out(2).wait()
        text_own().wait()
        for way in range(2):
            for hop in range(3):
                if hop:

                    @pl.when(text_sends(way, hop))
                    def _():
                        text_along(way, hop).wait_send()

                @pl.when(sums.distance(way) >= hop + 1)
                def _():
                    if hop == 0:
                        text_out(way).wait()
                    text_across(way, hop).wait()

    def self_stage(i):
        projected = loads.got("projected")
        r.mixed_grad[...] = product(
            image_rows(loads.got("self_grad"), i), loads.got("attention_out")[...], NT
        ).astype(BF16)
        tick()

        def read(n, h):
            if n == 3:
                return r.mixed_grad[:, tile_at(h, HDIM)]
            return image_rows(projected, i, tile_at(h + n * heads, HDIM))

        def write(n, h, done):
            put_image(r.grad_projected, i, tile_at(h + n * heads, HDIM), done)

        backward_heads(heads, read, write)
        tick()
        project(r, i, image_rows(r.grad_projected, i), loads.got("weight_in"))
        jobs[i].start()
        r.saves.save("grad_projected", i)
        tick()

    def entry_stage(i):
        job = jobs[i]
        job.arrived()
        before, entry = loads.got("own_grad"), loads.got("entry")
        for start in range(0, before.shape[1], 32):
            at = slice(start, start + 32)
            wide_rows, _, terms = post_entry(
                job.total(at), (before[i, at, :], entry[i, at, :], r.mask[i, at, :]), r.gains[0:1, :]
            )
            r.own_out[i, at, :] = wide_rows
            r.first_gain[...] += terms[0]
            r.embed_term[...] += terms[1]
        r.saves.save("own_out", i)

    def caption_tile(j, weight):
        grad = loads.got("grad_text")[...]
        done = product(grad.reshape(-1, grad.shape[2]), weight, NT)
        r.caption_part[:, tile_at(j)] = done.astype(BF16)

    text_in(2).start()
    tick = sums.pace(ENTRY_TICKS)
    text_step(1)
    tick()
    tick()
    for i in range(images):
        self_stage(i)
        if i:
            jobs[i - 1].forward()
        if i == 0:
            text_in(2).wait()
            text_out(2).start()
            for way in range(2):

                @pl.when(sums.distance(way) >= 1)
                def _():
                    text_in(way).wait()
                    text_out(way).start()

        if i == 1:
            text_step(2)
    tick()
    jobs[-1].forward()
    tick()
    loads.got("grad_text")
    text_own().start()
    for quarter in range(4):
        text.run(quarter * text.count // 4, (quarter + 1) * text.count // 4, caption_tile)
        tick()
        if quarter == 1:
            text_step(3)
    r.saves.save("caption_part")
    for i in range(images):
        entry_stage(i)
        tick()
    sums.tick()
    for g in range(sums.count - 2):
        r.expand_sum[:, g * WIDE : (g + 1) * WIDE] = sums.collect(g)
    r.query_sum[...] = sums.collect(sums.count - 2)
    r.cross_sum[...] = sums.collect(sums.count - 1).astype(F32).T.astype(BF16)
    for job in jobs:
        job.sent()
    text_settle()
    sums.settle()


def entry_rows(gains, mask, rows, back, projected, entry, attention_out, weight_in, weight_text):
    lead = projected.shape[:3]
    width = attention_out.shape[1]
    share = width // 8
    dma = pltpu.SemaphoreType.DMA
    text_tiles, text_sem = Stream.scratch(weight_text, depth=4)
    left = rows.grad_hidden.shape[3] - 2 * WIDE
    text_rows = back.grad_text.shape[0] * back.grad_text.shape[1]
    gain = struct((1, width), F32)
    return launch(
        entry_kernel,
        3,
        vmem=dict(gains=gains, mask=mask),
        loaded=dict(
            grad_hidden=(rows.grad_hidden, 2 * WIDE), self_grad=back.self_grad, attention_out=attention_out,
            projected=projected, weight_in=weight_in, own_grad=back.own_grad, entry=entry,
            grad_text=back.grad_text, grad_queries=back.grad_queries, cross_mixed=rows.cross_mixed,
        ),
        hbm=dict(
            third_normed=rows.third_normed, second_normed=rows.second_normed, cross_grad=back.cross_grad,
            weight_text=weight_text, near=back.near,
        ),
        saved=dict(
            grad_projected=struct(projected.shape, BF16),
            own_out=struct(back.own_grad.shape, F32),
            caption_part=struct((text_rows, weight_text.shape[0]), BF16),
        ),
        outs=dict(
            first_gain=gain,
            embed_term=gain,
            expand_sum=struct((share, left), BF16),
            query_sum=struct((share, WIDE), BF16),
            cross_sum=struct((WIDE, share), BF16),
        ),
        hbm_outs=dict(texts=struct((8,) + back.grad_text.shape, BF16)),
        scratch=dict(
            text_tiles=text_tiles, text_sem=text_sem,
            mixed_grad=pltpu.VMEM((lead[1] * lead[2], attention_out.shape[0]), BF16),
            text_send=dma((2, 3)), text_recv=dma((2, 3)), twin_send=dma((2, 4)), twin_recv=dma((2, 4)),
            stay_sem=dma((4,)), in_sem=dma((3,)), bounce=pltpu.VMEM(back.near.shape, BF16),
            **ImageSum.scratch(1, projected, width),
            **LineSum.scratch(left // WIDE + 2, 3, rows.third_normed),
        ),
    )


def line_kernel(r):
    square = Square()
    spot, beside, above, corner, peers = (
        square.spot, square.beside, square.above, square.corner, square.peers
    )
    pieces = [(0, "grad_projected", c) for c in (0, WIDE, 2 * WIDE)]
    pieces += [(1, "self_mixed", 0)]
    sums = LineSum(r, (r.first_normed, r.self_grad), pieces)
    sums.begin()
    loads = r.loads
    loads.start("grad_projected", "self_mixed", "active", "own_cross")
    shrink = Stream(r.feed_shrink, r.tiles, r.tile_sem, True)
    shrink.start()

    def text_load(j):
        slot = lax.rem(j, 2)
        return (
            pltpu.make_async_copy(r.captions.at[j], r.caption_block.at[slot], r.block_sem.at[0, slot]),
            pltpu.make_async_copy(r.texts.at[j], r.text_block.at[slot], r.block_sem.at[1, slot]),
        )

    for copy in text_load(0):
        copy.start()
    targets = [sums.targets[0]] + square.targets + sums.targets[1:] + [{"mp": corner}]
    rows, columns = r.held.shape[2], r.held.shape[3]
    greet(targets)

    low = rows // 3

    def row_block(owner, j):
        return owner * 3 + j

    def block(job, owner, side, j):
        if job == 0:
            b = row_block(owner, j)
            return r.mixed_part.at[lax.div(b, 4), lax.rem(b, 4), :, pl.ds(side * columns, columns)]
        at = pl.ds(pl.multiple_of(owner * columns, 128), columns)
        return r.caption_part.at[pl.ds(side * rows + j * low, low), at]

    thirds = [pl.ds(j * low, low) for j in range(3)]

    def load(job, slot, owner, side):
        return [
            pltpu.make_async_copy(
                block(job, owner, side, j), r.held.at[job, slot, thirds[j]], r.load_sem.at[job, slot, j]
            )
            for j in range(3)
        ]

    def first_copy(job, side, order):
        owner = corner if order == 0 else peers[side]
        slot = side * 2 + order
        return [
            remote(
                block(job, owner, side, j),
                r.flat_first.at[job, slot, thirds[j]],
                r.flat_send.at[job, slot, j],
                r.flat_recv.at[job, slot, j],
                {"mp": peers[side]},
            )
            for j in range(3)
        ]

    def second_copy(job, side):
        return remote(
            r.flat_out.at[job, side],
            r.flat_second.at[job, side],
            r.flat_send.at[job, 4 + side, 0],
            r.flat_recv.at[job, 4 + side, 0],
            {"mp": peers[1 - side]},
        )

    def flat_start(job):
        for order in range(2):
            for side in range(2):
                for copy in first_copy(job, side, order):
                    copy.start()
        for side in range(2):
            for copy in load(job, side, peers[1 - side], side) + load(job, 2 + side, spot, side):
                copy.start()

    def flat_forward(job):
        for side in range(2):
            for copy in load(job, side, peers[1 - side], side):
                copy.wait()
            for copy in first_copy(job, side, 0):
                copy.wait_recv()
            r.flat_out[job, side] = (
                r.held[job, side].astype(F32) + r.flat_first[job, side * 2].astype(F32)
            ).astype(BF16)
            second_copy(job, side).start()

    def flat_finish(job):
        for side in range(2):
            for copy in load(job, 2 + side, spot, side):
                copy.wait()
            for copy in first_copy(job, side, 1):
                copy.wait_recv()
            second_copy(job, side).wait_recv()
            total = (
                r.held[job, 2 + side].astype(F32)
                + r.flat_first[job, side * 2 + 1].astype(F32)
                + r.flat_second[job, side].astype(F32)
            )
            if job == 0:
                r.mixed_out[:, side * columns : (side + 1) * columns] = total.astype(BF16)
            else:
                r.caption_out[side * rows : (side + 1) * rows, :] = total.astype(BF16)
        for side in range(2):
            for order in range(2):
                for copy in first_copy(job, side, order):
                    copy.wait_send()
            second_copy(job, side).wait_send()

    def move(i):
        b = i * 4 + spot
        keeper, j = lax.div(b, 3), lax.rem(b, 3)
        target = r.tokens_out.at[pl.ds(pl.multiple_of(j * low, low), low)]
        away = remote(
            r.own_out.at[i], target, r.move_send.at[i], r.move_recv.at[j], {"mp": keeper}
        )
        here = pltpu.make_async_copy(r.own_out.at[i], target, r.stay_sem.at[0])
        return keeper, away, here

    def move_start():
        for i in range(3):
            keeper, away, here = move(i)

            @pl.when(keeper != spot)
            def _():
                away.start()

            @pl.when(keeper == spot)
            def _():
                here.start()

    def move_finish():
        for i in range(3):
            keeper, away, here = move(i)

            @pl.when(keeper != spot)
            def _():
                away.wait_send()

            @pl.when(keeper == spot)
            def _():
                here.wait()

        for j in range(3):
            arrival = remote(
                r.own_out.at[0], r.tokens_out.at[thirds[j]], r.move_send.at[0], r.move_recv.at[j], {"mp": corner}
            )

            @pl.when(lax.rem(row_block(spot, j), 4) != spot)
            def _():
                arrival.wait_recv()

    def mixed_tile(j, weight):
        done = product(all_rows(loads.got("active")), weight).astype(BF16)
        at = tile_at(j)
        r.mixed_part[:, :, :, at] = done.reshape(r.mixed_part.shape[:3] + (TILE,))
        for i in range(3):
            own = r.mixed_part[i, spot, :, at].astype(F32) + loads.got("own_cross")[i, :, at]
            r.mixed_part[i, spot, :, at] = own.astype(BF16)

    def text_product(j, carry):
        for copy in text_load(j):
            copy.wait()

        @pl.when(j < 7)
        def _():
            for copy in text_load(j + 1):
                copy.start()

        left = r.caption_block[lax.rem(j, 2)]

        def one(n, inner):
            at = tile_at(n)
            right = r.text_block[lax.rem(j, 2), :, :, at]
            r.text_sum[:, at] += product(left, right.reshape(-1, TILE), TN)
            return inner

        return lax.fori_loop(0, r.text_sum.shape[1] // TILE, one, carry)

    def small_step(slot, device):
        copy = remote(
            r.small_out, r.small_in.at[slot], r.small_send.at[slot], r.small_recv.at[slot], device
        )
        copy.start()
        return copy

    r.small_out[...] = r.small[...]
    r.text_sum[...] = jnp.zeros_like(r.text_sum)

    def small_add(slot, copy):
        copy.wait()
        r.small_out[...] += r.small_in[slot]

    copy = small_step(0, targets[0])
    sums.tick(2)
    small_add(0, copy)
    copy = small_step(1, targets[1])
    sums.tick(1)
    small_add(1, copy)
    copy = small_step(2, targets[2])
    flat_start(1)
    move_start()
    sums.tick(2)
    small_add(2, copy)
    wide = [small_step(3 + j, device) for j, device in enumerate(targets[3:6])]
    loads.got("active")
    loads.got("own_cross")
    shrink.run(0, shrink.count // 2, mixed_tile)
    sums.tick(2)
    shrink.run(shrink.count // 2, shrink.count, mixed_tile)
    flat_start(0)
    sums.tick(2)
    flat_forward(1)
    lax.fori_loop(0, 2, text_product, 0)
    sums.tick(2)
    lax.fori_loop(2, 4, text_product, 0)
    sums.tick(1)
    lax.fori_loop(4, 5, text_product, 0)
    sums.tick(1)
    flat_forward(0)
    lax.fori_loop(5, 6, text_product, 0)
    sums.tick(1)
    lax.fori_loop(6, 8, text_product, 0)
    sums.tick(1)
    flat_finish(1)
    sums.tick()
    move_finish()
    flat_finish(0)
    for copy in wide:
        copy.wait()
    r.small_out[...] += r.small_in[3] + r.small_in[4] + r.small_in[5]
    for g in range(3):
        r.in_sum[:, g * WIDE : (g + 1) * WIDE] = sums.collect(g)
    r.self_sum[...] = sums.collect(3).astype(F32).T.astype(BF16)
    sums.settle()


def line_sums(first_normed, rows, back, entry, small, feed_shrink):
    images, low, full = entry.own_out.shape
    height, columns = images * low, full // 2
    share = full // 8
    dma = pltpu.SemaphoreType.DMA
    block = (height, columns)
    lead = first_normed.shape[:3]
    tiles, tile_sem = Stream.scratch(feed_shrink, True, 3)
    captions, texts = rows.captions, entry.texts
    return launch(
        line_kernel,
        4,
        vmem=dict(small=small),
        loaded=dict(
            grad_projected=entry.grad_projected, self_mixed=rows.self_mixed, active=rows.active,
            own_cross=rows.own_cross,
        ),
        hbm=dict(
            first_normed=first_normed, self_grad=back.self_grad, caption_part=entry.caption_part,
            own_out=entry.own_out, feed_shrink=feed_shrink, captions=captions, texts=texts,
        ),
        outs=dict(
            in_sum=struct((share, 3 * WIDE), BF16),
            self_sum=struct((WIDE, share), BF16),
            text_sum=struct((captions.shape[2], texts.shape[3]), F32),
            small_out=struct(small.shape, F32),
            mixed_out=struct((height, full), BF16),
            caption_out=struct((entry.caption_part.shape[0], columns), BF16),
            tokens_out=struct((height, full), F32),
        ),
        scratch=dict(
            mixed_part=pltpu.VMEM(lead + (full,), BF16),
            tiles=tiles, tile_sem=tile_sem,
            caption_block=pltpu.VMEM((2,) + captions.shape[1:], BF16),
            text_block=pltpu.VMEM((2,) + texts.shape[1:], BF16),
            block_sem=dma((2, 2)),
            small_in=pltpu.VMEM((6,) + small.shape, F32),
            held=pltpu.VMEM((2, 4) + block, BF16),
            flat_first=pltpu.VMEM((2, 4) + block, BF16),
            flat_out=pltpu.VMEM((2, 2) + block, BF16),
            flat_second=pltpu.VMEM((2, 2) + block, BF16),
            small_send=dma((6,)),
            small_recv=dma((6,)),
            load_sem=dma((2, 4, 3)),
            flat_send=dma((2, 6, 3)),
            flat_recv=dma((2, 6, 3)),
            stay_sem=dma((1,)),
            move_send=dma((3,)),
            move_recv=dma((3,)),
            **LineSum.scratch(4, 2, first_normed),
        ),
    )


def plain_step(left, weight, dims, post, gain, rows_in):
    part = product(left, weight, dims).astype(BF16)
    total = lax.psum_scatter(part, "mp", scatter_dimension=0, tiled=True).astype(F32)
    wide, narrow, sums = post(total, rows_in, gain)
    if narrow is None:
        return (wide, *sums)
    return (wide, lax.all_gather(narrow, "mp", axis=0, tiled=True), *sums)


def plain_heads(array, images, parts=1):
    rows, columns = array.shape
    return array.reshape(images, rows // images, parts, -1, HDIM).transpose(2, 0, 3, 1, 4)


def plain_rows(array):
    images, heads, rows, _ = array.shape
    return array.transpose(0, 2, 1, 3).reshape(images * rows, heads * HDIM)


def per_head(function):
    return jax.vmap(jax.vmap(function))


def gelu_exact(values_in):
    return jax.nn.gelu(values_in, approximate=False)


def layer_plain(images, own_rows, gains, own_entry, own_float, first_normed, projected, feed_grad, weights):
    attention_out, cross_query, cross_out, feed_expand, feed_shrink, weight_in, weight_text, caption = weights
    queries, keys_in, values_in = plain_heads(projected, images, 3)
    text_pairs = product(caption, weight_text).astype(BF16)
    text_keys, text_values = plain_heads(text_pairs, images, 2)
    self_mixed = plain_rows(per_head(attend)(queries, keys_in, values_in))
    own_self, second_normed = plain_step(
        self_mixed, attention_out, NN, post_forward, gains[1:2], (own_entry,)
    )
    cross_queries = plain_heads(product(second_normed, cross_query).astype(BF16), images)[0]
    cross_mixed = plain_rows(per_head(attend)(cross_queries, text_keys, text_values))
    own_cross, third_normed = plain_step(
        cross_mixed, cross_out, NN, post_forward, gains[2:3], (own_self,)
    )
    hidden = product(third_normed, feed_expand)
    active = gelu_exact(hidden).astype(BF16)
    mixed_sum = lax.psum_scatter(
        product(active, feed_shrink).astype(BF16), "mp", scatter_dimension=0, tiled=True
    )
    mixed_out = (own_cross + mixed_sum.astype(F32)).astype(BF16)
    _, gelu_pull = jax.vjp(gelu_exact, hidden)
    grad_hidden = gelu_pull(product(feed_grad, feed_shrink, NT))[0].astype(BF16)
    own_grad, cross_grad, third_gain = plain_step(
        grad_hidden, feed_expand, NT, post_backward, gains[2:3],
        (own_rows(feed_grad).astype(F32), own_cross),
    )
    grad_mixed = plain_heads(product(cross_grad, cross_out, NT).astype(BF16), images)[0]
    back = per_head(attend_backward_head)(cross_queries, text_keys, text_values, grad_mixed)
    grad_queries, grad_keys, grad_values = (plain_rows(part) for part in back)
    grad_text = jnp.concatenate([grad_keys, grad_values], axis=1)
    own_grad, self_grad, second_gain = plain_step(
        grad_queries, cross_query, NT, post_backward, gains[1:2], (own_grad, own_self)
    )
    grad_mixed = plain_heads(product(self_grad, attention_out, NT).astype(BF16), images)[0]
    back = per_head(attend_backward_head)(queries, keys_in, values_in, grad_mixed)
    grad_projected = jnp.concatenate([plain_rows(part) for part in back], axis=1)
    tokens_grad, first_gain, embed_term = plain_step(
        grad_projected, weight_in, NN, post_entry, gains[0:1], (own_grad, own_entry, own_float)
    )
    caption_grad = lax.psum_scatter(
        product(grad_text, weight_text, NT).astype(BF16), "mp", scatter_dimension=1, tiled=True
    )
    small = jnp.concatenate([first_gain, second_gain, third_gain, embed_term], axis=0)
    return (
        mixed_out,
        tokens_grad,
        caption_grad,
        lax.psum_scatter(small, ("img", "mp"), scatter_dimension=1, tiled=True),
        image_sum(rows_product(first_normed, grad_projected)),
        image_sum(rows_product(self_mixed, self_grad), 1),
        image_sum(rows_product(second_normed, grad_queries)),
        image_sum(rows_product(caption, grad_text)),
        image_sum(rows_product(cross_mixed, cross_grad), 1),
        image_sum(rows_product(third_normed, grad_hidden)),
        image_sum(rows_product(active, feed_grad), 1),
    )


def layer_square(images, own_mask, gains, own_entry, first_normed, projected, feed_grad, weights):
    attention_out, cross_query, cross_out, feed_expand, feed_shrink, weight_in, weight_text, caption = weights
    width = first_normed.shape[1]
    spot = lax.axis_index("mp")

    def four(rows_in):
        return rows_in.reshape(images, 4, -1, rows_in.shape[-1])

    four_grad, four_projected, four_normed = four(feed_grad), four(projected), four(first_normed)
    rows = forward_rows(
        gains, four_projected, attention_out, own_entry, cross_query, weight_text, cross_out, four_grad,
        feed_expand, feed_shrink, caption,
    )
    back = middle_rows(gains, four_grad, rows, rows.text, cross_out, cross_query, feed_expand)
    entry = entry_rows(
        gains, own_mask, rows, back, four_projected, own_entry, attention_out, weight_in, weight_text,
    )
    terms = [entry.first_gain, back.second_gain, back.third_gain, entry.embed_term]
    small = jnp.concatenate(terms + [jnp.zeros_like(entry.embed_term)] * 4, axis=0)
    late = line_sums(four_normed, rows, back, entry, small, feed_shrink)
    slice_width = width // 32
    at = (lax.axis_index("img") * 4 + spot) * slice_width
    return (
        late.mixed_out,
        late.tokens_out,
        late.caption_out,
        lax.dynamic_slice_in_dim(late.small_out, at, slice_width, 1),
        late.in_sum,
        late.self_sum,
        entry.query_sum,
        late.text_sum,
        entry.cross_sum,
        jnp.concatenate([back.expand_sum, entry.expand_sum], axis=1),
        back.shrink_sum,
    )


def body(
    square,
    tokens,
    caption,
    masked,
    out_grad,
    mask_embed,
    norm_gains,
    attention_in,
    attention_out,
    cross_query,
    cross_text,
    cross_out,
    feed_expand,
    feed_shrink,
):
    images, length = masked.shape
    rows_all = images * length
    count = lax.axis_size("mp")
    spot = lax.axis_index("mp")
    text_width = caption.shape[1]

    def own_rows(rows_in):
        return lax.dynamic_slice_in_dim(rows_in, spot * (rows_all // count), rows_all // count, 0)

    def own_quarters(rows_in):
        parts = rows_in.reshape(images, count, length // count, -1)
        return lax.dynamic_index_in_dim(parts, spot, 1, False)

    def enter(rows_in, mask):
        return jnp.where(mask, mask_embed.astype(F32), rows_in.astype(F32))

    own = own_quarters if square else own_rows
    mask_column = masked.reshape(rows_all, 1) > 0
    own_mask = own(mask_column)
    own_float = own_mask.astype(F32)
    own_entry = enter(own(tokens), own_mask)
    first_unit, _ = norm_parts(enter(tokens, mask_column))
    first_normed = (first_unit * norm_gains[0:1]).astype(BF16)
    weight_in = attention_in.transpose(1, 2, 0).reshape(-1, tokens.shape[1])
    projected = product(first_normed, weight_in, NT).astype(BF16)
    weight_text = cross_text.reshape(text_width, -1)
    feed_grad = jnp.where(mask_column, out_grad, jnp.zeros_like(out_grad))
    weights = (
        attention_out, cross_query, cross_out, feed_expand, feed_shrink, weight_in, weight_text, caption,
    )
    if square:
        done = layer_square(
            images, own_float, norm_gains, own_entry, first_normed, projected, feed_grad, weights
        )
    else:
        done = layer_plain(
            images, own_rows, norm_gains, own_entry, own_float, first_normed, projected,
            feed_grad, weights,
        )
    mixed_out, tokens_grad, caption_grad, small_sums, self_in, *sums = done
    self_out, cross_query_sum, cross_text_sum, cross_out_sum, expand_sum, shrink_sum = (
        part.astype(F32) for part in sums
    )
    return (
        mixed_out,
        tokens_grad,
        caption_grad.astype(F32),
        small_sums[3],
        small_sums[0:3],
        self_in.astype(F32).reshape(-1, 3, attention_in.shape[2]),
        self_out,
        cross_query_sum,
        cross_text_sum.reshape(-1, 2, cross_text.shape[2]),
        cross_out_sum,
        expand_sum,
        shrink_sum,
    )


def solution(mesh):
    square = mesh.shape["mp"] == 4 and mesh.shape["img"] == 8
    return jax.shard_map(
        functools.partial(body, square),
        mesh=mesh,
        in_specs=(
            P("img", None),
            P("img", None),
            P("img", None),
            P("img", None),
            P(),
            P(),
            P(None, None, "mp"),
            P("mp", None),
            P(None, "mp"),
            P(None, None, "mp"),
            P("mp", None),
            P(None, "mp"),
            P("mp", None),
        ),
        out_specs=(
            P(("img", "mp"), None),
            P(("img", "mp"), None),
            P("img", "mp"),
            P(("img", "mp")),
            P(None, ("img", "mp")),
            P("img", None, "mp"),
            P("mp", "img"),
            P("img", "mp"),
            P("img", None, "mp"),
            P("mp", "img"),
            P("img", "mp"),
            P("mp", "img"),
        ),
        check_vma=False,
    )
```
